128 devices in a mesh: blk: 8 (over x, z_hi), fsdp: 16 (over z_lo, y, core).
Axes of the slice: x: 4, y: 4, z: 4 (z_hi: 2, z_lo: 2; z = z_hi * 2 + z_lo), core: 2. Of those that a mesh axis runs over, the one named last changes fastest.
Arguments:
- tokens: bfloat16 [8, 8192, 2048], P('blk', 'fsdp'), may hold values from -21 to 21
- student_weight: float32 [8, 2560, 2048], P('blk', 'fsdp'), may hold values from -0.125 to 0.125
- snapshot: bfloat16 [8, 2560, 2048], P('blk', 'fsdp'), may hold values from -0.125 to 0.125
- moment_one: float32 [8, 2560, 2048], P('blk', 'fsdp'), may hold values from -0.6 to 0.6
- moment_two: float32 [8, 2560, 2048], P('blk', 'fsdp'), may hold values from 0.001 to 0.1
Outputs:
- new_weight: float32 [8, 2560, 2048], P('blk', 'fsdp')
- new_moment_one: float32 [8, 2560, 2048], P('blk', 'fsdp')
- new_moment_two: float32 [8, 2560, 2048], P('blk', 'fsdp')
The draws below stay inside these ranges and needn't reach their ends.
All inputs are finite; a program needn't handle non-finite values.
Results may differ from the reference program's by a relative error of at most 0.0045.
The reference program's roundings to bfloat16 on the way count: a program that leaves them out, or rounds other values in their place, can miss the bound.
Values may be sent and summed in bfloat16 or wider, within the bound.
No kernel may reach another device: no remote copies, remote signals or barrier semaphores. Data moves between devices by JAX's collectives and lax.ppermute only.
A program may use at most 128 MiB of HBM per device.

```python
import math
import jax
import jax.numpy as jnp
from jax import lax

D = 2048
HEADS = 16
KVH = 4
HD = 128
SEQ = 256
STEP = 100
QKC = 2560
GROUPS = 8
GROUP_TOKENS = 8192


def draw_tokens(key, part):
    key = jax.random.fold_in(key, 11)
    key_base = jax.random.fold_in(key, 0)
    shape = (GROUPS, GROUP_TOKENS, D)
    values = jnp.clip(jax.random.normal(key_base, shape, jnp.float32), -6.0, 6.0)
    return values.astype(jnp.bfloat16)


def levels(own_key, extent, shards, low, largest):
    gain, own = 1.0, jax.random.fold_in(own_key, 6)
    for axis_at, blocks in shards:
        steps = jnp.exp(jax.random.uniform(jax.random.fold_in(own, axis_at), (blocks,), jnp.float32, low / len(shards), largest / len(shards)))
        gain = gain * jnp.repeat(steps, extent[axis_at] // blocks).reshape([-1 if axis == axis_at else 1 for axis in range(len(extent))])
    return gain


def scatter_about(own_key, extent, deviation, bound, cuts=(), held_as=jnp.bfloat16):
    factor_of = levels(own_key, extent, cuts, -0.22, 0.18) if cuts else 1.0
    values = jax.random.normal(own_key, extent, jnp.float32) * deviation * factor_of
    return jnp.minimum(jnp.maximum(values, -bound), bound).astype(held_as)


def setup_inputs(seed: int = 0) -> dict:
    arg_keys = jax.random.split(jax.random.key(seed), 6)
    return {
        "tokens": draw_tokens(jax.random.fold_in(arg_keys[5], 71), 0),
        "student_weight": scatter_about(arg_keys[1], (GROUPS, QKC, D), D ** -0.5, 0.125, ((0, 8), (1, 16)), jnp.float32),
        "snapshot": scatter_about(arg_keys[2], (GROUPS, QKC, D), D ** -0.5, 0.125, ((0, 8), (1, 16))),
        "moment_one": scatter_about(arg_keys[3], (GROUPS, QKC, D), 0.1, 0.6, ((0, 8), (1, 16)), jnp.float32),
        "moment_two": jnp.clip(jnp.exp(math.log(0.1) - 4.6051702 * jax.random.uniform(arg_keys[4], (GROUPS, QKC, D), jnp.float32) ** levels(arg_keys[4], (GROUPS, QKC, D), ((0, 8), (1, 16)), -0.2, 0.2)), 0.001, 0.1),
    }


THETA = 500000.0
BETA_ONE = 0.9
BETA_TWO = 0.95
LEARN_RATE = 0.002
DECAY = 0.1
EPSILON = 1e-08
MASKED = -1e+30

def rotary_tables(row_count, seq_len, head_size):
    positions = (jnp.arange(row_count) % seq_len).astype(jnp.float32)
    exponents = jnp.arange(head_size // 2).astype(jnp.float32) * (2.0 / head_size)
    frequency = THETA ** (-exponents)
    angles = positions[:, None] * frequency[None, :]
    return (jnp.cos(angles)[:, None, :], jnp.sin(angles)[:, None, :])

def rotate(vectors, cosine, sine_table, direction):
    row_count = vectors.shape[0]
    shaped = vectors.reshape(row_count, -1, HD)
    half_size = HD // 2
    front_half = shaped[..., :half_size]
    back_half = shaped[..., half_size:]
    turned = jnp.concatenate([front_half * cosine - direction * back_half * sine_table, back_half * cosine + direction * front_half * sine_table], axis=-1)
    return turned.reshape(row_count, -1)

def score_gradient(qk_student, qk_teacher):
    row_count = qk_student.shape[0]
    seq_count = row_count // SEQ
    group_size = HEADS // KVH
    inv_root = 1.0 / math.sqrt(HD)
    causal = jnp.arange(SEQ)[:, None] >= jnp.arange(SEQ)[None, :]

    def split_heads(packed):
        packed = packed.astype(jnp.float32)
        queries = packed[:, :HEADS * HD].reshape(seq_count, SEQ, KVH, group_size, HD)
        key_rows = packed[:, HEADS * HD:].reshape(seq_count, SEQ, KVH, HD)
        return (queries, key_rows)

    def log_probs(queries, key_rows):
        scores = jnp.einsum('bikrd,bjkd->bkrij', queries, key_rows) * inv_root
        scores = jnp.where(causal, scores, MASKED)
        return jax.nn.log_softmax(scores, axis=-1)
    query_student, key_student = split_heads(qk_student)
    query_teacher, key_teacher = split_heads(qk_teacher)
    spread = jnp.exp(log_probs(query_student, key_student)) - jnp.exp(log_probs(query_teacher, key_teacher))
    rounded = lax.optimization_barrier((jnp.where(causal, spread, 0.0) / HEADS).astype(jnp.bfloat16))
    weights_wide = rounded.astype(jnp.float32)
    query_grad = jnp.einsum('bkrij,bjkd->bikrd', weights_wide, key_student) * inv_root
    key_grad = jnp.einsum('bkrij,bikrd->bjkd', weights_wide, query_student) * inv_root
    return jnp.concatenate([query_grad.reshape(row_count, HEADS * HD), key_grad.reshape(row_count, KVH * HD)], axis=1)

def reference(tokens, student_weight, snapshot, moment_one, moment_two):
    cosine, sine_table = rotary_tables(GROUP_TOKENS, SEQ, HD)
    weight_list = []
    first_list = []
    second_list = []
    for group in range(GROUPS):
        rows_in = tokens[group]
        student_copy = student_weight[group].astype(jnp.bfloat16)
        teacher = snapshot[(group - 1) % GROUPS]
        raw_student = jnp.dot(rows_in, student_copy.T, preferred_element_type=jnp.float32)
        raw_teacher = jnp.dot(rows_in, teacher.T, preferred_element_type=jnp.float32)
        qk_student = lax.optimization_barrier(rotate(raw_student, cosine, sine_table, 1.0).astype(jnp.bfloat16))
        qk_teacher = lax.optimization_barrier(rotate(raw_teacher, cosine, sine_table, 1.0).astype(jnp.bfloat16))
        proj_grad = rotate(score_gradient(qk_student, qk_teacher), cosine, sine_table, -1.0).astype(jnp.bfloat16)
        gradient = jnp.dot(proj_grad.T, rows_in, preferred_element_type=jnp.float32)
        first_new = BETA_ONE * moment_one[group] + (1.0 - BETA_ONE) * gradient
        second_new = BETA_TWO * moment_two[group] + (1.0 - BETA_TWO) * gradient * gradient
        step_dir = first_new / (1.0 - BETA_ONE ** STEP) / (jnp.sqrt(second_new / (1.0 - BETA_TWO ** STEP)) + EPSILON)
        master = student_weight[group]
        weight_list.append(master - LEARN_RATE * (step_dir + DECAY * master))
        first_list.append(first_new)
        second_list.append(second_new)
    return (jnp.stack(weight_list, 0), jnp.stack(first_list, 0), jnp.stack(second_list, 0))
```

```python
import math

import jax
import jax.numpy as jnp
import numpy as np
from jax import lax
from jax.experimental import pallas as pl
from jax.experimental.pallas import tpu as pltpu
from jax.sharding import PartitionSpec as P

HEADS = 16
KVH = 4
HD = 128
SEQ = 256
STEP = 100
D = 2048
THETA = 500000.0
BETA_ONE = 0.9
BETA_TWO = 0.95
LEARN_RATE = 0.002
DECAY = 0.1
EPSILON = 1e-08
MASKED = -1e30

BF = jnp.bfloat16
F32 = jnp.float32
SHARD = 160
UNIT = 32
HALF = HD // 2
KVROWS = 640
FAR = 96
INV_ROOT = 1.0 / math.sqrt(HD)

ARRANGED = [[5 * d + k for k in range(5)] for d in range(16)]
ARRANGED[12] = [60, 61, 64, 62, 63]
ARRANGED[14] = [72, 73, 74, 70, 71]
ALIGNED = [list(units) for units in ARRANGED]
ALIGNED[6] = [30, 31, 64, 70, 71]
ALIGNED[7] = [65, 66, 67, 68, 69]
ALIGNED[12] = [60, 61, 32, 62, 63]
ALIGNED[13] = [35, 36, 37, 38, 39]
ALIGNED[14] = [72, 73, 74, 33, 34]
OWNER = list(range(16))
OWNER[7], OWNER[13] = 13, 7


def head_position(unit, plane):
    if unit < 64:
        return (unit // 16 - 2 * plane) * 20 + unit % 16
    return ((unit - 64) // 4 - 2 * plane) * 20 + 16 + (unit - 64) % 4


def build_tables():
    order = np.array([[u - 5 * d for u in ARRANGED[d]] for d in range(16)], np.int32)
    inverse = np.argsort(order, axis=1).astype(np.int32)
    place = np.zeros((16, 40), np.int32)
    for d in range(16):
        z, y, c = d // 8, d % 8 // 2, d % 2
        row = []
        for r in range(2):
            for step in range(4):
                other = 8 * z + 2 * ((y + step) % 4) + (c ^ r)
                row += [head_position(u, z) for u in ALIGNED[other]]
        assert sorted(row) == list(range(40))
        place[d] = row
    return order, inverse, place


ORDER, INVERSE, PLACE = build_tables()


def pairs_of(function):
    out = []
    for d in range(16):
        z, y, c = function(d // 8, d % 8 // 2, d % 2)
        out.append((d, z % 2 * 8 + y % 4 * 2 + c % 2))
    return out


TO_CORE = pairs_of(lambda z, y, c: (z, y, c + 1))
TO_PLANE = pairs_of(lambda z, y, c: (z + 1, y, c))
UP = pairs_of(lambda z, y, c: (z, y + 1, c))
DOWN = pairs_of(lambda z, y, c: (z, y - 1, c))
SWAP_A = [(7, 13), (13, 7), (6, 14), (14, 6)]
SWAP_PART = [(6, 14), (14, 6)]
SWAP_B = [(6, 12), (12, 6)]


def send(value, pairs):
    return lax.ppermute(value, "fsdp", pairs)


def send_next(value, pairs):
    return lax.ppermute(
        value,
        ("blk", "fsdp"),
        [(g * 16 + a, (g + 1) % 8 * 16 + b) for g in range(8) for a, b in pairs],
    )


def params(mib):
    return pltpu.CompilerParams(vmem_limit_bytes=mib * 2**20)


def arrange_kernel(order, weight, snapshot, weight_out, snapshot_out):
    weight_out[...] = weight[...].astype(BF)
    snapshot_out[...] = snapshot[...]


def arrange(order, weight, snapshot):
    picked = pl.BlockSpec((UNIT, D), lambda k, order: (order[k], 0))
    straight = pl.BlockSpec((UNIT, D), lambda k, order: (k, 0))
    return pl.pallas_call(
        arrange_kernel,
        grid_spec=pltpu.PrefetchScalarGridSpec(
            num_scalar_prefetch=1, grid=(5,), in_specs=[picked, picked], out_specs=[straight, straight]
        ),
        out_shape=[jax.ShapeDtypeStruct((SHARD, D), BF)] * 2,
        compiler_params=params(32),
        name="arrange",
    )(order, weight, snapshot)


PIECES = ((0, SHARD, 0), (1, SHARD, 0), (2, SHARD, 0), (3, SHARD, 0))


def copies(place, arrays, held, sems):
    out = []
    for at, array in enumerate(arrays):
        for k in range(5):
            n = at * 5 + k
            row = pl.multiple_of(place[n] * UNIT, UNIT)
            out.append(
                pltpu.make_async_copy(
                    array.at[pl.ds(k * UNIT, UNIT)], held.at[pl.ds(row, UNIT)], sems.at[n]
                )
            )
    return out


def load_weight(place, arrays, held, sems):
    @pl.when(pl.program_id(0) == 0)
    def _():
        for copy in copies(place, arrays, held, sems):
            copy.start()
        for copy in copies(place, arrays, held, sems):
            copy.wait()


def rotated(raw, cosine, sine):
    front, back = raw[:HALF], raw[HALF:]
    return jnp.concatenate([front * cosine - back * sine, back * cosine + front * sine], axis=0)


def project(held, rows_in, cosine, sine, kv):
    raw = lax.dot_general(
        held[kv * KVROWS : (kv + 1) * KVROWS, :],
        rows_in,
        (((1,), (1,)), ((), ())),
        preferred_element_type=F32,
    )
    return [rotated(raw[h * HD : (h + 1) * HD], cosine, sine).astype(BF) for h in range(5)]


def student_kernel(place, x, cosine, sine, *rest):
    arrays, (out, held, sems) = rest[:8], rest[8:]
    load_weight(place, arrays, held, sems)
    for kv in range(2):
        for h, value in enumerate(project(held, x[...], cosine[...], sine[...], kv)):
            out[kv * KVROWS + h * HD : kv * KVROWS + (h + 1) * HD, :] = value


ANY = pl.BlockSpec(memory_space=pl.ANY)
TABLE = pl.BlockSpec((HALF, SEQ), lambda s, place: (0, 0))
ROWS = pl.BlockSpec((SEQ, D), lambda s, place: (s, 0))
COLUMNS = pl.BlockSpec((2 * KVROWS, SEQ), lambda s, place: (0, s))


def student_projection(place, x, cosine, sine, arrays):
    count = x.shape[0] // SEQ
    return pl.pallas_call(
        student_kernel,
        grid_spec=pltpu.PrefetchScalarGridSpec(
            num_scalar_prefetch=1,
            grid=(count,),
            in_specs=[ROWS, TABLE, TABLE] + [ANY] * 8,
            out_specs=COLUMNS,
            scratch_shapes=[pltpu.VMEM((2 * KVROWS, D), BF), pltpu.SemaphoreType.DMA((40,))],
        ),
        out_shape=jax.ShapeDtypeStruct((2 * KVROWS, x.shape[0]), BF),
        compiler_params=params(48),
        cost_estimate=pl.CostEstimate(
            flops=2 * x.shape[0] * 2 * KVROWS * D, bytes_accessed=9 * 2**20, transcendentals=0
        ),
        name="student_projection",
    )(place, x, cosine, sine, *arrays)


GRID_SCALE = INV_ROOT * math.log2(math.e)


def softmax_parts(scores, diagonal):
    scores = scores * GRID_SCALE
    low = scores.shape[0] - HD
    masked = jnp.where(diagonal, scores[low:], MASKED)
    if low:
        scores = jnp.concatenate([scores[:low], masked], axis=0)
    else:
        scores = masked
    power = jnp.exp2(scores - jnp.max(scores, axis=0, keepdims=True))
    return power, (1.0 / HEADS) / jnp.sum(power, axis=0, keepdims=True)


def dot(a, b, dims=((1,), (0,))):
    return lax.dot_general(a, b, (dims, ((), ())), preferred_element_type=F32)


def side_by_side(heads, half):
    return jnp.concatenate([q[:, half * HD : (half + 1) * HD] for q in heads], axis=1)


def attention_gradient(student, teacher, cosine, sine):
    key_s = student[4]
    rows_s, rows_t = key_s.T, teacher[4].T
    lane = lax.broadcasted_iota(jnp.int32, (HD, 4 * HD), 1) % HD
    diagonal = lax.broadcasted_iota(jnp.int32, (HD, 4 * HD), 0) <= lane
    query_parts, key_grad = [], None
    for half in range(2):
        extent = (half + 1) * HD
        q_s = side_by_side(student[:4], half)
        q_t = side_by_side(teacher[:4], half)
        power_s, inverse_s = softmax_parts(dot(rows_s[:extent], q_s), diagonal)
        power_t, inverse_t = softmax_parts(dot(rows_t[:extent], q_t), diagonal)
        spread = (power_s * inverse_s - power_t * inverse_t).astype(BF)
        query_parts.append(dot(key_s[:, :extent], spread))
        part = dot(q_s, spread, ((1,), (1,)))
        if half == 0:
            key_grad = part
        else:
            key_grad = jnp.concatenate([part[:, :HD] + key_grad, part[:, HD:]], axis=1)
    grads = [
        jnp.concatenate([p[:, h * HD : (h + 1) * HD] for p in query_parts], axis=1)
        for h in range(4)
    ] + [key_grad]
    return [rotated(g * INV_ROOT, cosine, -sine).astype(BF) for g in grads]


def gradient_kernel(place, x, qk_student, cosine, sine, *rest):
    arrays, (out, held, grads, sems) = rest[:8], rest[8:]
    load_weight(place, arrays, held, sems)
    for kv in range(2):
        teacher = project(held, x[...], cosine[...], sine[...], kv)
        base = kv * KVROWS
        student = [qk_student[base + h * HD : base + (h + 1) * HD, :] for h in range(5)]
        for h, value in enumerate(attention_gradient(student, teacher, cosine[...], sine[...])):
            grads[base + h * HD : base + (h + 1) * HD, :] = value
    for n in range(40):
        row = pl.multiple_of(place[n] * UNIT, UNIT)
        out[n * UNIT : (n + 1) * UNIT, :] = grads[pl.ds(row, UNIT), :]


def projection_gradient(place, x, qk_student, cosine, sine, arrays):
    count = x.shape[0] // SEQ
    return pl.pallas_call(
        gradient_kernel,
        grid_spec=pltpu.PrefetchScalarGridSpec(
            num_scalar_prefetch=1,
            grid=(count,),
            in_specs=[ROWS, COLUMNS, TABLE, TABLE] + [ANY] * 8,
            out_specs=COLUMNS,
            scratch_shapes=[
                pltpu.VMEM((2 * KVROWS, D), BF),
                pltpu.VMEM((2 * KVROWS, SEQ), BF),
                pltpu.SemaphoreType.DMA((40,)),
            ],
        ),
        out_shape=jax.ShapeDtypeStruct((2 * KVROWS, x.shape[0]), BF),
        compiler_params=params(56),
        cost_estimate=pl.CostEstimate(
            flops=6 * x.shape[0] * 2 * KVROWS * D, bytes_accessed=9 * 2**20, transcendentals=0
        ),
        name="projection_gradient",
    )(place, x, qk_student, cosine, sine, *arrays)


TILE = 512


def weight_kernel(first, count, own_a, own_b, other_a, other_b, xa, xb, ya, yb, *outs):
    lo, hi = first * SHARD, (first + count) * SHARD
    total = dot(own_a[lo:hi, :], xa[...])
    total += dot(own_b[lo:hi, :], xb[...])
    total += dot(other_a[lo:hi, :], ya[...])
    total += dot(other_b[lo:hi, :], yb[...])
    for n, out in enumerate(outs):
        out[...] = total[n * SHARD : (n + 1) * SHARD].astype(BF)


def weight_gradient(first, count, grads, tokens):
    whole = [pl.BlockSpec((KVROWS, 2 * SEQ), lambda t: (0, 0))] * 4
    return pl.pallas_call(
        lambda *refs: weight_kernel(first, count, *refs),
        grid=(D // TILE,),
        in_specs=whole + [pl.BlockSpec((2 * SEQ, TILE), lambda t: (0, t))] * 4,
        out_specs=[pl.BlockSpec((SHARD, TILE), lambda t: (0, t))] * count,
        out_shape=[jax.ShapeDtypeStruct((SHARD, D), BF)] * count,
        compiler_params=params(48),
        cost_estimate=pl.CostEstimate(
            flops=2 * count * SHARD * 8 * SEQ * D, bytes_accessed=12 * 2**20, transcendentals=0
        ),
        name="weight_gradient",
    )(*grads, *tokens)


def adam_kernel(table, b0, b1, b2, b3, part_a, part_b, weight, one, two, weight_out, one_out, two_out):
    k = pl.program_id(0)
    at = table[k]
    swapped = table[5]
    gradient = (b0[...].astype(F32) + b1[...].astype(F32)) + (
        b2[...].astype(F32) + b3[...].astype(F32)
    )
    take_a = jnp.logical_and(at >= 3, swapped % 2 == 1)
    take_b = jnp.logical_and(at == 2, swapped // 2 == 1)
    gradient = jnp.where(take_a, part_a[...], jnp.where(take_b, part_b[...], gradient))
    first_new = BETA_ONE * one[...] + (1.0 - BETA_ONE) * gradient
    second_new = BETA_TWO * two[...] + (1.0 - BETA_TWO) * gradient * gradient
    step_dir = (
        first_new
        / (1.0 - BETA_ONE**STEP)
        / (jnp.sqrt(second_new / (1.0 - BETA_TWO**STEP)) + EPSILON)
    )
    master = weight[...]
    weight_out[...] = master - LEARN_RATE * (step_dir + DECAY * master)
    one_out[...] = first_new
    two_out[...] = second_new


def adam(table, blocks, part_a, part_b, weight, one, two):
    picked = pl.BlockSpec((UNIT, D), lambda k, t: (t[k], 0))
    from_a = pl.BlockSpec((UNIT, D), lambda k, t: (jnp.maximum(t[k] - 3, 0), 0))
    from_b = pl.BlockSpec((UNIT, D), lambda k, t: (0, 0))
    straight = pl.BlockSpec((UNIT, D), lambda k, t: (k, 0))
    return pl.pallas_call(
        adam_kernel,
        grid_spec=pltpu.PrefetchScalarGridSpec(
            num_scalar_prefetch=1,
            grid=(5,),
            in_specs=[picked] * 4 + [from_a, from_b] + [straight] * 3,
            out_specs=[straight] * 3,
        ),
        out_shape=[jax.ShapeDtypeStruct((SHARD, D), F32)] * 3,
        compiler_params=params(32),
        name="adam",
    )(table, *blocks, part_a, part_b, weight, one, two)


def rotary_tables():
    positions = jnp.arange(SEQ).astype(F32)
    exponents = jnp.arange(HALF).astype(F32) * (2.0 / HD)
    frequency = THETA ** (-exponents)
    angles = frequency[:, None] * positions[None, :]
    return jnp.cos(angles), jnp.sin(angles)


def ring_gather(shard):
    below = send(shard, UP)
    above = send(shard, DOWN)
    far_low = send(below[:FAR], UP)
    far_high = send(above[FAR:], DOWN)
    far = jnp.concatenate([far_low, far_high], axis=0)
    own = [shard, above, far, below]
    return own + [send(piece, TO_CORE) for piece in own]


def per_device(tokens, student_weight, snapshot, moment_one, moment_two):
    own_tokens = tokens[0]
    master = student_weight[0]
    me = lax.axis_index("fsdp")
    order = jnp.asarray(ORDER)[me]
    place = jnp.asarray(PLACE)[me]
    cosine, sine = rotary_tables()

    student_shard, teacher_shard = arrange(order, master, snapshot[0])
    row = lax.broadcasted_iota(jnp.int32, (SHARD, 1), 0)
    whole = (me == 7) | (me == 13)
    mask_a = whole | (((me == 6) | (me == 14)) & (row >= 96))
    mask_b = ((me == 6) | (me == 12)) & (row >= 64) & (row < 96)

    main = send_next(teacher_shard, list(enumerate(OWNER)))
    tail = send_next(teacher_shard[96:], SWAP_PART)
    middle = send_next(teacher_shard[64:96], SWAP_B)
    swap_a = send(student_shard, SWAP_A)
    swap_b = send(student_shard[64:96], SWAP_B)

    def widen(part, low):
        return jnp.pad(part, ((low, SHARD - low - part.shape[0]), (0, 0)))

    student = jnp.where(mask_a, swap_a, jnp.where(mask_b, widen(swap_b, 64), student_shard))
    mask_tail = ((me == 6) | (me == 14)) & (row >= 96)
    teacher = jnp.where(mask_tail, widen(tail, 96), jnp.where(mask_b, widen(middle, 64), main))

    plane_tokens = send(own_tokens, TO_PLANE)
    student_rows = ring_gather(student)
    teacher_rows = ring_gather(teacher)
    core_tokens = send(own_tokens, TO_CORE)
    far_tokens = send(plane_tokens, TO_CORE)

    grads, others = [], []
    for x in (own_tokens, plane_tokens):
        qk_student = student_projection(place, x, cosine, sine, student_rows)
        grad = projection_gradient(place, x, qk_student, cosine, sine, teacher_rows)
        grads.append(grad)
        others.append(send(grad[KVROWS:], TO_CORE))

    parts = grads + others
    all_tokens = (own_tokens, plane_tokens, core_tokens, far_tokens)

    def to_owner(block, step):
        return send(
            block,
            [
                (d, OWNER[d // 8 * 8 + (d % 8 // 2 + step) % 4 * 2 + d % 2])
                for d in range(16)
            ],
        )

    (block_two,) = weight_gradient(2, 1, parts, all_tokens)
    got_two = to_owner(block_two, 2)
    block_zero, block_one = weight_gradient(0, 2, parts, all_tokens)
    (block_three,) = weight_gradient(3, 1, parts, all_tokens)
    got_one = to_owner(block_one, 1)
    got_three = to_owner(block_three, 3)
    got_zero = to_owner(block_zero, 0)
    blocks = [got_zero, got_one, got_two, got_three]

    reduced = sum(block[64:].astype(F32) for block in blocks)
    part_b = send(reduced[:32], SWAP_B)
    part_a = send(reduced[32:], SWAP_PART)
    in_a = ((me == 6) | (me == 14)).astype(jnp.int32)
    in_b = ((me == 6) | (me == 12)).astype(jnp.int32)
    table = jnp.concatenate([jnp.asarray(INVERSE)[me], (in_a + 2 * in_b)[None]])
    updated = adam(table, blocks, part_a, part_b, master, moment_one[0], moment_two[0])
    return tuple(value[None] for value in updated)


def solution(mesh):
    spec = P("blk", "fsdp", None)
    return jax.shard_map(
        per_device,
        mesh=mesh,
        in_specs=(spec,) * 5,
        out_specs=(spec,) * 3,
        check_vma=False,
    )
```

```python
import math

import jax
import jax.numpy as jnp
import numpy as np
from jax import lax
from jax.experimental import pallas as pl
from jax.experimental.pallas import tpu as pltpu
from jax.sharding import PartitionSpec as P

HEADS = 16
KVH = 4
HD = 128
SEQ = 256
STEP = 100
D = 2048
THETA = 500000.0
BETA_ONE = 0.9
BETA_TWO = 0.95
LEARN_RATE = 0.002
DECAY = 0.1
EPSILON = 1e-08
MASKED = -1e30

BF = jnp.bfloat16
F32 = jnp.float32
SHARD = 160
UNIT = 32
HALF = HD // 2
KVROWS = 640
INV_ROOT = 1.0 / math.sqrt(HD)

ARRANGED = [[5 * d + k for k in range(5)] for d in range(16)]
ARRANGED[12] = [60, 61, 64, 62, 63]
ARRANGED[14] = [72, 73, 74, 70, 71]
ALIGNED = [list(units) for units in ARRANGED]
ALIGNED[6] = [30, 31, 64, 70, 71]
ALIGNED[7] = [65, 66, 67, 68, 69]
ALIGNED[12] = [60, 61, 32, 62, 63]
ALIGNED[13] = [35, 36, 37, 38, 39]
ALIGNED[14] = [72, 73, 74, 33, 34]
OWNER = list(range(16))
OWNER[7], OWNER[13] = 13, 7
PARTS = ((0, 64), (64, 96), (96, 160))
PART_OWNER = [list(OWNER) for _ in PARTS]
PART_OWNER[1][6], PART_OWNER[1][12] = 12, 6
PART_OWNER[2][6], PART_OWNER[2][14] = 14, 6


def head_position(unit, plane):
    if unit < 64:
        return (unit // 16 - 2 * plane) * 20 + unit % 16
    return ((unit - 64) // 4 - 2 * plane) * 20 + 16 + (unit - 64) % 4


def build_tables():
    order = np.array([[u - 5 * d for u in ARRANGED[d]] for d in range(16)], np.int32)
    place = np.zeros((16, 40), np.int32)
    for d in range(16):
        z, y, c = d // 8, d % 8 // 2, d % 2
        row = []
        for r in range(2):
            for step in range(4):
                other = 8 * z + 2 * ((y + step) % 4) + (c ^ r)
                row += [head_position(u, z) for u in ALIGNED[other]]
        assert sorted(row) == list(range(40))
        place[d] = row
    return order, place


ORDER, PLACE = build_tables()


def pairs_of(function):
    out = []
    for d in range(16):
        z, y, c = function(d // 8, d % 8 // 2, d % 2)
        out.append((d, z % 2 * 8 + y % 4 * 2 + c % 2))
    return out


TO_CORE = pairs_of(lambda z, y, c: (z, y, c + 1))
TO_PLANE = pairs_of(lambda z, y, c: (z + 1, y, c))
UP = pairs_of(lambda z, y, c: (z, y + 1, c))
DOWN = pairs_of(lambda z, y, c: (z, y - 1, c))
SWAP_A = [(7, 13), (13, 7), (6, 14), (14, 6)]
SWAP_PART = [(6, 14), (14, 6)]
SWAP_B = [(6, 12), (12, 6)]


def send(value, pairs):
    return lax.ppermute(value, "fsdp", pairs)


def send_next(value, pairs):
    return lax.ppermute(
        value,
        ("blk", "fsdp"),
        [(g * 16 + a, (g + 1) % 8 * 16 + b) for g in range(8) for a, b in pairs],
    )


def params(mib):
    return pltpu.CompilerParams(vmem_limit_bytes=mib * 2**20)


def arrange_kernel(order, weight, snapshot, weight_out, snapshot_out):
    weight_out[...] = weight[...].astype(BF)
    snapshot_out[...] = snapshot[...]


def arrange(order, weight, snapshot):
    picked = pl.BlockSpec((UNIT, D), lambda k, order: (order[k], 0))
    straight = pl.BlockSpec((UNIT, D), lambda k, order: (k, 0))
    return pl.pallas_call(
        arrange_kernel,
        grid_spec=pltpu.PrefetchScalarGridSpec(
            num_scalar_prefetch=1, grid=(5,), in_specs=[picked, picked], out_specs=[straight, straight]
        ),
        out_shape=[jax.ShapeDtypeStruct((SHARD, D), BF)] * 2,
        compiler_params=params(56),
        name="arrange",
    )(order, weight, snapshot)


def copies(place, arrays, held, sems):
    out = []
    for at, array in enumerate(arrays):
        for k in range(5):
            n = at * 5 + k
            row = pl.multiple_of(place[n] * UNIT, UNIT)
            out.append(
                pltpu.make_async_copy(
                    array.at[pl.ds(k * UNIT, UNIT)], held.at[pl.ds(row, UNIT)], sems.at[n]
                )
            )
    return out


def load_weight(place, arrays, held, sems):
    @pl.when(pl.program_id(0) == 0)
    def _():
        for copy in copies(place, arrays, held, sems):
            copy.start()
        for copy in copies(place, arrays, held, sems):
            copy.wait()


def rotated(raw, cosine, sine):
    front, back = raw[:HALF], raw[HALF:]
    return jnp.concatenate([front * cosine - back * sine, back * cosine + front * sine], axis=0)


def project(held, rows_in, cosine, sine, kv):
    raw = lax.dot_general(
        held[kv * KVROWS : (kv + 1) * KVROWS, :],
        rows_in,
        (((1,), (1,)), ((), ())),
        preferred_element_type=F32,
    )
    return [rotated(raw[h * HD : (h + 1) * HD], cosine, sine).astype(BF) for h in range(5)]


def student_kernel(place, x, cosine, sine, *rest):
    arrays, (out, held, sems) = rest[:8], rest[8:]
    load_weight(place, arrays, held, sems)
    for kv in range(2):
        for h, value in enumerate(project(held, x[...], cosine[...], sine[...], kv)):
            out[kv * KVROWS + h * HD : kv * KVROWS + (h + 1) * HD, :] = value


ANY = pl.BlockSpec(memory_space=pl.ANY)
TABLE = pl.BlockSpec((HALF, SEQ), lambda s, place: (0, 0))
ROWS = pl.BlockSpec((SEQ, D), lambda s, place: (s, 0))
COLUMNS = pl.BlockSpec((2 * KVROWS, SEQ), lambda s, place: (0, s))
HALF_COLUMNS = pl.BlockSpec((KVROWS, SEQ), lambda s, place: (0, s))


def student_projection(place, x, cosine, sine, arrays):
    count = x.shape[0] // SEQ
    return pl.pallas_call(
        student_kernel,
        grid_spec=pltpu.PrefetchScalarGridSpec(
            num_scalar_prefetch=1,
            grid=(count,),
            in_specs=[ROWS, TABLE, TABLE] + [ANY] * 8,
            out_specs=COLUMNS,
            scratch_shapes=[pltpu.VMEM((2 * KVROWS, D), BF), pltpu.SemaphoreType.DMA((40,))],
        ),
        out_shape=jax.ShapeDtypeStruct((2 * KVROWS, x.shape[0]), BF),
        compiler_params=params(56),
        cost_estimate=pl.CostEstimate(
            flops=2 * x.shape[0] * 2 * KVROWS * D, bytes_accessed=9 * 2**20, transcendentals=0
        ),
        name="student_projection",
    )(place, x, cosine, sine, *arrays)


GRID_SCALE = INV_ROOT * math.log2(math.e)


def softmax_parts(scores, diagonal):
    scores = scores * GRID_SCALE
    low = scores.shape[0] - HD
    masked = jnp.where(diagonal, scores[low:], MASKED)
    if low:
        scores = jnp.concatenate([scores[:low], masked], axis=0)
    else:
        scores = masked
    power = jnp.exp2(scores - jnp.max(scores, axis=0, keepdims=True))
    return power, (1.0 / HEADS) / jnp.sum(power, axis=0, keepdims=True)


def dot(a, b, dims=((1,), (0,))):
    return lax.dot_general(a, b, (dims, ((), ())), preferred_element_type=F32)


def side_by_side(heads, half):
    return jnp.concatenate([q[:, half * HD : (half + 1) * HD] for q in heads], axis=1)


def attention_gradient(student, teacher, cosine, sine):
    key_s = student[4]
    rows_s, rows_t = key_s.T, teacher[4].T
    lane = lax.broadcasted_iota(jnp.int32, (HD, 4 * HD), 1) % HD
    diagonal = lax.broadcasted_iota(jnp.int32, (HD, 4 * HD), 0) <= lane
    query_parts, key_grad = [], None
    for half in range(2):
        extent = (half + 1) * HD
        q_s = side_by_side(student[:4], half)
        q_t = side_by_side(teacher[:4], half)
        power_s, inverse_s = softmax_parts(dot(rows_s[:extent], q_s), diagonal)
        power_t, inverse_t = softmax_parts(dot(rows_t[:extent], q_t), diagonal)
        spread = (power_s * inverse_s - power_t * inverse_t).astype(BF)
        query_parts.append(dot(key_s[:, :extent], spread))
        part = dot(q_s, spread, ((1,), (1,)))
        if half == 0:
            key_grad = part
        else:
            key_grad = jnp.concatenate([part[:, :HD] + key_grad, part[:, HD:]], axis=1)
    grads = [
        jnp.concatenate([p[:, h * HD : (h + 1) * HD] for p in query_parts], axis=1)
        for h in range(4)
    ] + [key_grad]
    return [rotated(g * INV_ROOT, cosine, -sine).astype(BF) for g in grads]


def gradient_kernel(place, x, qk_student, cosine, sine, *rest):
    arrays, (out, out_other, held, grads, sems) = rest[:8], rest[8:]
    load_weight(place, arrays, held, sems)
    for kv in range(2):
        teacher = project(held, x[...], cosine[...], sine[...], kv)
        base = kv * KVROWS
        student = [qk_student[base + h * HD : base + (h + 1) * HD, :] for h in range(5)]
        for h, value in enumerate(attention_gradient(student, teacher, cosine[...], sine[...])):
            grads[base + h * HD : base + (h + 1) * HD, :] = value
    for n in range(40):
        row = pl.multiple_of(place[n] * UNIT, UNIT)
        target, at = (out, n) if n < 20 else (out_other, n - 20)
        target[at * UNIT : (at + 1) * UNIT, :] = grads[pl.ds(row, UNIT), :]


def projection_gradient(place, x, qk_student, cosine, sine, arrays):
    count = x.shape[0] // SEQ
    return pl.pallas_call(
        gradient_kernel,
        grid_spec=pltpu.PrefetchScalarGridSpec(
            num_scalar_prefetch=1,
            grid=(count,),
            in_specs=[ROWS, COLUMNS, TABLE, TABLE] + [ANY] * 8,
            out_specs=[HALF_COLUMNS] * 2,
            scratch_shapes=[
                pltpu.VMEM((2 * KVROWS, D), BF),
                pltpu.VMEM((2 * KVROWS, SEQ), BF),
                pltpu.SemaphoreType.DMA((40,)),
            ],
        ),
        out_shape=[jax.ShapeDtypeStruct((KVROWS, x.shape[0]), BF)] * 2,
        compiler_params=params(56),
        cost_estimate=pl.CostEstimate(
            flops=6 * x.shape[0] * 2 * KVROWS * D, bytes_accessed=9 * 2**20, transcendentals=0
        ),
        name="projection_gradient",
    )(place, x, qk_student, cosine, sine, *arrays)


TILE = 512


def weight_kernel(steps, own_a, own_b, other_a, other_b, xa, xb, ya, yb, *outs):
    for at, step in enumerate(steps):
        rows = slice(step * SHARD, (step + 1) * SHARD)
        total = dot(own_a[rows, :], xa[...])
        total += dot(own_b[rows, :], xb[...])
        total += dot(other_a[rows, :], ya[...])
        total += dot(other_b[rows, :], yb[...])
        total = total.astype(BF)
        for n, (low, high) in enumerate(PARTS):
            outs[at * 3 + n][...] = total[low:high]


def weight_gradient(steps, grads, tokens):
    whole = [pl.BlockSpec((KVROWS, 2 * SEQ), lambda t: (0, 0))] * 4
    return pl.pallas_call(
        lambda *refs: weight_kernel(steps, *refs),
        grid=(D // TILE,),
        in_specs=whole + [pl.BlockSpec((2 * SEQ, TILE), lambda t: (0, t))] * 4,
        out_specs=[pl.BlockSpec((h - l, TILE), lambda t: (0, t)) for l, h in PARTS] * len(steps),
        out_shape=[jax.ShapeDtypeStruct((h - l, D), BF) for l, h in PARTS] * len(steps),
        compiler_params=params(56),
        cost_estimate=pl.CostEstimate(
            flops=2 * len(steps) * SHARD * 8 * SEQ * D, bytes_accessed=12 * 2**20, transcendentals=0
        ),
        name="weight_gradient",
    )(*grads, *tokens)


def adam_kernel(table, *refs):
    position = pl.program_id(0)
    pieces, (weight, one, two, weight_out, one_out, two_out) = refs[:12], refs[12:]
    sums = []
    for n in range(3):
        a, b, c, d = (pieces[4 * n + s][...].astype(F32) for s in range(4))
        sums.append((a + b) + (c + d))
    gradient = jnp.where(position < 2, sums[0], jnp.where(position == 2, sums[1], sums[2]))
    first_new = BETA_ONE * one[...] + (1.0 - BETA_ONE) * gradient
    second_new = BETA_TWO * two[...] + (1.0 - BETA_TWO) * gradient * gradient
    step_dir = (
        first_new
        / (1.0 - BETA_ONE**STEP)
        / (jnp.sqrt(second_new / (1.0 - BETA_TWO**STEP)) + EPSILON)
    )
    master = weight[...]
    weight_out[...] = master - LEARN_RATE * (step_dir + DECAY * master)
    one_out[...] = first_new
    two_out[...] = second_new


def adam(order, pieces, weight, one, two):
    native = pl.BlockSpec((UNIT, D), lambda k, order: (order[k], 0))
    parts = [
        pl.BlockSpec((UNIT, D), lambda k, order: (jnp.minimum(k, 1), 0)),
        pl.BlockSpec((UNIT, D), lambda k, order: (0, 0)),
        pl.BlockSpec((UNIT, D), lambda k, order: (jnp.maximum(k - 3, 0), 0)),
    ]
    return pl.pallas_call(
        adam_kernel,
        grid_spec=pltpu.PrefetchScalarGridSpec(
            num_scalar_prefetch=1,
            grid=(5,),
            in_specs=[part for part in parts for _ in range(4)] + [native] * 3,
            out_specs=[native] * 3,
        ),
        out_shape=[jax.ShapeDtypeStruct((SHARD, D), F32)] * 3,
        compiler_params=params(56),
        name="adam",
    )(order, *pieces, weight, one, two)


def rotary_tables():
    positions = jnp.arange(SEQ).astype(F32)
    exponents = jnp.arange(HALF).astype(F32) * (2.0 / HD)
    frequency = THETA ** (-exponents)
    angles = frequency[:, None] * positions[None, :]
    return jnp.cos(angles), jnp.sin(angles)


def ring_gather(shard, up_again):
    below = send(shard, UP)
    above = send(shard, DOWN)
    far = send(below, UP) if up_again else send(above, DOWN)
    return [shard, above, far, below]


def both_cores(pieces):
    return pieces + [send(piece, TO_CORE) for piece in pieces]


def per_device(tokens, student_weight, snapshot, moment_one, moment_two):
    own_tokens = tokens[0]
    master = student_weight[0]
    me = lax.axis_index("fsdp")
    order = jnp.asarray(ORDER)[me]
    place = jnp.asarray(PLACE)[me]
    cosine, sine = rotary_tables()

    student_shard, teacher_shard = arrange(order, master, snapshot[0])
    row = lax.broadcasted_iota(jnp.int32, (SHARD, 1), 0)
    whole = (me == 7) | (me == 13)
    mask_a = ((me == 6) | (me == 14)) & (row >= 96)
    mask_b = ((me == 6) | (me == 12)) & (row >= 64) & (row < 96)

    def widen(part, low):
        return jnp.pad(part, ((low, SHARD - low - part.shape[0]), (0, 0)))

    swap_a = send(student_shard, SWAP_A)
    swap_b = send(student_shard[64:96], SWAP_B)
    main = send_next(teacher_shard, list(enumerate(OWNER)))
    plane_tokens = send(own_tokens, TO_PLANE)
    student = jnp.where(whole | mask_a, swap_a, jnp.where(mask_b, widen(swap_b, 64), student_shard))
    tail = send(main[96:], SWAP_PART)
    middle = send(main[64:96], SWAP_B)
    teacher = jnp.where(mask_a, widen(tail, 96), jnp.where(mask_b, widen(middle, 64), main))

    student_rows = both_cores(ring_gather(student, True))
    qk_own = student_projection(place, own_tokens, cosine, sine, student_rows)
    teacher_own = ring_gather(teacher, False)
    teacher_own[2], qk_own = lax.optimization_barrier((teacher_own[2], qk_own))
    teacher_rows = both_cores(teacher_own)
    qk_plane = student_projection(place, plane_tokens, cosine, sine, student_rows)
    core_tokens = send(own_tokens, TO_CORE)
    far_tokens = send(plane_tokens, TO_CORE)

    grads, others = [], []
    for x, qk_student in ((own_tokens, qk_own), (plane_tokens, qk_plane)):
        grad, other = projection_gradient(place, x, qk_student, cosine, sine, teacher_rows)
        grads.append(grad)
        others.append(send(other, TO_CORE))

    parts = grads + others
    all_tokens = (own_tokens, plane_tokens, core_tokens, far_tokens)

    def to_owner(blocks, step):
        out = []
        for part, block in enumerate(blocks):
            pairs = []
            for d in range(16):
                aligned = d // 8 * 8 + (d % 8 // 2 + step) % 4 * 2 + d % 2
                pairs.append((d, PART_OWNER[part][aligned]))
            out.append(send(block, pairs))
        return out

    two = weight_gradient((2,), parts, all_tokens)
    got = {2: to_owner(two, 2)}
    rest = weight_gradient((1, 3, 0), parts, all_tokens)
    for at, step in enumerate((1, 3, 0)):
        got[step] = to_owner(rest[at * 3 : at * 3 + 3], step)
    pieces = [got[step][part] for part in range(3) for step in range(4)]
    updated = adam(order, pieces, master, moment_one[0], moment_two[0])
    return tuple(value[None] for value in updated)


def solution(mesh):
    spec = P("blk", "fsdp", None)
    return jax.shard_map(
        per_device,
        mesh=mesh,
        in_specs=(spec,) * 5,
        out_specs=(spec,) * 3,
        check_vma=False,
    )
```

```python
import math

import jax
import jax.numpy as jnp
import numpy as np
from jax import lax
from jax.experimental import pallas as pl
from jax.experimental.pallas import tpu as pltpu
from jax.sharding import PartitionSpec as P

HEADS = 16
KVH = 4
HD = 128
SEQ = 256
STEP = 100
D = 2048
THETA = 500000.0
BETA_ONE = 0.9
BETA_TWO = 0.95
LEARN_RATE = 0.002
DECAY = 0.1
EPSILON = 1e-08
MASKED = -1e30

BF = jnp.bfloat16
F32 = jnp.float32
SHARD = 160
UNIT = 32
HALF = HD // 2
KVROWS = 640
INV_ROOT = 1.0 / math.sqrt(HD)

ARRANGED = [[5 * d + k for k in range(5)] for d in range(16)]
ARRANGED[12] = [60, 61, 64, 62, 63]
ARRANGED[14] = [72, 73, 74, 70, 71]
ALIGNED = [list(units) for units in ARRANGED]
ALIGNED[6] = [30, 31, 64, 70, 71]
ALIGNED[7] = [65, 66, 67, 68, 69]
ALIGNED[12] = [60, 61, 32, 62, 63]
ALIGNED[13] = [35, 36, 37, 38, 39]
ALIGNED[14] = [72, 73, 74, 33, 34]
OWNER = list(range(16))
OWNER[7], OWNER[13] = 13, 7
MIXED = [[64, 70, 71], [32, 33, 34]]


def head_position(unit, plane):
    if unit < 64:
        return (unit // 16 - 2 * plane) * 20 + unit % 16
    return ((unit - 64) // 4 - 2 * plane) * 20 + 16 + (unit - 64) % 4


def build_tables():
    order = np.array([[u - 5 * d for u in ARRANGED[d]] for d in range(16)], np.int32)
    place = np.zeros((16, 43), np.int32)
    slot = np.full((16, 3), -1, np.int32)
    for d in range(16):
        z, y, c = d // 8, d % 8 // 2, d % 2
        row = []
        for r in range(2):
            for step in range(4):
                other = 8 * z + 2 * ((y + step) % 4) + (c ^ r)
                row += [head_position(u, z) for u in ALIGNED[other]]
        assert sorted(row) == list(range(40))
        place[d] = row + [head_position(u, z) for u in MIXED[z]]
        if c == 0:
            for n, u in enumerate(MIXED[z]):
                (other,) = [e for e in range(16) if u in ALIGNED[e]]
                assert other // 8 == z and other % 2 == 0
                at = ALIGNED[other].index(u)
                assert ARRANGED[other][at] == MIXED[1 - z][n]
                slot[d, n] = (other % 8 // 2 - y) % 4 * SHARD + at * UNIT
    return order, place, slot


ORDER, PLACE, SLOT = build_tables()


def pairs_of(function):
    out = []
    for d in range(16):
        z, y, c = function(d // 8, d % 8 // 2, d % 2)
        out.append((d, z % 2 * 8 + y % 4 * 2 + c % 2))
    return out


TO_CORE = pairs_of(lambda z, y, c: (z, y, c + 1))
TO_PLANE = pairs_of(lambda z, y, c: (z + 1, y, c))
UP = pairs_of(lambda z, y, c: (z, y + 1, c))
DOWN = pairs_of(lambda z, y, c: (z, y - 1, c))
SWAP_A = [(7, 13), (13, 7), (6, 14), (14, 6)]
SWAP_PART = [(6, 14), (14, 6)]
SWAP_B = [(6, 12), (12, 6)]


def send(value, pairs):
    return lax.ppermute(value, "fsdp", pairs)


def send_next(value, pairs):
    return lax.ppermute(
        value,
        ("blk", "fsdp"),
        [(g * 16 + a, (g + 1) % 8 * 16 + b) for g in range(8) for a, b in pairs],
    )


def params(mib):
    return pltpu.CompilerParams(vmem_limit_bytes=mib * 2**20)


def arrange_kernel(order, weight, snapshot, weight_out, snapshot_out):
    weight_out[...] = weight[...].astype(BF)
    snapshot_out[...] = snapshot[...]


def arrange(order, weight, snapshot):
    picked = pl.BlockSpec((UNIT, D), lambda k, order: (order[k], 0))
    straight = pl.BlockSpec((UNIT, D), lambda k, order: (k, 0))
    return pl.pallas_call(
        arrange_kernel,
        grid_spec=pltpu.PrefetchScalarGridSpec(
            num_scalar_prefetch=1, grid=(5,), in_specs=[picked, picked], out_specs=[straight, straight]
        ),
        out_shape=[jax.ShapeDtypeStruct((SHARD, D), BF)] * 2,
        compiler_params=params(56),
        name="arrange",
    )(order, weight, snapshot)


def copies(place, arrays, held, sems):
    out = []
    for at, array in enumerate(arrays):
        for k in range(5):
            n = at * 5 + k
            row = pl.multiple_of(place[n] * UNIT, UNIT)
            out.append(
                pltpu.make_async_copy(
                    array.at[pl.ds(k * UNIT, UNIT)], held.at[pl.ds(row, UNIT)], sems.at[n]
                )
            )
    return out


def load_weight(place, arrays, held, sems):
    @pl.when(pl.program_id(0) == 0)
    def _():
        for copy in copies(place, arrays, held, sems):
            copy.start()
        for copy in copies(place, arrays, held, sems):
            copy.wait()


def rotated(raw, cosine, sine):
    front, back = raw[:HALF], raw[HALF:]
    return jnp.concatenate([front * cosine - back * sine, back * cosine + front * sine], axis=0)


def project(held, rows_in, cosine, sine, kv):
    raw = lax.dot_general(
        held[kv * KVROWS : (kv + 1) * KVROWS, :],
        rows_in,
        (((1,), (1,)), ((), ())),
        preferred_element_type=F32,
    )
    return [rotated(raw[h * HD : (h + 1) * HD], cosine, sine).astype(BF) for h in range(5)]


def student_kernel(place, x, cosine, sine, *rest):
    arrays, (out, held, sems) = rest[:8], rest[8:]
    load_weight(place, arrays, held, sems)
    for kv in range(2):
        for h, value in enumerate(project(held, x[...], cosine[...], sine[...], kv)):
            out[kv * KVROWS + h * HD : kv * KVROWS + (h + 1) * HD, :] = value


ANY = pl.BlockSpec(memory_space=pl.ANY)
TABLE = pl.BlockSpec((HALF, SEQ), lambda s, place: (0, 0))
ROWS = pl.BlockSpec((SEQ, D), lambda s, place: (s, 0))
COLUMNS = pl.BlockSpec((2 * KVROWS, SEQ), lambda s, place: (0, s))
HALF_COLUMNS = pl.BlockSpec((KVROWS, SEQ), lambda s, place: (0, s))
MIXED_COLUMNS = pl.BlockSpec((3 * UNIT, SEQ), lambda s, place: (0, s))


def student_projection(place, x, cosine, sine, arrays):
    count = x.shape[0] // SEQ
    return pl.pallas_call(
        student_kernel,
        grid_spec=pltpu.PrefetchScalarGridSpec(
            num_scalar_prefetch=1,
            grid=(count,),
            in_specs=[ROWS, TABLE, TABLE] + [ANY] * 8,
            out_specs=COLUMNS,
            scratch_shapes=[pltpu.VMEM((2 * KVROWS, D), BF), pltpu.SemaphoreType.DMA((40,))],
        ),
        out_shape=jax.ShapeDtypeStruct((2 * KVROWS, x.shape[0]), BF),
        compiler_params=params(56),
        cost_estimate=pl.CostEstimate(
            flops=2 * x.shape[0] * 2 * KVROWS * D, bytes_accessed=9 * 2**20, transcendentals=0
        ),
        name="student_projection",
    )(place, x, cosine, sine, *arrays)


GRID_SCALE = INV_ROOT * math.log2(math.e)


def softmax_parts(scores, diagonal):
    scores = scores * GRID_SCALE
    low = scores.shape[0] - HD
    masked = jnp.where(diagonal, scores[low:], MASKED)
    if low:
        scores = jnp.concatenate([scores[:low], masked], axis=0)
    else:
        scores = masked
    power = jnp.exp2(scores - jnp.max(scores, axis=0, keepdims=True))
    return power, (1.0 / HEADS) / jnp.sum(power, axis=0, keepdims=True)


def dot(a, b, dims=((1,), (0,))):
    return lax.dot_general(a, b, (dims, ((), ())), preferred_element_type=F32)


def side_by_side(heads, half):
    return jnp.concatenate([q[:, half * HD : (half + 1) * HD] for q in heads], axis=1)


def attention_gradient(student, teacher, cosine, sine):
    key_s = student[4]
    rows_s, rows_t = key_s.T, teacher[4].T
    lane = lax.broadcasted_iota(jnp.int32, (HD, 4 * HD), 1) % HD
    diagonal = lax.broadcasted_iota(jnp.int32, (HD, 4 * HD), 0) <= lane
    query_parts, key_grad = [], None
    for half in range(2):
        extent = (half + 1) * HD
        q_s = side_by_side(student[:4], half)
        q_t = side_by_side(teacher[:4], half)
        power_s, inverse_s = softmax_parts(dot(rows_s[:extent], q_s), diagonal)
        power_t, inverse_t = softmax_parts(dot(rows_t[:extent], q_t), diagonal)
        spread = (power_s * inverse_s - power_t * inverse_t).astype(BF)
        query_parts.append(dot(key_s[:, :extent], spread))
        part = dot(q_s, spread, ((1,), (1,)))
        if half == 0:
            key_grad = part
        else:
            key_grad = jnp.concatenate([part[:, :HD] + key_grad, part[:, HD:]], axis=1)
    grads = [
        jnp.concatenate([p[:, h * HD : (h + 1) * HD] for p in query_parts], axis=1)
        for h in range(4)
    ] + [key_grad]
    return [rotated(g * INV_ROOT, cosine, -sine).astype(BF) for g in grads]


def gradient_kernel(place, x, qk_student, cosine, sine, *rest):
    arrays, (out, out_other, out_mixed, held, grads, sems) = rest[:8], rest[8:]
    load_weight(place, arrays, held, sems)
    for kv in range(2):
        teacher = project(held, x[...], cosine[...], sine[...], kv)
        base = kv * KVROWS
        student = [qk_student[base + h * HD : base + (h + 1) * HD, :] for h in range(5)]
        for h, value in enumerate(attention_gradient(student, teacher, cosine[...], sine[...])):
            grads[base + h * HD : base + (h + 1) * HD, :] = value
    for n in range(43):
        row = pl.multiple_of(place[n] * UNIT, UNIT)
        target, at = ((out, n), (out_other, n - 20), (out_mixed, n - 40))[n // 20]
        target[at * UNIT : (at + 1) * UNIT, :] = grads[pl.ds(row, UNIT), :]


def projection_gradient(place, x, qk_student, cosine, sine, arrays):
    count = x.shape[0] // SEQ
    return pl.pallas_call(
        gradient_kernel,
        grid_spec=pltpu.PrefetchScalarGridSpec(
            num_scalar_prefetch=1,
            grid=(count,),
            in_specs=[ROWS, COLUMNS, TABLE, TABLE] + [ANY] * 8,
            out_specs=[HALF_COLUMNS] * 2 + [MIXED_COLUMNS],
            scratch_shapes=[
                pltpu.VMEM((2 * KVROWS, D), BF),
                pltpu.VMEM((2 * KVROWS, SEQ), BF),
                pltpu.SemaphoreType.DMA((40,)),
            ],
        ),
        out_shape=[jax.ShapeDtypeStruct((rows, x.shape[0]), BF) for rows in (KVROWS, KVROWS, 3 * UNIT)],
        compiler_params=params(56),
        cost_estimate=pl.CostEstimate(
            flops=6 * x.shape[0] * 2 * KVROWS * D, bytes_accessed=9 * 2**20, transcendentals=0
        ),
        name="projection_gradient",
    )(place, x, qk_student, cosine, sine, *arrays)


TILE = 512


def weight_kernel(steps, slot, *refs):
    grads, mixed, tokens, outs, held = refs[:4], refs[4:8], refs[8:12], refs[12:-1], refs[-1]
    span = 2 * SEQ

    @pl.when(pl.program_id(0) == 0)
    def _():
        for n in range(4):
            held[:, n * span : (n + 1) * span] = grads[n][...]

        @pl.when(slot[0] >= 0)
        def _():
            for u in range(3):
                row = pl.multiple_of(slot[u], UNIT)
                for n in range(4):
                    unit = mixed[n][u * UNIT : (u + 1) * UNIT, :]
                    held[pl.ds(row, UNIT), n * span : (n + 1) * span] = unit

    for step, out in zip(steps, outs):
        rows = slice(step * SHARD, (step + 1) * SHARD)
        total = dot(held[rows, :span], tokens[0][...])
        for n in range(1, 4):
            total += dot(held[rows, n * span : (n + 1) * span], tokens[n][...])
        out[...] = total.astype(BF)


def weight_gradient(steps, slot, grads, mixed, tokens):
    span = 2 * SEQ
    return pl.pallas_call(
        lambda *refs: weight_kernel(steps, *refs),
        grid_spec=pltpu.PrefetchScalarGridSpec(
            num_scalar_prefetch=1,
            grid=(D // TILE,),
            in_specs=[pl.BlockSpec((KVROWS, span), lambda t, slot: (0, 0))] * 4
            + [pl.BlockSpec((3 * UNIT, span), lambda t, slot: (0, 0))] * 4
            + [pl.BlockSpec((span, TILE), lambda t, slot: (0, t))] * 4,
            out_specs=[pl.BlockSpec((SHARD, TILE), lambda t, slot: (0, t))] * len(steps),
            scratch_shapes=[pltpu.VMEM((KVROWS, 4 * span), BF)],
        ),
        out_shape=[jax.ShapeDtypeStruct((SHARD, D), BF)] * len(steps),
        compiler_params=params(56),
        cost_estimate=pl.CostEstimate(
            flops=2 * len(steps) * SHARD * 8 * SEQ * D, bytes_accessed=12 * 2**20, transcendentals=0
        ),
        name="weight_gradient",
    )(slot, *grads, *mixed, *tokens)


def adam_kernel(order, a, b, c, d, weight, one, two, weight_out, one_out, two_out):
    gradient = (a[...].astype(F32) + b[...].astype(F32)) + (c[...].astype(F32) + d[...].astype(F32))
    first_new = BETA_ONE * one[...] + (1.0 - BETA_ONE) * gradient
    second_new = BETA_TWO * two[...] + (1.0 - BETA_TWO) * gradient * gradient
    step_dir = (
        first_new
        / (1.0 - BETA_ONE**STEP)
        / (jnp.sqrt(second_new / (1.0 - BETA_TWO**STEP)) + EPSILON)
    )
    master = weight[...]
    weight_out[...] = master - LEARN_RATE * (step_dir + DECAY * master)
    one_out[...] = first_new
    two_out[...] = second_new


def adam(order, blocks, weight, one, two):
    native = pl.BlockSpec((UNIT, D // 2), lambda k, h, order: (order[k], h))
    straight = pl.BlockSpec((UNIT, D // 2), lambda k, h, order: (k, h))
    return pl.pallas_call(
        adam_kernel,
        grid_spec=pltpu.PrefetchScalarGridSpec(
            num_scalar_prefetch=1,
            grid=(5, 2),
            in_specs=[straight] * 4 + [native] * 3,
            out_specs=[native] * 3,
        ),
        out_shape=[jax.ShapeDtypeStruct((SHARD, D), F32)] * 3,
        compiler_params=params(56),
        name="adam",
    )(order, *blocks, weight, one, two)


def rotary_tables():
    positions = jnp.arange(SEQ).astype(F32)
    exponents = jnp.arange(HALF).astype(F32) * (2.0 / HD)
    frequency = THETA ** (-exponents)
    angles = frequency[:, None] * positions[None, :]
    return jnp.cos(angles), jnp.sin(angles)


def ring_gather(shard, up_again):
    below = send(shard, UP)
    above = send(shard, DOWN)
    far = send(below, UP) if up_again else send(above, DOWN)
    return [shard, above, far, below]


def both_cores(pieces):
    return pieces + [send(piece, TO_CORE) for piece in pieces]


def per_device(tokens, student_weight, snapshot, moment_one, moment_two):
    own_tokens = tokens[0]
    master = student_weight[0]
    me = lax.axis_index("fsdp")
    order = jnp.asarray(ORDER)[me]
    place = jnp.asarray(PLACE)[me]
    slot = jnp.asarray(SLOT)[me]
    cosine, sine = rotary_tables()

    student_shard, teacher_shard = arrange(order, master, snapshot[0])
    row = lax.broadcasted_iota(jnp.int32, (SHARD, 1), 0)
    whole = (me == 7) | (me == 13)
    mask_a = ((me == 6) | (me == 14)) & (row >= 96)
    mask_b = ((me == 6) | (me == 12)) & (row >= 64) & (row < 96)

    def widen(part, low):
        return jnp.pad(part, ((low, SHARD - low - part.shape[0]), (0, 0)))

    swap_a = send(student_shard, SWAP_A)
    swap_b = send(student_shard[64:96], SWAP_B)
    main = send_next(teacher_shard, list(enumerate(OWNER)))
    tail = send_next(teacher_shard[96:], SWAP_PART)
    middle = send_next(teacher_shard[64:96], SWAP_B)
    plane_tokens = send(own_tokens, TO_PLANE)
    student = jnp.where(whole | mask_a, swap_a, jnp.where(mask_b, widen(swap_b, 64), student_shard))
    student_too, main, tail, middle = lax.optimization_barrier((student, main, tail, middle))
    teacher = jnp.where(mask_a, widen(tail, 96), jnp.where(mask_b, widen(middle, 64), main))

    student_own = ring_gather(student, True)
    student_rows = student_own + [send(p, TO_CORE) for p in [student_too] + student_own[1:]]
    qk_own = student_projection(place, own_tokens, cosine, sine, student_rows)
    teacher_own = ring_gather(teacher, False)
    teacher_own[2], qk_own = lax.optimization_barrier((teacher_own[2], qk_own))
    teacher_rows = both_cores(teacher_own)
    qk_plane = student_projection(place, plane_tokens, cosine, sine, student_rows)
    core_tokens = send(own_tokens, TO_CORE)
    far_tokens = send(plane_tokens, TO_CORE)

    grads, others, given = [], [], []
    for x, qk_student in ((own_tokens, qk_own), (plane_tokens, qk_plane)):
        grad, other, mixed = projection_gradient(place, x, qk_student, cosine, sine, teacher_rows)
        grads.append(grad)
        others.append(send(other, TO_CORE))
        given.append(send(mixed, TO_PLANE))
    received = given[::-1]
    parts = grads + others
    mixed_parts = received + [send(value, TO_CORE) for value in received]
    all_tokens = (own_tokens, plane_tokens, core_tokens, far_tokens)

    def to_owner(block, step):
        pairs = []
        for d in range(16):
            pairs.append((d, OWNER[d // 8 * 8 + (d % 8 // 2 + step) % 4 * 2 + d % 2]))
        return send(block, pairs)

    blocks = []
    for steps in ((2,), (1, 3, 0)):
        made = weight_gradient(steps, slot, parts, mixed_parts, all_tokens)
        blocks += [to_owner(block, step) for block, step in zip(made, steps)]
    updated = adam(order, blocks, master, moment_one[0], moment_two[0])
    return tuple(value[None] for value in updated)


def solution(mesh):
    spec = P("blk", "fsdp", None)
    return jax.shard_map(
        per_device,
        mesh=mesh,
        in_specs=(spec,) * 5,
        out_specs=(spec,) * 3,
        check_vma=False,
    )
```

```python
import math

import jax
import jax.numpy as jnp
import numpy as np
from jax import lax
from jax.experimental import pallas as pl
from jax.experimental.pallas import tpu as pltpu
from jax.sharding import PartitionSpec as P

HEADS = 16
KVH = 4
HD = 128
SEQ = 256
STEP = 100
D = 2048
THETA = 500000.0
BETA_ONE = 0.9
BETA_TWO = 0.95
LEARN_RATE = 0.002
DECAY = 0.1
EPSILON = 1e-08
MASKED = -1e30

BF = jnp.bfloat16
F32 = jnp.float32
SHARD = 160
ROWS = 8 * SHARD
UNIT = 32
HALF = HD // 2
CORE = 4 * SHARD
EXCHANGED = 2 * HD
INV_ROOT = 1.0 / math.sqrt(HD)

AT_WEIGHT, AT_GIVEN, AT_QUERY, AT_KEY, AT_CORE, AT_STEP, AT_FILL = 0, 8, 9, 17, 19, 27, 31
GIVEN = (1024, 768)
QUERY = (tuple(range(8)), (10, 11, 0, 1, 2, 3, 4, 5))
KEY = ((10, 11), (8, 9))


def build_table():
    table = np.zeros((16, 39), np.int32)
    for d in range(16):
        z, y, c = d // 8, d % 8 // 2, d % 2
        gathered = [320 * ((y + s) % 4) + 160 * (c ^ r) for r in range(2) for s in range(4)]
        cores = [320 * k + 160 * (c ^ r) for r in range(2) for k in range(4)]
        steps = [160 * ((y + s) % 4) for s in range(4)]
        fill = []
        for unit in range(8):
            row = GIVEN[z] + UNIT * unit
            mine = row % 320 // 160 == c
            fill.append(row // 320 * 160 + row % 160 if mine else -1)
        table[d] = gathered + [GIVEN[z], *QUERY[z], *KEY[z]] + cores + steps + fill
    return table


TABLE = build_table()


def pairs_of(function):
    out = []
    for d in range(16):
        z, y, c = function(d // 8, d % 8 // 2, d % 2)
        out.append((d, z % 2 * 8 + y % 4 * 2 + c % 2))
    return out


TO_CORE = pairs_of(lambda z, y, c: (z, y, c + 1))
TO_PLANE = pairs_of(lambda z, y, c: (z + 1, y, c))
ALONG_Y = [pairs_of(lambda z, y, c, s=s: (z, y + s, c)) for s in range(4)]


def send(value, pairs):
    return lax.ppermute(value, "fsdp", pairs)


def params(mib):
    return pltpu.CompilerParams(vmem_limit_bytes=mib * 2**20)


def cost(flops, mib):
    return pl.CostEstimate(flops=flops, bytes_accessed=mib * 2**20, transcendentals=0)


def dot(a, b, dims=((1,), (0,))):
    return lax.dot_general(a, b, (dims, ((), ())), preferred_element_type=F32)


def rotated(raw, cosine, sine):
    front, back = raw[:HALF], raw[HALF:]
    return jnp.concatenate([front * cosine - back * sine, back * cosine + front * sine], axis=0)


ANY = pl.BlockSpec(memory_space=pl.ANY)
ANGLES = pl.BlockSpec((HALF, SEQ), lambda s, table: (0, 0))
TOKENS = pl.BlockSpec((SEQ, D), lambda s, table: (s, 0))


def columns(rows):
    return pl.BlockSpec((rows, SEQ), lambda s, table: (0, s))


def project_kernel(table, x, cosine, sine, *rest):
    arrays, (out, given, held, raw, sems) = rest[:8], rest[8:]
    first = pl.program_id(0) == 0

    def copy(n):
        rows = pl.ds(n * SHARD, SHARD)
        return pltpu.make_async_copy(arrays[n], held.at[rows], sems.at[n])

    @pl.when(first)
    def _():
        for n in range(8):
            copy(n).start()

    for half in range(2):

        @pl.when(first)
        def _():
            for n in range(4):
                copy(half * 4 + n).wait()

        part = dot(held[half * CORE : (half + 1) * CORE, :], x[...], ((1,), (1,)))
        for n in range(4):
            row = pl.multiple_of(table[AT_WEIGHT + half * 4 + n], SHARD)
            raw[pl.ds(row, SHARD), :] = part[n * SHARD : (n + 1) * SHARD]
    for h in range(10):
        rows = slice(h * HD, (h + 1) * HD)
        out[rows, :] = rotated(raw[rows, :], cosine[...], sine[...]).astype(BF)
    given[...] = out[pl.ds(pl.multiple_of(table[AT_GIVEN], EXCHANGED), EXCHANGED), :]


def project(table, x, cosine, sine, arrays):
    count = x.shape[0]
    return pl.pallas_call(
        project_kernel,
        grid_spec=pltpu.PrefetchScalarGridSpec(
            num_scalar_prefetch=1,
            grid=(count // SEQ,),
            in_specs=[TOKENS, ANGLES, ANGLES] + [ANY] * 8,
            out_specs=[columns(ROWS), columns(EXCHANGED)],
            scratch_shapes=[
                pltpu.VMEM((ROWS, D), BF),
                pltpu.VMEM((ROWS, SEQ), F32),
                pltpu.SemaphoreType.DMA((8,)),
            ],
        ),
        out_shape=[jax.ShapeDtypeStruct((rows, count), BF) for rows in (ROWS, EXCHANGED)],
        compiler_params=params(56),
        cost_estimate=cost(2 * count * ROWS * D, 9),
        name="project",
    )(table, x, cosine, sine, *arrays)


SCALE = INV_ROOT * math.log2(math.e)


def softmax_parts(scores, diagonal):
    scores = scores * SCALE
    low = scores.shape[0] - HD
    masked = jnp.where(diagonal, scores[low:], MASKED)
    if low:
        scores = jnp.concatenate([scores[:low], masked], axis=0)
    else:
        scores = masked
    power = jnp.exp2(scores - jnp.max(scores, axis=0, keepdims=True))
    return power, (1.0 / HEADS) / jnp.sum(power, axis=0, keepdims=True)


def side_by_side(heads, half):
    return jnp.concatenate([q[:, half * HD : (half + 1) * HD] for q in heads], axis=1)


def attention_gradient(student, teacher, cosine, sine):
    key_s = student[4]
    rows_s, rows_t = key_s.T, teacher[4].T
    lane = lax.broadcasted_iota(jnp.int32, (HD, 4 * HD), 1) % HD
    diagonal = lax.broadcasted_iota(jnp.int32, (HD, 4 * HD), 0) <= lane
    query_parts, key_grad = [], None
    for half in range(2):
        extent = (half + 1) * HD
        q_s = side_by_side(student[:4], half)
        q_t = side_by_side(teacher[:4], half)
        power_s, inverse_s = softmax_parts(dot(rows_s[:extent], q_s), diagonal)
        power_t, inverse_t = softmax_parts(dot(rows_t[:extent], q_t), diagonal)
        spread = (power_s * inverse_s - power_t * inverse_t).astype(BF)
        query_parts.append(dot(key_s[:, :extent], spread))
        part = dot(q_s, spread, ((1,), (1,)))
        if half == 0:
            key_grad = part
        else:
            key_grad = jnp.concatenate([part[:, :HD] + key_grad, part[:, HD:]], axis=1)
    grads = [
        jnp.concatenate([p[:, h * HD : (h + 1) * HD] for p in query_parts], axis=1)
        for h in range(4)
    ] + [key_grad]
    return [rotated(g * INV_ROOT, cosine, -sine).astype(BF) for g in grads]


def attend_kernel(table, own_s, got_s, own_t, got_t, cosine, sine, out, other, back, both_s, both_t, grads):
    for both, own, got in ((both_s, own_s, got_s), (both_t, own_t, got_t)):
        both[:ROWS, :] = own[...]
        both[ROWS:, :] = got[...]
    for kv in range(2):
        blocks = [table[AT_QUERY + 4 * kv + h] for h in range(4)] + [table[AT_KEY + kv]]
        rows = [pl.ds(pl.multiple_of(block * HD, HD), HD) for block in blocks]
        student = [both_s[at, :] for at in rows]
        teacher = [both_t[at, :] for at in rows]
        for at, value in zip(rows, attention_gradient(student, teacher, cosine[...], sine[...])):
            grads[at, :] = value
    for n in range(8):
        row = pl.multiple_of(table[AT_CORE + n], SHARD)
        target = out if n < 4 else other
        target[n % 4 * SHARD : (n % 4 + 1) * SHARD, :] = grads[pl.ds(row, SHARD), :]
    back[...] = grads[ROWS:, :]


def attend(table, student, teacher, cosine, sine):
    count = student[0].shape[1]
    wide = ROWS + EXCHANGED
    return pl.pallas_call(
        attend_kernel,
        grid_spec=pltpu.PrefetchScalarGridSpec(
            num_scalar_prefetch=1,
            grid=(count // SEQ,),
            in_specs=[columns(ROWS), columns(EXCHANGED)] * 2 + [ANGLES, ANGLES],
            out_specs=[columns(CORE), columns(CORE), columns(EXCHANGED)],
            scratch_shapes=[pltpu.VMEM((wide, SEQ), BF)] * 3,
        ),
        out_shape=[jax.ShapeDtypeStruct((rows, count), BF) for rows in (CORE, CORE, EXCHANGED)],
        compiler_params=params(56),
        cost_estimate=cost(12 * count * SEQ * HD * 8, 8),
        name="attend",
    )(table, *student, *teacher, cosine, sine)


TILE = 512
SPAN = 2 * SEQ


def weight_kernel(steps, table, *refs):
    grads, backs, tokens, outs, held = refs[:4], refs[4:8], refs[8:12], refs[12:-1], refs[-1]

    @pl.when(pl.program_id(0) == 0)
    def _():
        for n in range(4):
            held[:, n * SPAN : (n + 1) * SPAN] = grads[n][...]
        for unit in range(8):
            row = table[AT_FILL + unit]

            @pl.when(row >= 0)
            def _():
                at = pl.ds(pl.multiple_of(row, UNIT), UNIT)
                for n in range(4):
                    value = backs[n][unit * UNIT : (unit + 1) * UNIT, :]
                    held[at, n * SPAN : (n + 1) * SPAN] = value

    for step, out in zip(steps, outs):
        rows = pl.ds(pl.multiple_of(table[AT_STEP + step], SHARD), SHARD)
        total = dot(held[rows, :SPAN], tokens[0][...])
        for n in range(1, 4):
            total += dot(held[rows, n * SPAN : (n + 1) * SPAN], tokens[n][...])
        out[...] = total.astype(BF)


def weight_gradient(steps, table, grads, backs, tokens):
    return pl.pallas_call(
        lambda *refs: weight_kernel(steps, *refs),
        grid_spec=pltpu.PrefetchScalarGridSpec(
            num_scalar_prefetch=1,
            grid=(D // TILE,),
            in_specs=[pl.BlockSpec((CORE, SPAN), lambda t, table: (0, 0))] * 4
            + [pl.BlockSpec((EXCHANGED, SPAN), lambda t, table: (0, 0))] * 4
            + [pl.BlockSpec((SPAN, TILE), lambda t, table: (0, t))] * 4,
            out_specs=[pl.BlockSpec((SHARD, TILE), lambda t, table: (0, t))] * len(steps),
            scratch_shapes=[pltpu.VMEM((CORE, 4 * SPAN), BF)],
        ),
        out_shape=[jax.ShapeDtypeStruct((SHARD, D), BF)] * len(steps),
        compiler_params=params(56),
        cost_estimate=cost(2 * len(steps) * SHARD * 4 * SPAN * D, 12),
        name="weight_gradient",
    )(table, *grads, *backs, *tokens)


def adam_kernel(a, b, c, d, weight, one, two, weight_out, one_out, two_out):
    gradient = (a[...].astype(F32) + b[...].astype(F32)) + (c[...].astype(F32) + d[...].astype(F32))
    first_new = BETA_ONE * one[...] + (1.0 - BETA_ONE) * gradient
    second_new = BETA_TWO * two[...] + (1.0 - BETA_TWO) * gradient * gradient
    step_dir = (
        first_new
        / (1.0 - BETA_ONE**STEP)
        / (jnp.sqrt(second_new / (1.0 - BETA_TWO**STEP)) + EPSILON)
    )
    master = weight[...]
    weight_out[...] = master - LEARN_RATE * (step_dir + DECAY * master)
    one_out[...] = first_new
    two_out[...] = second_new


def adam(blocks, weight, one, two):
    block = pl.BlockSpec((UNIT, D), lambda k: (k, 0))
    return pl.pallas_call(
        adam_kernel,
        grid=(SHARD // UNIT,),
        in_specs=[block] * 7,
        out_specs=[block] * 3,
        out_shape=[jax.ShapeDtypeStruct((SHARD, D), F32)] * 3,
        compiler_params=params(56),
        name="adam",
    )(*blocks, weight, one, two)


def rotary_tables():
    positions = jnp.arange(SEQ).astype(F32)
    exponents = jnp.arange(HALF).astype(F32) * (2.0 / HD)
    frequency = THETA ** (-exponents)
    angles = frequency[:, None] * positions[None, :]
    return jnp.cos(angles), jnp.sin(angles)


def ring_gather(shard, up_again):
    below = send(shard, ALONG_Y[1])
    above = send(shard, ALONG_Y[3])
    far = send(below, ALONG_Y[1]) if up_again else send(above, ALONG_Y[3])
    return [shard, above, far, below]


def both_cores(pieces):
    return pieces + [send(piece, TO_CORE) for piece in pieces]


def per_device(tokens, student_weight, snapshot, moment_one, moment_two):
    own_tokens = tokens[0]
    master = student_weight[0]
    table = jnp.asarray(TABLE)[lax.axis_index("fsdp")]
    cosine, sine = rotary_tables()

    teacher = lax.ppermute(snapshot[0], "blk", [(g, (g + 1) % 8) for g in range(8)])
    plane_tokens = send(own_tokens, TO_PLANE)
    halves = (own_tokens, plane_tokens)
    student_rows = both_cores(ring_gather(master.astype(BF), True))
    teacher_own = ring_gather(teacher, False)
    core_tokens = send(own_tokens, TO_CORE)
    far_tokens = send(plane_tokens, TO_CORE)

    def crossed(both):
        received = [send(given, TO_PLANE) for _, given in both]
        return [(both[half][0], received[1 - half]) for half in range(2)]

    student = [project(table, own_tokens, cosine, sine, student_rows)]
    teacher_own[2], _ = lax.optimization_barrier((teacher_own[2], student[0][0]))
    teacher_rows = both_cores(teacher_own)
    student.append(project(table, plane_tokens, cosine, sine, student_rows))
    student = crossed(student)
    teacher = crossed([project(table, x, cosine, sine, teacher_rows) for x in halves])

    grads, others, backs = [], [], []
    for half in range(2):
        grad, other, back = attend(table, student[half], teacher[half], cosine, sine)
        grads.append(grad)
        others.append(send(other, TO_CORE))
        backs.append(send(back, TO_PLANE))
    backs = backs[::-1]
    parts = grads + others
    backs += [send(value, TO_CORE) for value in backs]
    all_tokens = (own_tokens, plane_tokens, core_tokens, far_tokens)

    blocks = []
    for steps in ((2,), (1, 3, 0)):
        made = weight_gradient(steps, table, parts, backs, all_tokens)
        blocks += [send(block, ALONG_Y[s]) if s else block for block, s in zip(made, steps)]
    updated = adam(blocks, master, moment_one[0], moment_two[0])
    return tuple(value[None] for value in updated)


def solution(mesh):
    spec = P("blk", "fsdp", None)
    return jax.shard_map(
        per_device,
        mesh=mesh,
        in_specs=(spec,) * 5,
        out_specs=(spec,) * 3,
        check_vma=False,
    )
```

```python
import math

import jax
import jax.numpy as jnp
import numpy as np
from jax import lax
from jax.experimental import pallas as pl
from jax.experimental.pallas import tpu as pltpu
from jax.sharding import PartitionSpec as P

HEADS = 16
KVH = 4
HD = 128
SEQ = 256
STEP = 100
D = 2048
THETA = 500000.0
BETA_ONE = 0.9
BETA_TWO = 0.95
LEARN_RATE = 0.002
DECAY = 0.1
EPSILON = 1e-08
MASKED = -1e30

BF = jnp.bfloat16
F32 = jnp.float32
SHARD = 160
ROWS = 8 * SHARD
UNIT = 32
HALF = HD // 2
CORE = 4 * SHARD
EXCHANGED = 2 * HD
INV_ROOT = 1.0 / math.sqrt(HD)

AT_WEIGHT, AT_GIVEN, AT_QUERY, AT_KEY, AT_CORE, AT_STEP, AT_FILL = 0, 8, 9, 17, 19, 27, 31
GIVEN = (1024, 768)
QUERY = (tuple(range(8)), (10, 11, 0, 1, 2, 3, 4, 5))
KEY = ((10, 11), (8, 9))


def build_table():
    table = np.zeros((16, 39), np.int32)
    for d in range(16):
        z, y, c = d // 8, d % 8 // 2, d % 2
        gathered = [320 * ((y + s) % 4) + 160 * (c ^ r) for r in range(2) for s in range(4)]
        cores = [320 * k + 160 * (c ^ r) for r in range(2) for k in range(4)]
        steps = [160 * ((y + s) % 4) for s in range(4)]
        fill = []
        for unit in range(8):
            row = GIVEN[z] + UNIT * unit
            mine = row % 320 // 160 == c
            fill.append(row // 320 * 160 + row % 160 if mine else -1)
        table[d] = gathered + [GIVEN[z], *QUERY[z], *KEY[z]] + cores + steps + fill
    return table


TABLE = build_table()


def pairs_of(function):
    out = []
    for d in range(16):
        z, y, c = function(d // 8, d % 8 // 2, d % 2)
        out.append((d, z % 2 * 8 + y % 4 * 2 + c % 2))
    return out


TO_CORE = pairs_of(lambda z, y, c: (z, y, c + 1))
TO_PLANE = pairs_of(lambda z, y, c: (z + 1, y, c))
ALONG_Y = [pairs_of(lambda z, y, c, s=s: (z, y + s, c)) for s in range(4)]


def send(value, pairs):
    return lax.ppermute(value, "fsdp", pairs)


def params(mib):
    return pltpu.CompilerParams(vmem_limit_bytes=mib * 2**20)


def cost(microseconds):
    return pl.CostEstimate(flops=int(microseconds * 1e9), bytes_accessed=2**20, transcendentals=0)


def dot(a, b, dims=((1,), (0,))):
    return lax.dot_general(a, b, (dims, ((), ())), preferred_element_type=F32)


def rotated(raw, cosine, sine):
    front, back = raw[:HALF], raw[HALF:]
    return jnp.concatenate([front * cosine - back * sine, back * cosine + front * sine], axis=0)


ANY = pl.BlockSpec(memory_space=pl.ANY)


def block(shape, row=0, column=0):
    return pl.BlockSpec(shape, lambda s, table: (row, column))


def call(kernel, name, operands, outs, scratch, microseconds):
    return pl.pallas_call(
        kernel,
        grid_spec=pltpu.PrefetchScalarGridSpec(
            num_scalar_prefetch=1,
            grid=(1,),
            in_specs=[spec for _, spec in operands[1:]],
            out_specs=[block(shape) for shape, _ in outs],
            scratch_shapes=scratch,
        ),
        out_shape=[jax.ShapeDtypeStruct(shape, dtype) for shape, dtype in outs],
        compiler_params=params(56),
        cost_estimate=cost(microseconds),
        name=name,
    )(*[value for value, _ in operands])


def project_kernel(jobs, groups, x_count, set_count, table, *refs):
    refs = list(refs)
    carried, refs = refs[0], refs[1:]
    xs, refs = refs[:x_count], refs[x_count:]
    cosine, sine, refs = refs[0], refs[1], refs[2:]
    arrays, refs = refs[: 8 * set_count], refs[8 * set_count :]
    outs, refs = refs[: len(jobs)], refs[len(jobs) :]
    givens, refs = refs[: len(groups)], refs[len(groups) :]
    held, sems = refs[:-1], refs[-1]

    def copy(at, n):
        rows = pl.ds(pl.multiple_of(table[AT_WEIGHT + n], SHARD), SHARD)
        return pltpu.make_async_copy(arrays[8 * at + n], held[at].at[rows], sems.at[8 * at + n])

    for at in range(set_count):
        for n in range(8):
            copy(at, n).start()
    for at in range(set_count):
        for n in range(8):
            copy(at, n).wait()
        for job, (x, own_set) in enumerate(jobs):
            if own_set != at:
                continue
            for half in range(2):
                part = dot(held[at][half * CORE : (half + 1) * CORE, :], xs[x][...], ((1,), (1,)))
                for h in range(5):
                    row = half * CORE + h * HD
                    value = rotated(part[h * HD : (h + 1) * HD], cosine[...], sine[...])
                    outs[job][row : row + HD, :] = value.astype(BF)
    rows = pl.ds(pl.multiple_of(table[AT_GIVEN], EXCHANGED), EXCHANGED)
    for given, group in zip(givens, groups):
        for n, job in enumerate(group):
            lanes = slice(n * SEQ, (n + 1) * SEQ)
            given[:, lanes] = outs[job][rows, :] if job >= 0 else carried[:, lanes]


def project(table, angles, xs, sets, jobs, groups, carried=None):
    if carried is None:
        carried = jnp.zeros((16, 128), BF)
    operands = [(table, None), (carried, block(carried.shape))]
    operands += [(x, block((SEQ, D), at)) for x, at in xs]
    operands += [(value, block((HALF, SEQ))) for value in angles]
    operands += [(array, ANY) for arrays in sets for array in arrays]
    return call(
        lambda *refs: project_kernel(jobs, groups, len(xs), len(sets), *refs),
        "project",
        operands,
        [((ROWS, SEQ), BF)] * len(jobs) + [((EXCHANGED, SEQ * len(group)), BF) for group in groups],
        [pltpu.VMEM((ROWS, D), BF)] * len(sets) + [pltpu.SemaphoreType.DMA((8 * len(sets),))],
        0.5 if len(sets) == 1 else 8.0,
    )


SCALE = INV_ROOT * math.log2(math.e)


def softmax_parts(scores, diagonal):
    scores = scores * SCALE
    low = scores.shape[0] - HD
    masked = jnp.where(diagonal, scores[low:], MASKED)
    if low:
        scores = jnp.concatenate([scores[:low], masked], axis=0)
    else:
        scores = masked
    power = jnp.exp2(scores - jnp.max(scores, axis=0, keepdims=True))
    return power, (1.0 / HEADS) / jnp.sum(power, axis=0, keepdims=True)


def side_by_side(heads, half):
    return jnp.concatenate([q[:, half * HD : (half + 1) * HD] for q in heads], axis=1)


def attention_gradient(student, teacher, cosine, sine):
    key_s = student[4]
    rows_s, rows_t = key_s.T, teacher[4].T
    lane = lax.broadcasted_iota(jnp.int32, (HD, 4 * HD), 1) % HD
    diagonal = lax.broadcasted_iota(jnp.int32, (HD, 4 * HD), 0) <= lane
    query_parts, key_grad = [], None
    for half in range(2):
        extent = (half + 1) * HD
        q_s = side_by_side(student[:4], half)
        q_t = side_by_side(teacher[:4], half)
        power_s, inverse_s = softmax_parts(dot(rows_s[:extent], q_s), diagonal)
        power_t, inverse_t = softmax_parts(dot(rows_t[:extent], q_t), diagonal)
        spread = (power_s * inverse_s - power_t * inverse_t).astype(BF)
        query_parts.append(dot(key_s[:, :extent], spread))
        part = dot(q_s, spread, ((1,), (1,)))
        if half == 0:
            key_grad = part
        else:
            key_grad = jnp.concatenate([part[:, :HD] + key_grad, part[:, HD:]], axis=1)
    grads = [
        jnp.concatenate([p[:, h * HD : (h + 1) * HD] for p in query_parts], axis=1)
        for h in range(4)
    ] + [key_grad]
    return [rotated(g * INV_ROOT, cosine, -sine).astype(BF) for g in grads]


def attend_kernel(count, table, *refs):
    inputs, (cosine, sine, out, other, back, both_s, both_t, grads) = refs[: 4 * count], refs[4 * count :]
    for seq in range(count):
        own_s, got_s, own_t, got_t = inputs[4 * seq : 4 * seq + 4]
        lanes = slice(seq * SEQ, (seq + 1) * SEQ)
        for both, own, got in ((both_s, own_s, got_s), (both_t, own_t, got_t)):
            both[:ROWS, lanes] = own[...]
            both[ROWS:, lanes] = got[...]
    for seq in range(count):
        lanes = slice(seq * SEQ, (seq + 1) * SEQ)
        for kv in range(2):
            blocks = [table[AT_QUERY + 4 * kv + h] for h in range(4)] + [table[AT_KEY + kv]]
            rows = [pl.ds(pl.multiple_of(n * HD, HD), HD) for n in blocks]
            student = [both_s[at, lanes] for at in rows]
            teacher = [both_t[at, lanes] for at in rows]
            made = attention_gradient(student, teacher, cosine[...], sine[...])
            for at, value in zip(rows, made):
                grads[at, lanes] = value
    for n in range(8):
        row = pl.multiple_of(table[AT_CORE + n], SHARD)
        target = out if n < 4 else other
        target[n % 4 * SHARD : (n % 4 + 1) * SHARD, :] = grads[pl.ds(row, SHARD), :]
    back[...] = grads[ROWS:, :]


def attend(table, angles, sequences):
    count = len(sequences)
    operands = [(table, None)]
    for sequence in sequences:
        for own, (got, at) in sequence:
            operands += [(own, block((ROWS, SEQ))), (got, block((EXCHANGED, SEQ), 0, at))]
    operands += [(value, block((HALF, SEQ))) for value in angles]
    return call(
        lambda *refs: attend_kernel(count, *refs),
        "attend",
        operands,
        [((rows, count * SEQ), BF) for rows in (CORE, CORE, EXCHANGED)],
        [pltpu.VMEM((ROWS + EXCHANGED, count * SEQ), BF)] * 3,
        1.0 + 3.5 * count,
    )


TILE = 512
SPAN = 2 * SEQ


def fill(table, held, grads, backs):
    for n in range(2):
        held[:, n * SPAN : (n + 1) * SPAN] = grads[n][...]
    for unit in range(8):
        row = table[AT_FILL + unit]

        @pl.when(row >= 0)
        def _():
            at = pl.ds(pl.multiple_of(row, UNIT), UNIT)
            for n in range(2):
                held[at, n * SPAN : (n + 1) * SPAN] = backs[n][unit * UNIT : (unit + 1) * UNIT, :]


def first_kernel(table, *refs):
    grads, backs, tokens, out, held = refs[:2], refs[2:4], refs[4:6], refs[6], refs[7]

    @pl.when(pl.program_id(0) == 0)
    def _():
        fill(table, held, grads, backs)

    out[...] = dot(held[:, :SPAN], tokens[0][...]) + dot(held[:, SPAN:], tokens[1][...])


def second_kernel(steps, table, *refs):
    grads, backs, tokens, before, outs, held = refs[:2], refs[2:4], refs[4:6], refs[6], refs[7:-1], refs[-1]

    @pl.when(pl.program_id(0) == 0)
    def _():
        fill(table, held, grads, backs)

    for step, out in zip(steps, outs):
        rows = pl.ds(pl.multiple_of(table[AT_STEP + step], SHARD), SHARD)
        total = before[rows, :] + dot(held[rows, :SPAN], tokens[0][...])
        total += dot(held[rows, SPAN:], tokens[1][...])
        out[...] = total.astype(BF)


def weight_call(kernel, table, grads, backs, tokens, more, outs, microseconds):
    tile = lambda t, table: (0, t)
    return pl.pallas_call(
        kernel,
        grid_spec=pltpu.PrefetchScalarGridSpec(
            num_scalar_prefetch=1,
            grid=(D // TILE,),
            in_specs=[block((CORE, SPAN))] * 2
            + [block((EXCHANGED, SPAN))] * 2
            + [pl.BlockSpec((x.shape[0], TILE), tile) for x in tokens + more],
            out_specs=[pl.BlockSpec((rows, TILE), tile) for rows, _ in outs],
            scratch_shapes=[pltpu.VMEM((CORE, 2 * SPAN), BF)],
        ),
        out_shape=[jax.ShapeDtypeStruct((rows, D), dtype) for rows, dtype in outs],
        compiler_params=params(56),
        cost_estimate=cost(microseconds),
        name="weight_gradient",
    )(table, *grads, *backs, *tokens, *more)


def adam_kernel(a, b, c, d, weight, one, two, weight_out, one_out, two_out):
    gradient = (a[...].astype(F32) + b[...].astype(F32)) + (c[...].astype(F32) + d[...].astype(F32))
    first_new = BETA_ONE * one[...] + (1.0 - BETA_ONE) * gradient
    second_new = BETA_TWO * two[...] + (1.0 - BETA_TWO) * gradient * gradient
    step_dir = (
        first_new
        / (1.0 - BETA_ONE**STEP)
        / (jnp.sqrt(second_new / (1.0 - BETA_TWO**STEP)) + EPSILON)
    )
    master = weight[...]
    weight_out[...] = master - LEARN_RATE * (step_dir + DECAY * master)
    one_out[...] = first_new
    two_out[...] = second_new


def adam(blocks, weight, one, two):
    block = pl.BlockSpec((UNIT, D), lambda k: (k, 0))
    return pl.pallas_call(
        adam_kernel,
        grid=(SHARD // UNIT,),
        in_specs=[block] * 7,
        out_specs=[block] * 3,
        out_shape=[jax.ShapeDtypeStruct((SHARD, D), F32)] * 3,
        compiler_params=params(56),
        name="adam",
    )(*blocks, weight, one, two)


def rotary_tables():
    positions = jnp.arange(SEQ).astype(F32)
    exponents = jnp.arange(HALF).astype(F32) * (2.0 / HD)
    frequency = THETA ** (-exponents)
    angles = frequency[:, None] * positions[None, :]
    return jnp.cos(angles), jnp.sin(angles)


def ring_gather(shard, up_again):
    below = send(shard, ALONG_Y[1])
    above = send(shard, ALONG_Y[3])
    far = send(below, ALONG_Y[1]) if up_again else send(above, ALONG_Y[3])
    return [shard, above, far, below]


def both_cores(pieces):
    return pieces + [send(piece, TO_CORE) for piece in pieces]


def per_device(tokens, student_weight, snapshot, moment_one, moment_two):
    own = tokens[0]
    master = student_weight[0]
    table = jnp.asarray(TABLE)[lax.axis_index("fsdp")]
    angles = rotary_tables()

    teacher = lax.ppermute(snapshot[0], "blk", [(g, (g + 1) % 8) for g in range(8)])
    plane = send(own, TO_PLANE)
    student_rows = both_cores(ring_gather(master.astype(BF), True))
    teacher_own = ring_gather(teacher, False)

    own_two, plane_two = [(own, 0), (own, 1)], [(plane, 0), (plane, 1)]
    two = [(0, 0), (1, 0)]
    *own_s, given = project(table, angles, own_two, [student_rows], two, [[0, 1]])
    teacher_own[2], given = lax.optimization_barrier((teacher_own[2], given))
    teacher_rows = both_cores(teacher_own)
    *own_t, given = project(table, angles, own_two, [teacher_rows], two, [[-1, -1, 0, 1]], given)
    got_own = send(given, TO_PLANE)
    plane_after, _ = lax.optimization_barrier((plane, own_t[0]))
    plane_two = [(plane_after, 0), (plane_after, 1)]
    *made, given_s, given_t = project(
        table,
        angles,
        plane_two,
        [student_rows, teacher_rows],
        two + [(0, 1), (1, 1)],
        [[0, 1], [2, 3]],
    )
    plane_s, plane_t = made[:2], made[2:]
    got_s, got_t = send(given_s, TO_PLANE), send(given_t, TO_PLANE)

    second = attend(
        table,
        angles,
        [[(plane_s[n], (got_own, n)), (plane_t[n], (got_own, 2 + n))] for n in range(2)],
    )
    got_s, got_t, _ = lax.optimization_barrier((got_s, got_t, second[2]))
    first = attend(
        table, angles, [[(own_s[n], (got_s, n)), (own_t[n], (got_t, n))] for n in range(2)]
    )
    back_first = send(second[2], TO_PLANE)
    back_second = send(first[2], TO_PLANE)
    core_first = [first[0], send(first[1], TO_CORE)], [back_first, send(back_first, TO_CORE)]
    core_second = [second[0], send(second[1], TO_CORE)], [back_second, send(back_second, TO_CORE)]

    planes = [plane, send(plane, TO_CORE)]
    cores = [own, send(own, TO_CORE)]
    (before,) = weight_call(first_kernel, table, *core_first, cores, [], [(CORE, F32)], 6.0)
    blocks = []
    for steps in ((2,), (1, 3, 0)):
        made = weight_call(
            lambda *refs: second_kernel(steps, *refs),
            table,
            *core_second,
            planes,
            [before],
            [(SHARD, BF)] * len(steps),
            5.0,
        )
        blocks += [send(value, ALONG_Y[s]) if s else value for value, s in zip(made, steps)]
    updated = adam(blocks, master, moment_one[0], moment_two[0])
    return tuple(value[None] for value in updated)


def solution(mesh):
    spec = P("blk", "fsdp", None)
    return jax.shard_map(
        per_device,
        mesh=mesh,
        in_specs=(spec,) * 5,
        out_specs=(spec,) * 3,
        check_vma=False,
    )
```

```python
import math

import jax
import jax.numpy as jnp
import numpy as np
from jax import lax
from jax.experimental import pallas as pl
from jax.experimental.pallas import tpu as pltpu
from jax.sharding import PartitionSpec as P

HEADS = 16
KVH = 4
HD = 128
SEQ = 256
STEP = 100
D = 2048
THETA = 500000.0
BETA_ONE = 0.9
BETA_TWO = 0.95
LEARN_RATE = 0.002
DECAY = 0.1
EPSILON = 1e-08
MASKED = -1e30

BF = jnp.bfloat16
F32 = jnp.float32
SHARD = 160
ROWS = 8 * SHARD
UNIT = 32
HALF = HD // 2
CORE = 4 * SHARD
EXCHANGED = 2 * HD
INV_ROOT = 1.0 / math.sqrt(HD)

AT_WEIGHT, AT_GIVEN, AT_QUERY, AT_KEY, AT_CORE, AT_STEP, AT_FILL, AT_BACK = 0, 8, 9, 17, 19, 27, 31, 36
GIVEN = (1024, 768)
QUERY = (tuple(range(8)), (10, 11, 0, 1, 2, 3, 4, 5))
KEY = ((10, 11), (8, 9))


def given_units(plane, core):
    rows = [GIVEN[plane] + UNIT * unit for unit in range(8)]
    return [(u, r // 320 * 160 + r % 160) for u, r in enumerate(rows) if r % 320 // 160 == core]


def build_table():
    table = np.zeros((16, 46), np.int32)
    for d in range(16):
        z, y, c = d // 8, d % 8 // 2, d % 2
        gathered = [320 * ((y + s) % 4) + 160 * (c ^ r) for r in range(2) for s in range(4)]
        cores = [320 * k + 160 * (c ^ r) for r in range(2) for k in range(4)]
        steps = [160 * ((y + s) % 4) for s in range(4)]
        fill = ([row for _, row in given_units(z, c)] + [-1] * 5)[:5]
        back = []
        for r in range(2):
            back += ([unit for unit, _ in given_units(1 - z, c ^ r)] + [0] * 5)[:5]
        table[d] = gathered + [GIVEN[z], *QUERY[z], *KEY[z]] + cores + steps + fill + back
    return table


TABLE = build_table()


def pairs_of(function):
    out = []
    for d in range(16):
        z, y, c = function(d // 8, d % 8 // 2, d % 2)
        out.append((d, z % 2 * 8 + y % 4 * 2 + c % 2))
    return out


TO_CORE = pairs_of(lambda z, y, c: (z, y, c + 1))
TO_PLANE = pairs_of(lambda z, y, c: (z + 1, y, c))
TO_BOTH = pairs_of(lambda z, y, c: (z + 1, y, c + 1))
ALONG_Y = [pairs_of(lambda z, y, c, s=s: (z, y + s, c)) for s in range(4)]


def send(value, pairs):
    return lax.ppermute(value, "fsdp", pairs)


def params(mib):
    return pltpu.CompilerParams(vmem_limit_bytes=mib * 2**20)


def cost(microseconds):
    return pl.CostEstimate(flops=int(microseconds * 1e9), bytes_accessed=2**20, transcendentals=0)


def dot(a, b, dims=((1,), (0,))):
    return lax.dot_general(a, b, (dims, ((), ())), preferred_element_type=F32)


def rotated(raw, cosine, sine):
    front, back = raw[:HALF], raw[HALF:]
    return jnp.concatenate([front * cosine - back * sine, back * cosine + front * sine], axis=0)


ANY = pl.BlockSpec(memory_space=pl.ANY)


def block(shape, row=0, column=0):
    return pl.BlockSpec(shape, lambda s, table: (row, column))


def call(kernel, name, operands, outs, scratch, microseconds):
    return pl.pallas_call(
        kernel,
        grid_spec=pltpu.PrefetchScalarGridSpec(
            num_scalar_prefetch=1,
            grid=(1,),
            in_specs=[spec for _, spec in operands[1:]],
            out_specs=[block(shape) for shape, _ in outs],
            scratch_shapes=scratch,
        ),
        out_shape=[jax.ShapeDtypeStruct(shape, dtype) for shape, dtype in outs],
        compiler_params=params(56),
        cost_estimate=cost(microseconds),
        name=name,
    )(*[value for value, _ in operands])


def project_kernel(jobs, groups, x_count, set_count, table, *refs):
    refs = list(refs)
    carried, refs = refs[0], refs[1:]
    xs, refs = refs[:x_count], refs[x_count:]
    cosine, sine, refs = refs[0], refs[1], refs[2:]
    arrays, refs = refs[: 8 * set_count], refs[8 * set_count :]
    outs, refs = refs[: len(jobs)], refs[len(jobs) :]
    givens, refs = refs[: len(groups)], refs[len(groups) :]
    held, sems = refs[:-1], refs[-1]

    def copy(at, n):
        rows = pl.ds(pl.multiple_of(table[AT_WEIGHT + n], SHARD), SHARD)
        return pltpu.make_async_copy(arrays[8 * at + n], held[at].at[rows], sems.at[8 * at + n])

    for at in range(set_count):
        for n in range(8):
            copy(at, n).start()
    for at in range(set_count):
        for n in range(8):
            copy(at, n).wait()
        for job, (x, own_set) in enumerate(jobs):
            if own_set != at:
                continue
            for half in range(2):
                part = dot(held[at][half * CORE : (half + 1) * CORE, :], xs[x][...], ((1,), (1,)))
                for h in range(5):
                    row = half * CORE + h * HD
                    value = rotated(part[h * HD : (h + 1) * HD], cosine[...], sine[...])
                    outs[job][row : row + HD, :] = value.astype(BF)
    rows = pl.ds(pl.multiple_of(table[AT_GIVEN], EXCHANGED), EXCHANGED)
    for given, group in zip(givens, groups):
        for n, job in enumerate(group):
            lanes = slice(n * SEQ, (n + 1) * SEQ)
            given[:, lanes] = outs[job][rows, :] if job >= 0 else carried[:, lanes]


def project(table, angles, xs, sets, jobs, groups, carried=None):
    if carried is None:
        carried = jnp.zeros((16, 128), BF)
    operands = [(table, None), (carried, block(carried.shape))]
    operands += [(x, block((SEQ, D), at)) for x, at in xs]
    operands += [(value, block((HALF, SEQ))) for value in angles]
    operands += [(array, ANY) for arrays in sets for array in arrays]
    return call(
        lambda *refs: project_kernel(jobs, groups, len(xs), len(sets), *refs),
        "project",
        operands,
        [((ROWS, SEQ), BF)] * len(jobs) + [((EXCHANGED, SEQ * len(group)), BF) for group in groups],
        [pltpu.VMEM((ROWS, D), BF)] * len(sets) + [pltpu.SemaphoreType.DMA((8 * len(sets),))],
        0.5 if len(sets) == 1 else 8.0,
    )


SCALE = INV_ROOT * math.log2(math.e)


def softmax_parts(scores, diagonal):
    scores = scores * SCALE
    low = scores.shape[0] - HD
    masked = jnp.where(diagonal, scores[low:], MASKED)
    if low:
        scores = jnp.concatenate([scores[:low], masked], axis=0)
    else:
        scores = masked
    power = jnp.exp2(scores - jnp.max(scores, axis=0, keepdims=True))
    return power, (1.0 / HEADS) / jnp.sum(power, axis=0, keepdims=True)


def side_by_side(heads, half):
    return jnp.concatenate([q[:, half * HD : (half + 1) * HD] for q in heads], axis=1)


def attention_gradient(student, teacher, cosine, sine):
    key_s = student[4]
    rows_s, rows_t = key_s.T, teacher[4].T
    lane = lax.broadcasted_iota(jnp.int32, (HD, 4 * HD), 1) % HD
    diagonal = lax.broadcasted_iota(jnp.int32, (HD, 4 * HD), 0) <= lane
    query_parts, key_grad = [], None
    for half in range(2):
        extent = (half + 1) * HD
        q_s = side_by_side(student[:4], half)
        q_t = side_by_side(teacher[:4], half)
        power_s, inverse_s = softmax_parts(dot(rows_s[:extent], q_s), diagonal)
        power_t, inverse_t = softmax_parts(dot(rows_t[:extent], q_t), diagonal)
        spread = (power_s * inverse_s - power_t * inverse_t).astype(BF)
        query_parts.append(dot(key_s[:, :extent], spread))
        part = dot(q_s, spread, ((1,), (1,)))
        if half == 0:
            key_grad = part
        else:
            key_grad = jnp.concatenate([part[:, :HD] + key_grad, part[:, HD:]], axis=1)
    grads = [
        jnp.concatenate([p[:, h * HD : (h + 1) * HD] for p in query_parts], axis=1)
        for h in range(4)
    ] + [key_grad]
    return [rotated(g * INV_ROOT, cosine, -sine).astype(BF) for g in grads]


def attend_kernel(count, carry_count, table, *refs):
    carried, refs = refs[:carry_count], refs[carry_count:]
    inputs, (cosine, sine, out, other, back, back_other, both_s, both_t, grads) = refs[: 4 * count], refs[4 * count :]
    for seq in range(count):
        own_s, got_s, own_t, got_t = inputs[4 * seq : 4 * seq + 4]
        lanes = slice(seq * SEQ, (seq + 1) * SEQ)
        for both, own, got in ((both_s, own_s, got_s), (both_t, own_t, got_t)):
            both[:ROWS, lanes] = own[...]
            both[ROWS:, lanes] = got[...]
    for seq in range(count):
        lanes = slice(seq * SEQ, (seq + 1) * SEQ)
        for kv in range(2):
            blocks = [table[AT_QUERY + 4 * kv + h] for h in range(4)] + [table[AT_KEY + kv]]
            rows = [pl.ds(pl.multiple_of(n * HD, HD), HD) for n in blocks]
            student = [both_s[at, lanes] for at in rows]
            teacher = [both_t[at, lanes] for at in rows]
            made = attention_gradient(student, teacher, cosine[...], sine[...])
            for at, value in zip(rows, made):
                grads[at, lanes] = value
    for n in range(8):
        row = pl.multiple_of(table[AT_CORE + n], SHARD)
        target = out if n < 4 else other
        target[n % 4 * SHARD : (n % 4 + 1) * SHARD, :] = grads[pl.ds(row, SHARD), :]
    for n in range(10):
        row = pl.multiple_of(ROWS + table[AT_BACK + n] * UNIT, UNIT)
        target = back if n < 5 else back_other
        unit = slice(n % 5 * UNIT, (n % 5 + 1) * UNIT)
        target[unit, target.shape[1] - count * SEQ :] = grads[pl.ds(row, UNIT), :]
    for value, target in zip(carried, (back, back_other)):
        target[:, : value.shape[1]] = value[...]


def attend(table, angles, sequences, carried=()):
    count = len(sequences)
    operands = [(table, None)] + [(value, block(value.shape)) for value in carried]
    wide = count * SEQ + (carried[0].shape[1] if carried else 0)
    for sequence in sequences:
        for own, (got, at) in sequence:
            operands += [(own, block((ROWS, SEQ))), (got, block((EXCHANGED, SEQ), 0, at))]
    operands += [(value, block((HALF, SEQ))) for value in angles]
    return call(
        lambda *refs: attend_kernel(count, len(carried), *refs),
        "attend",
        operands,
        [((CORE, count * SEQ), BF)] * 2 + [((SHARD, wide), BF)] * 2,
        [pltpu.VMEM((ROWS + EXCHANGED, count * SEQ), BF)] * 3,
        1.0 + 3.5 * count,
    )


TILE = 512
SPAN = 2 * SEQ
PART = SHARD // 2


def fill(table, held, grads, backs):
    first = 0
    for grad in grads:
        held[:, first : first + grad.shape[1]] = grad[...]
        first += grad.shape[1]
    for unit in range(5):
        row = table[AT_FILL + unit]

        @pl.when(row >= 0)
        def _():
            at, first = pl.ds(pl.multiple_of(row, UNIT), UNIT), 0
            for back in backs:
                lanes = slice(first, first + back.shape[1])
                held[at, lanes] = back[unit * UNIT : (unit + 1) * UNIT, :]
                first = lanes.stop


def split(refs, counts):
    out, refs = [], list(refs)
    for count in counts:
        out.append(refs[:count])
        refs = refs[count:]
    return out + [refs]


def first_kernel(counts, table, *refs):
    grads, backs, tokens, (out, held) = split(refs, counts)

    @pl.when(pl.program_id(0) == 0)
    def _():
        fill(table, held, grads, backs)

    out[...] = dot(held[:, :SPAN], tokens[0][...]) + dot(held[:, SPAN:], tokens[1][...])


def second_kernel(steps, counts, table, *refs):
    grads, backs, tokens, (before, *outs, held) = split(refs, counts)

    @pl.when(pl.program_id(0) == 0)
    def _():
        fill(table, held, grads, backs)

    for at, step in enumerate(steps):
        rows = pl.ds(pl.multiple_of(table[AT_STEP + step], SHARD), SHARD)
        total = before[rows, :] + dot(held[rows, :SPAN], tokens[0][...])
        total += dot(held[rows, SPAN:], tokens[1][...])
        total = total.astype(BF)
        outs[2 * at][...] = total[:PART]
        outs[2 * at + 1][...] = total[PART:]


def weight_call(kernel, table, grads, backs, tokens, more, outs, microseconds):
    tile = lambda t, table: (0, t)
    return pl.pallas_call(
        lambda *refs: kernel((len(grads), len(backs), len(tokens)), *refs),
        grid_spec=pltpu.PrefetchScalarGridSpec(
            num_scalar_prefetch=1,
            grid=(D // TILE,),
            in_specs=[block(value.shape) for value in grads + backs]
            + [pl.BlockSpec((x.shape[0], TILE), tile) for x in tokens + more],
            out_specs=[pl.BlockSpec((rows, TILE), tile) for rows, _ in outs],
            scratch_shapes=[pltpu.VMEM((CORE, 2 * SPAN), BF)],
        ),
        out_shape=[jax.ShapeDtypeStruct((rows, D), dtype) for rows, dtype in outs],
        compiler_params=params(56),
        cost_estimate=cost(microseconds),
        name="weight_gradient",
    )(table, *grads, *backs, *tokens, *more)


def adam_kernel(a, b, c, weight, one, two, weight_out, one_out, two_out):
    gradient = a[...].astype(F32) + (b[...].astype(F32) + c[...].astype(F32))
    first_new = BETA_ONE * one[...] + (1.0 - BETA_ONE) * gradient
    second_new = BETA_TWO * two[...] + (1.0 - BETA_TWO) * gradient * gradient
    step_dir = (
        first_new
        / (1.0 - BETA_ONE**STEP)
        / (jnp.sqrt(second_new / (1.0 - BETA_TWO**STEP)) + EPSILON)
    )
    master = weight[...]
    weight_out[...] = master - LEARN_RATE * (step_dir + DECAY * master)
    one_out[...] = first_new
    two_out[...] = second_new


def adam_body(*refs):
    pairs, rest = refs[:6], refs[6:]
    half = pl.program_id(0) // (PART // ADAM_ROWS)
    for at in range(2):

        @pl.when(half == at)
        def _():
            adam_kernel(*pairs[at::2], *rest)


ADAM_ROWS = 16


def adam(pairs, weight, one, two):
    steps = PART // ADAM_ROWS
    straight = pl.BlockSpec((ADAM_ROWS, D), lambda k: (k, 0))
    low = pl.BlockSpec((ADAM_ROWS, D), lambda k: (jnp.minimum(k, steps - 1), 0))
    high = pl.BlockSpec((ADAM_ROWS, D), lambda k: (jnp.maximum(k - steps, 0), 0))
    return pl.pallas_call(
        adam_body,
        grid=(2 * steps,),
        in_specs=[low, high] * 3 + [straight] * 3,
        out_specs=[straight] * 3,
        out_shape=[jax.ShapeDtypeStruct((SHARD, D), F32)] * 3,
        compiler_params=params(56),
        name="adam",
    )(*[value for pair in pairs for value in pair], weight, one, two)


def rotary_tables():
    positions = jnp.arange(SEQ).astype(F32)
    exponents = jnp.arange(HALF).astype(F32) * (2.0 / HD)
    frequency = THETA ** (-exponents)
    angles = frequency[:, None] * positions[None, :]
    return jnp.cos(angles), jnp.sin(angles)


def ring_gather(shard, up_again):
    below = send(shard, ALONG_Y[1])
    above = send(shard, ALONG_Y[3])
    far = send(below, ALONG_Y[1]) if up_again else send(above, ALONG_Y[3])
    return [shard, above, far, below]


def both_cores(pieces):
    return pieces + [send(piece, TO_CORE) for piece in pieces]


def per_device(tokens, student_weight, snapshot, moment_one, moment_two):
    own = tokens[0]
    master = student_weight[0]
    table = jnp.asarray(TABLE)[lax.axis_index("fsdp")]
    angles = rotary_tables()

    teacher = lax.ppermute(snapshot[0], "blk", [(g, (g + 1) % 8) for g in range(8)])
    plane = send(own, TO_PLANE)
    student_rows = both_cores(ring_gather(master.astype(BF), True))
    teacher_own = ring_gather(teacher, False)

    own_two, plane_two = [(own, 0), (own, 1)], [(plane, 0), (plane, 1)]
    two = [(0, 0), (1, 0)]
    *own_s, given = project(table, angles, own_two, [student_rows], two, [[0, 1]])
    teacher_own[2], teacher_own[3], given = lax.optimization_barrier(
        (teacher_own[2], teacher_own[3], given)
    )
    teacher_rows = both_cores(teacher_own)
    *own_t, given = project(table, angles, own_two, [teacher_rows], two, [[-1, -1, 0, 1]], given)
    got_own = send(given, TO_PLANE)
    plane_after, _ = lax.optimization_barrier((plane, own_t[0]))
    plane_two = [(plane_after, 0), (plane_after, 1)]
    *made, given_s, given_t = project(
        table,
        angles,
        plane_two,
        [student_rows, teacher_rows],
        two + [(0, 1), (1, 1)],
        [[0, 1], [2, 3]],
    )
    plane_s, plane_t = made[:2], made[2:]
    got_s, got_t = send(given_s, TO_PLANE), send(given_t, TO_PLANE)

    second = attend(
        table,
        angles,
        [[(plane_s[n], (got_own, n)), (plane_t[n], (got_own, 2 + n))] for n in range(2)],
    )
    got_s, got_t, _ = lax.optimization_barrier((got_s, got_t, second[2]))
    first = [attend(table, angles, [[(own_s[0], (got_s, 0)), (own_t[0], (got_t, 0))]])]
    back_first = [send(second[2], TO_PLANE), send(second[3], TO_PLANE)]
    got_s, got_t, *back_first, carried = lax.optimization_barrier(
        (got_s, got_t, *back_first, first[0][2])
    )
    back_first[1] = send(back_first[1], TO_CORE)
    first.append(
        attend(
            table,
            angles,
            [[(own_s[1], (got_s, 1)), (own_t[1], (got_t, 1))]],
            (carried, first[0][3]),
        )
    )
    back_second = [send(first[1][2], TO_PLANE), send(first[1][3], TO_BOTH)]
    (before,) = weight_call(
        first_kernel,
        table,
        [part[0] for part in first] + [send(part[1], TO_CORE) for part in first],
        back_first,
        [own, send(own, TO_CORE)],
        [],
        [(CORE, F32)],
        6.0,
    )

    def weight_blocks(steps):
        return weight_call(
            lambda *refs: second_kernel(steps, *refs),
            table,
            [second[0], send(second[1], TO_CORE)],
            back_second,
            [plane_after, send(plane_after, TO_CORE)],
            [before],
            [(PART, BF)] * (2 * len(steps)),
            5.0,
        )

    up, down = ALONG_Y[1], ALONG_Y[3]
    far_low, far_high = weight_blocks((2,))
    far_low, far_high = send(far_low, up), send(far_high, down)
    next_low, next_high, last_low, last_high, own_low, own_high = weight_blocks((1, 3, 0))
    from_below = [None, send(next_high, up)]
    from_above = [send(last_low, down), None]
    from_below[0] = send((next_low.astype(F32) + far_low.astype(F32)).astype(BF), up)
    from_above[1] = send((last_high.astype(F32) + far_high.astype(F32)).astype(BF), down)
    pairs = [(own_low, own_high), from_below, from_above]
    updated = adam(pairs, master, moment_one[0], moment_two[0])
    return tuple(value[None] for value in updated)


def solution(mesh):
    spec = P("blk", "fsdp", None)
    return jax.shard_map(
        per_device,
        mesh=mesh,
        in_specs=(spec,) * 5,
        out_specs=(spec,) * 3,
        check_vma=False,
    )
```

```python
import math

import jax
import jax.numpy as jnp
import numpy as np
from jax import lax
from jax.experimental import pallas as pl
from jax.experimental.pallas import tpu as pltpu
from jax.sharding import PartitionSpec as P

HEADS = 16
KVH = 4
HD = 128
SEQ = 256
STEP = 100
D = 2048
THETA = 500000.0
BETA_ONE = 0.9
BETA_TWO = 0.95
LEARN_RATE = 0.002
DECAY = 0.1
EPSILON = 1e-08
MASKED = -1e30

BF = jnp.bfloat16
F32 = jnp.float32
SHARD = 160
ROWS = 8 * SHARD
UNIT = 32
PART = SHARD // 2
GATHERED = ((0, 0, SHARD), (1, 0, SHARD), (2, 0, PART), (2, PART, PART), (3, 0, SHARD))
HALF = HD // 2
CORE = 4 * SHARD
EXCHANGED = 2 * HD
INV_ROOT = 1.0 / math.sqrt(HD)

AT_WEIGHT, AT_GIVEN, AT_QUERY, AT_KEY, AT_CORE, AT_STEP, AT_FILL, AT_BACK = 0, 8, 9, 17, 19, 27, 31, 36
GIVEN = (1024, 768)
QUERY = (tuple(range(8)), (10, 11, 0, 1, 2, 3, 4, 5))
KEY = ((10, 11), (8, 9))


def given_units(plane, core):
    rows = [GIVEN[plane] + UNIT * unit for unit in range(8)]
    return [(u, r // 320 * 160 + r % 160) for u, r in enumerate(rows) if r % 320 // 160 == core]


def build_table():
    table = np.zeros((16, 46), np.int32)
    for d in range(16):
        z, y, c = d // 8, d % 8 // 2, d % 2
        gathered = [320 * ((y + s) % 4) + 160 * (c ^ r) for r in range(2) for s in range(4)]
        cores = [320 * k + 160 * (c ^ r) for r in range(2) for k in range(4)]
        steps = [160 * ((y + s) % 4) for s in range(4)]
        fill = ([row for _, row in given_units(z, c)] + [-1] * 5)[:5]
        back = []
        for r in range(2):
            back += ([unit for unit, _ in given_units(1 - z, c ^ r)] + [0] * 5)[:5]
        table[d] = gathered + [GIVEN[z], *QUERY[z], *KEY[z]] + cores + steps + fill + back
    return table


TABLE = build_table()


def pairs_of(function):
    out = []
    for d in range(16):
        z, y, c = function(d // 8, d % 8 // 2, d % 2)
        out.append((d, z % 2 * 8 + y % 4 * 2 + c % 2))
    return out


TO_CORE = pairs_of(lambda z, y, c: (z, y, c + 1))
TO_PLANE = pairs_of(lambda z, y, c: (z + 1, y, c))
TO_BOTH = pairs_of(lambda z, y, c: (z + 1, y, c + 1))
ALONG_Y = [pairs_of(lambda z, y, c, s=s: (z, y + s, c)) for s in range(4)]


def send(value, pairs):
    return lax.ppermute(value, "fsdp", pairs)


def params(mib):
    return pltpu.CompilerParams(vmem_limit_bytes=mib * 2**20)


def cost(microseconds):
    return pl.CostEstimate(flops=int(microseconds * 1e9), bytes_accessed=2**20, transcendentals=0)


def dot(a, b, dims=((1,), (0,))):
    return lax.dot_general(a, b, (dims, ((), ())), preferred_element_type=F32)


def rotated(raw, cosine, sine):
    front, back = raw[:HALF], raw[HALF:]
    return jnp.concatenate([front * cosine - back * sine, back * cosine + front * sine], axis=0)


def split(refs, counts):
    out, refs = [], list(refs)
    for count in counts:
        out.append(refs[:count])
        refs = refs[count:]
    return out + [refs]


ANY = pl.BlockSpec(memory_space=pl.ANY)


def block(shape, row=0, column=0):
    return pl.BlockSpec(shape, lambda s, table: (row, column))


def call(kernel, name, operands, outs, scratch, microseconds):
    return pl.pallas_call(
        kernel,
        grid_spec=pltpu.PrefetchScalarGridSpec(
            num_scalar_prefetch=1,
            grid=(1,),
            in_specs=[spec for _, spec in operands[1:]],
            out_specs=[spec[0] if spec else block(shape) for shape, _, *spec in outs],
            scratch_shapes=scratch,
        ),
        out_shape=[jax.ShapeDtypeStruct(shape, dtype) for shape, dtype, *_ in outs],
        compiler_params=params(56),
        cost_estimate=cost(microseconds),
        name=name,
    )(*[value for value, _ in operands])


def project_kernel(jobs, groups, x_places, set_count, table, *refs):
    pieces = 2 * len(GATHERED)
    (carried, cosine, sine), xs, arrays, outs, givens, (tokens, made, sems, *held) = split(
        refs, (3, len(x_places), pieces * set_count, len(jobs), len(groups))
    )
    x_count = len(x_places)

    def token_copy(n):
        rows = pl.ds(x_places[n] * SEQ, SEQ)
        return pltpu.make_async_copy(xs[n].at[rows], tokens.at[n], sems.at[n])

    def weight_copy(at, n):
        step, first, rows = GATHERED[n % len(GATHERED)]
        row = table[AT_WEIGHT + n // len(GATHERED) * 4 + step] + first
        place = held[at].at[pl.ds(pl.multiple_of(row, 16), rows)]
        n += at * pieces
        return pltpu.make_async_copy(arrays[n], place, sems.at[x_count + n])

    def result_copy(job):
        sem = sems.at[x_count + pieces * set_count + job]
        return pltpu.make_async_copy(made.at[job], outs[job], sem)

    for n in range(x_count):
        token_copy(n).start()
    for at in range(set_count):
        for n in range(pieces):
            weight_copy(at, n).start()
    for n in range(x_count):
        token_copy(n).wait()
    for at in range(set_count):
        for n in range(pieces):
            weight_copy(at, n).wait()
        for job, (x, own_set) in enumerate(jobs):
            if own_set != at:
                continue
            for half in range(2):
                part = dot(held[at][half * CORE : (half + 1) * CORE, :], tokens[x], ((1,), (1,)))
                for h in range(5):
                    row = half * CORE + h * HD
                    value = rotated(part[h * HD : (h + 1) * HD], cosine[...], sine[...])
                    made[job, row : row + HD, :] = value.astype(BF)
            result_copy(job).start()
    rows = pl.ds(pl.multiple_of(table[AT_GIVEN], EXCHANGED), EXCHANGED)
    for given, group in zip(givens, groups):
        for n, job in enumerate(group):
            lanes = slice(n * SEQ, (n + 1) * SEQ)
            given[:, lanes] = made[job, rows, :] if job >= 0 else carried[:, lanes]
    for job in range(len(jobs)):
        result_copy(job).wait()


def project(table, angles, xs, sets, jobs, groups, carried=None):
    if carried is None:
        carried = jnp.zeros((16, 128), BF)
    pieces = 2 * len(GATHERED)
    operands = [(table, None), (carried, block(carried.shape))]
    operands += [(value, block((HALF, SEQ))) for value in angles]
    operands += [(x, ANY) for x, _ in xs]
    operands += [(array, ANY) for arrays in sets for array in arrays]
    places = tuple(at for _, at in xs)
    count = len(xs) + pieces * len(sets) + len(jobs)
    return call(
        lambda *refs: project_kernel(jobs, groups, places, len(sets), *refs),
        "project",
        operands,
        [((ROWS, SEQ), BF, ANY)] * len(jobs)
        + [((EXCHANGED, SEQ * len(group)), BF) for group in groups],
        [
            pltpu.VMEM((len(xs), SEQ, D), BF),
            pltpu.VMEM((len(jobs), ROWS, SEQ), BF),
            pltpu.SemaphoreType.DMA((count,)),
        ]
        + [pltpu.VMEM((ROWS, D), BF)] * len(sets),
        0.5 if len(sets) == 1 else 8.0,
    )


SCALE = INV_ROOT * math.log2(math.e)
SPAN = 2 * SEQ


def softmax_parts(scores, diagonal):
    scores = scores * SCALE
    low = scores.shape[0] - HD
    masked = jnp.where(diagonal, scores[low:], MASKED)
    if low:
        scores = jnp.concatenate([scores[:low], masked], axis=0)
    else:
        scores = masked
    power = jnp.exp2(scores - jnp.max(scores, axis=0, keepdims=True))
    return power, (1.0 / HEADS) / jnp.sum(power, axis=0, keepdims=True)


def side_by_side(heads, half):
    return jnp.concatenate([q[:, half * HD : (half + 1) * HD] for q in heads], axis=1)


def attention_gradient(student, teacher, cosine, sine):
    key_s = student[4]
    rows_s, rows_t = key_s.T, teacher[4].T
    lane = lax.broadcasted_iota(jnp.int32, (HD, 4 * HD), 1) % HD
    diagonal = lax.broadcasted_iota(jnp.int32, (HD, 4 * HD), 0) <= lane
    query_parts, key_grad = [], None
    for half in range(2):
        extent = (half + 1) * HD
        q_s = side_by_side(student[:4], half)
        q_t = side_by_side(teacher[:4], half)
        power_s, inverse_s = softmax_parts(dot(rows_s[:extent], q_s), diagonal)
        power_t, inverse_t = softmax_parts(dot(rows_t[:extent], q_t), diagonal)
        spread = (power_s * inverse_s - power_t * inverse_t).astype(BF)
        query_parts.append(dot(key_s[:, :extent], spread))
        part = dot(q_s, spread, ((1,), (1,)))
        if half == 0:
            key_grad = part
        else:
            key_grad = jnp.concatenate([part[:, :HD] + key_grad, part[:, HD:]], axis=1)
    grads = [
        jnp.concatenate([p[:, h * HD : (h + 1) * HD] for p in query_parts], axis=1)
        for h in range(4)
    ] + [key_grad]
    return [rotated(g * INV_ROOT, cosine, -sine).astype(BF) for g in grads]


def attend_kernel(count, carry_count, table, *refs):
    carried, refs = refs[:carry_count], refs[carry_count:]
    inputs, (cosine, sine, out, other, back, back_other, both_s, both_t, grads) = refs[: 4 * count], refs[4 * count :]
    for seq in range(count):
        own_s, got_s, own_t, got_t = inputs[4 * seq : 4 * seq + 4]
        lanes = slice(seq * SEQ, (seq + 1) * SEQ)
        for both, own, got in ((both_s, own_s, got_s), (both_t, own_t, got_t)):
            both[:ROWS, lanes] = own[...]
            both[ROWS:, lanes] = got[...]
    for seq in range(count):
        lanes = slice(seq * SEQ, (seq + 1) * SEQ)
        for kv in range(2):
            blocks = [table[AT_QUERY + 4 * kv + h] for h in range(4)] + [table[AT_KEY + kv]]
            rows = [pl.ds(pl.multiple_of(n * HD, HD), HD) for n in blocks]
            student = [both_s[at, lanes] for at in rows]
            teacher = [both_t[at, lanes] for at in rows]
            made = attention_gradient(student, teacher, cosine[...], sine[...])
            for at, value in zip(rows, made):
                grads[at, lanes] = value
    for n in range(8):
        row = pl.multiple_of(table[AT_CORE + n], SHARD)
        target = out if n < 4 else other
        target[n % 4 * SHARD : (n % 4 + 1) * SHARD, :] = grads[pl.ds(row, SHARD), :]
    for n in range(10):
        row = pl.multiple_of(ROWS + table[AT_BACK + n] * UNIT, UNIT)
        target = back if n < 5 else back_other
        unit = slice(n % 5 * UNIT, (n % 5 + 1) * UNIT)
        target[unit, target.shape[1] - count * SEQ :] = grads[pl.ds(row, UNIT), :]
    for value, target in zip(carried, (back, back_other)):
        target[:, : value.shape[1]] = value[...]


def attend(table, angles, sequences, carried=()):
    count = len(sequences)
    operands = [(table, None)] + [(value, block(value.shape)) for value in carried]
    wide = count * SEQ + (carried[0].shape[1] if carried else 0)
    for sequence in sequences:
        for own, (got, at) in sequence:
            operands += [(own, block((ROWS, SEQ))), (got, block((EXCHANGED, SEQ), 0, at))]
    operands += [(value, block((HALF, SEQ))) for value in angles]
    return call(
        lambda *refs: attend_kernel(count, len(carried), *refs),
        "attend",
        operands,
        [((CORE, count * SEQ), BF)] * 2 + [((SHARD, wide), BF)] * 2,
        [pltpu.VMEM((ROWS + EXCHANGED, count * SEQ), BF)] * 3,
        1.0 + 3.5 * count,
    )


TILE = 512


def fill(table, held, grads, backs):
    first = 0
    for grad in grads:
        held[:, first : first + grad.shape[1]] = grad[...]
        first += grad.shape[1]
    for unit in range(5):
        row = table[AT_FILL + unit]

        @pl.when(row >= 0)
        def _():
            at, first = pl.ds(pl.multiple_of(row, UNIT), UNIT), 0
            for back in backs:
                lanes = slice(first, first + back.shape[1])
                held[at, lanes] = back[unit * UNIT : (unit + 1) * UNIT, :]
                first = lanes.stop


def first_kernel(counts, table, *refs):
    grads, backs, tokens, (out, held) = split(refs, counts)

    @pl.when(pl.program_id(0) == 0)
    def _():
        fill(table, held, grads, backs)

    out[...] = dot(held[:, :SPAN], tokens[0][...]) + dot(held[:, SPAN:], tokens[1][...])


def second_kernel(parts, counts, table, *refs):
    grads, backs, tokens, befores, rest = split(refs, (*counts, len(parts)))
    outs, held = rest[:-1], rest[-1]

    @pl.when(pl.program_id(0) == 0)
    def _():
        fill(table, held, grads, backs)

    for (step, first, _), before, out in zip(parts, befores, outs):
        rows = pl.ds(pl.multiple_of(table[AT_STEP + step] + first, 16), PART)
        total = before[...] + dot(held[rows, :SPAN], tokens[0][...])
        total += dot(held[rows, SPAN:], tokens[1][...])
        out[...] = total.astype(out.dtype)


def weight_call(kernel, table, grads, backs, tokens, more, outs, microseconds):
    tile = lambda t, table: (0, t)
    return pl.pallas_call(
        lambda *refs: kernel((len(grads), len(backs), len(tokens)), *refs),
        grid_spec=pltpu.PrefetchScalarGridSpec(
            num_scalar_prefetch=1,
            grid=(D // TILE,),
            in_specs=[block(value.shape) for value in grads + backs]
            + [pl.BlockSpec((x.shape[0], TILE), tile) for x in tokens]
            + [pl.BlockSpec((PART, TILE), index) for _, index in more],
            out_specs=[pl.BlockSpec((rows, TILE), tile) for rows, _ in outs],
            scratch_shapes=[pltpu.VMEM((CORE, 2 * SPAN), BF)],
        ),
        out_shape=[jax.ShapeDtypeStruct((rows, D), dtype) for rows, dtype in outs],
        compiler_params=params(56),
        cost_estimate=cost(microseconds),
        name="weight_gradient",
    )(table, *grads, *backs, *tokens, *[value for value, _ in more])


def part_index(step, first):
    return lambda t, table: (table[AT_STEP + step] // PART + first // PART, t)


def adam_kernel(a, b, c, weight, one, two, weight_out, one_out, two_out):
    gradient = a[...].astype(F32) + (b[...].astype(F32) + c[...].astype(F32))
    first_new = BETA_ONE * one[...] + (1.0 - BETA_ONE) * gradient
    second_new = BETA_TWO * two[...] + (1.0 - BETA_TWO) * gradient * gradient
    step_dir = (
        first_new
        / (1.0 - BETA_ONE**STEP)
        / (jnp.sqrt(second_new / (1.0 - BETA_TWO**STEP)) + EPSILON)
    )
    master = weight[...]
    weight_out[...] = master - LEARN_RATE * (step_dir + DECAY * master)
    one_out[...] = first_new
    two_out[...] = second_new


def adam_body(*refs):
    pairs, rest = refs[:6], refs[6:]
    for at in range(2):

        @pl.when(pl.program_id(0) == at)
        def _():
            adam_kernel(*pairs[at::2], *rest)


ADAM_TILE = 1024


def adam(pairs, weight, one, two):
    straight = pl.BlockSpec((PART, ADAM_TILE), lambda k, t: (k, t))
    last = D // ADAM_TILE - 1
    low = pl.BlockSpec((PART, ADAM_TILE), lambda k, t: (0, jnp.where(k == 0, t, last)))
    high = pl.BlockSpec((PART, ADAM_TILE), lambda k, t: (0, jnp.where(k == 0, 0, t)))
    return pl.pallas_call(
        adam_body,
        grid=(2, D // ADAM_TILE),
        in_specs=[low, high] * 3 + [straight] * 3,
        out_specs=[straight] * 3,
        out_shape=[jax.ShapeDtypeStruct((SHARD, D), F32)] * 3,
        compiler_params=params(56),
        name="adam",
    )(*[value for pair in pairs for value in pair], weight, one, two)


def rotary_tables():
    positions = jnp.arange(SEQ).astype(F32)
    exponents = jnp.arange(HALF).astype(F32) * (2.0 / HD)
    frequency = THETA ** (-exponents)
    angles = frequency[:, None] * positions[None, :]
    return jnp.cos(angles), jnp.sin(angles)


def ring_gather(shard):
    up, down = ALONG_Y[1], ALONG_Y[3]
    below, above = send(shard, up), send(shard, down)
    return [shard, above, send(below[:PART], up), send(above[PART:], down), below]


def both_cores(pieces):
    return pieces + [send(piece, TO_CORE) for piece in pieces]


def per_device(tokens, student_weight, snapshot, moment_one, moment_two):
    own = tokens[0]
    master = student_weight[0]
    table = jnp.asarray(TABLE)[lax.axis_index("fsdp")]
    angles = rotary_tables()

    teacher = lax.ppermute(snapshot[0], "blk", [(g, (g + 1) % 8) for g in range(8)])
    plane = send(own, TO_PLANE)
    student_rows = both_cores(ring_gather(master.astype(BF)))
    teacher_own = ring_gather(teacher)

    own_two, plane_two = [(own, 0), (own, 1)], [(plane, 0), (plane, 1)]
    two = [(0, 0), (1, 0)]
    *own_s, given = project(table, angles, own_two, [student_rows], two, [[0, 1]])
    *teacher_own[2:], given = lax.optimization_barrier((*teacher_own[2:], given))
    teacher_rows = both_cores(teacher_own)
    *own_t, given = project(table, angles, own_two, [teacher_rows], two, [[-1, -1, 0, 1]], given)
    got_own = send(given, TO_PLANE)
    plane_after, _ = lax.optimization_barrier((plane, own_t[0]))
    plane_two = [(plane_after, 0), (plane_after, 1)]
    *made, given_s, given_t = project(
        table,
        angles,
        plane_two,
        [student_rows, teacher_rows],
        two + [(0, 1), (1, 1)],
        [[0, 1], [2, 3]],
    )
    plane_s, plane_t = made[:2], made[2:]
    got_s, got_t = send(given_s, TO_PLANE), send(given_t, TO_PLANE)

    second = attend(
        table,
        angles,
        [[(plane_s[n], (got_own, n)), (plane_t[n], (got_own, 2 + n))] for n in range(2)],
    )
    got_s, got_t, _ = lax.optimization_barrier((got_s, got_t, second[2]))
    first = [attend(table, angles, [[(own_s[0], (got_s, 0)), (own_t[0], (got_t, 0))]])]
    back_first = [send(second[2], TO_PLANE), send(second[3], TO_PLANE)]
    got_s, got_t, *back_first, carried = lax.optimization_barrier(
        (got_s, got_t, *back_first, first[0][2])
    )
    back_first[1] = send(back_first[1], TO_CORE)
    first.append(
        attend(
            table,
            angles,
            [[(own_s[1], (got_s, 1)), (own_t[1], (got_t, 1))]],
            (carried, first[0][3]),
        )
    )
    back_second = [send(first[1][2], TO_PLANE), send(first[1][3], TO_BOTH)]
    (before,) = weight_call(
        first_kernel,
        table,
        [part[0] for part in first] + [send(part[1], TO_CORE) for part in first],
        back_first,
        [own, send(own, TO_CORE)],
        [],
        [(CORE, F32)],
        6.0,
    )

    def weight_blocks(parts):
        return weight_call(
            lambda *refs: second_kernel(parts, *refs),
            table,
            [second[0], send(second[1], TO_CORE)],
            back_second,
            [plane_after, send(plane_after, TO_CORE)],
            [(before, part_index(step, first)) for step, first, _ in parts],
            [(PART, dtype) for _, _, dtype in parts],
            5.0,
        )

    up, down = ALONG_Y[1], ALONG_Y[3]
    far_low, far_high, next_high, last_low = weight_blocks(
        ((2, 0, BF), (2, PART, BF), (1, PART, BF), (3, 0, BF))
    )
    far_low, far_high = send(far_low, up), send(far_high, down)
    from_below, from_above = [None, send(next_high, up)], [send(last_low, down), None]
    next_low, last_high, *own_parts = weight_blocks(
        ((1, 0, F32), (3, PART, F32), (0, 0, F32), (0, PART, F32))
    )
    from_below[0] = send((next_low + far_low.astype(F32)).astype(BF), up)
    from_above[1] = send((last_high + far_high.astype(F32)).astype(BF), down)
    pairs = [own_parts, from_below, from_above]
    updated = adam(pairs, master, moment_one[0], moment_two[0])
    return tuple(value[None] for value in updated)


def solution(mesh):
    spec = P("blk", "fsdp", None)
    return jax.shard_map(
        per_device,
        mesh=mesh,
        in_specs=(spec,) * 5,
        out_specs=(spec,) * 3,
        check_vma=False,
    )
```

```python
import math

import jax
import jax.numpy as jnp
import numpy as np
from jax import lax
from jax.experimental import pallas as pl
from jax.experimental.pallas import tpu as pltpu
from jax.sharding import PartitionSpec as P

HEADS = 16
KVH = 4
HD = 128
SEQ = 256
STEP = 100
D = 2048
THETA = 500000.0
BETA_ONE = 0.9
BETA_TWO = 0.95
LEARN_RATE = 0.002
DECAY = 0.1
EPSILON = 1e-08
MASKED = -1e30

BF = jnp.bfloat16
F32 = jnp.float32
SHARD = 160
ROWS = 8 * SHARD
UNIT = 32
PART = SHARD // 2
HALF = HD // 2
CORE = 4 * SHARD
EXCHANGED = 2 * HD
INV_ROOT = 1.0 / math.sqrt(HD)

AT_WEIGHT, AT_GIVEN, AT_QUERY, AT_KEY, AT_CORE, AT_STEP, AT_FILL, AT_BACK = 0, 8, 9, 17, 19, 27, 31, 36
GIVEN = (1024, 768)
QUERY = (tuple(range(8)), (10, 11, 0, 1, 2, 3, 4, 5))
KEY = ((10, 11), (8, 9))


def given_units(plane, core):
    rows = [GIVEN[plane] + UNIT * unit for unit in range(8)]
    return [(u, r // 320 * 160 + r % 160) for u, r in enumerate(rows) if r % 320 // 160 == core]


def build_table():
    table = np.zeros((16, 46), np.int32)
    for d in range(16):
        z, y, c = d // 8, d % 8 // 2, d % 2
        gathered = [320 * ((y + s) % 4) + 160 * (c ^ r) for r in range(2) for s in range(4)]
        cores = [320 * k + 160 * (c ^ r) for r in range(2) for k in range(4)]
        steps = [160 * ((y + s) % 4) for s in range(4)]
        fill = ([row for _, row in given_units(z, c)] + [-1] * 5)[:5]
        back = []
        for r in range(2):
            back += ([unit for unit, _ in given_units(1 - z, c ^ r)] + [0] * 5)[:5]
        table[d] = gathered + [GIVEN[z], *QUERY[z], *KEY[z]] + cores + steps + fill + back
    return table


TABLE = build_table()


def pairs_of(function):
    out = []
    for d in range(16):
        z, y, c = function(d // 8, d % 8 // 2, d % 2)
        out.append((d, z % 2 * 8 + y % 4 * 2 + c % 2))
    return out


TO_CORE = pairs_of(lambda z, y, c: (z, y, c + 1))
TO_PLANE = pairs_of(lambda z, y, c: (z + 1, y, c))
TO_BOTH = pairs_of(lambda z, y, c: (z + 1, y, c + 1))
ALONG_Y = [pairs_of(lambda z, y, c, s=s: (z, y + s, c)) for s in range(4)]


def send(value, pairs):
    return lax.ppermute(value, "fsdp", pairs)


def params(mib):
    return pltpu.CompilerParams(vmem_limit_bytes=mib * 2**20)


def cost(microseconds):
    return pl.CostEstimate(flops=int(microseconds * 1e9), bytes_accessed=2**20, transcendentals=0)


def dot(a, b, dims=((1,), (0,))):
    return lax.dot_general(a, b, (dims, ((), ())), preferred_element_type=F32)


def rotated(raw, cosine, sine):
    front, back = raw[:HALF], raw[HALF:]
    return jnp.concatenate([front * cosine - back * sine, back * cosine + front * sine], axis=0)


def split(refs, counts):
    out, refs = [], list(refs)
    for count in counts:
        out.append(refs[:count])
        refs = refs[count:]
    return out + [refs]


ANY = pl.BlockSpec(memory_space=pl.ANY)


def block(shape, row=0, column=0):
    return pl.BlockSpec(shape, lambda s, table: (row, column))


def call(kernel, name, operands, outs, scratch, microseconds):
    return pl.pallas_call(
        kernel,
        grid_spec=pltpu.PrefetchScalarGridSpec(
            num_scalar_prefetch=1,
            grid=(1,),
            in_specs=[spec for _, spec in operands[1:]],
            out_specs=[spec[0] if spec else block(shape) for shape, _, *spec in outs],
            scratch_shapes=scratch,
        ),
        out_shape=[jax.ShapeDtypeStruct(shape, dtype) for shape, dtype, *_ in outs],
        compiler_params=params(56),
        cost_estimate=cost(microseconds),
        name=name,
    )(*[value for value, _ in operands])


def project_kernel(jobs, groups, x_count, set_count, table, *refs):
    refs = list(refs)
    carried, refs = refs[0], refs[1:]
    xs, refs = refs[:x_count], refs[x_count:]
    cosine, sine, refs = refs[0], refs[1], refs[2:]
    arrays, refs = refs[: 8 * set_count], refs[8 * set_count :]
    outs, refs = refs[: len(jobs)], refs[len(jobs) :]
    givens, refs = refs[: len(groups)], refs[len(groups) :]
    held, sems = refs[:-1], refs[-1]

    def copy(at, n):
        rows = pl.ds(pl.multiple_of(table[AT_WEIGHT + n], SHARD), SHARD)
        return pltpu.make_async_copy(arrays[8 * at + n], held[at].at[rows], sems.at[8 * at + n])

    for at in range(set_count):
        for n in range(8):
            copy(at, n).start()
    for at in range(set_count):
        for n in range(8):
            copy(at, n).wait()
        for job, (x, own_set) in enumerate(jobs):
            if own_set != at:
                continue
            for half in range(2):
                part = dot(held[at][half * CORE : (half + 1) * CORE, :], xs[x][...], ((1,), (1,)))
                for h in range(5):
                    row = half * CORE + h * HD
                    value = rotated(part[h * HD : (h + 1) * HD], cosine[...], sine[...])
                    outs[job][row : row + HD, :] = value.astype(BF)
    rows = pl.ds(pl.multiple_of(table[AT_GIVEN], EXCHANGED), EXCHANGED)
    for given, group in zip(givens, groups):
        for n, job in enumerate(group):
            lanes = slice(n * SEQ, (n + 1) * SEQ)
            given[:, lanes] = outs[job][rows, :] if job >= 0 else carried[:, lanes]


def project(table, angles, xs, sets, jobs, groups, carried=None):
    if carried is None:
        carried = jnp.zeros((16, 128), BF)
    operands = [(table, None), (carried, block(carried.shape))]
    operands += [(x, block((SEQ, D), at)) for x, at in xs]
    operands += [(value, block((HALF, SEQ))) for value in angles]
    operands += [(array, ANY) for arrays in sets for array in arrays]
    return call(
        lambda *refs: project_kernel(jobs, groups, len(xs), len(sets), *refs),
        "project",
        operands,
        [((ROWS, SEQ), BF)] * len(jobs) + [((EXCHANGED, SEQ * len(group)), BF) for group in groups],
        [pltpu.VMEM((ROWS, D), BF)] * len(sets) + [pltpu.SemaphoreType.DMA((8 * len(sets),))],
        0.5 if len(sets) == 1 else 8.0,
    )


SCALE = INV_ROOT * math.log2(math.e)
SPAN = 2 * SEQ


def softmax_parts(scores, diagonal):
    scores = scores * SCALE
    low = scores.shape[0] - HD
    masked = jnp.where(diagonal, scores[low:], MASKED)
    if low:
        scores = jnp.concatenate([scores[:low], masked], axis=0)
    else:
        scores = masked
    power = jnp.exp2(scores - jnp.max(scores, axis=0, keepdims=True))
    return power, (1.0 / HEADS) / jnp.sum(power, axis=0, keepdims=True)


def side_by_side(heads, half):
    return jnp.concatenate([q[:, half * HD : (half + 1) * HD] for q in heads], axis=1)


def attention_gradient(student, teacher, cosine, sine):
    key_s = student[4]
    rows_s, rows_t = key_s.T, teacher[4].T
    lane = lax.broadcasted_iota(jnp.int32, (HD, 4 * HD), 1) % HD
    diagonal = lax.broadcasted_iota(jnp.int32, (HD, 4 * HD), 0) <= lane
    query_parts, key_grad = [], None
    for half in range(2):
        extent = (half + 1) * HD
        q_s = side_by_side(student[:4], half)
        q_t = side_by_side(teacher[:4], half)
        power_s, inverse_s = softmax_parts(dot(rows_s[:extent], q_s), diagonal)
        power_t, inverse_t = softmax_parts(dot(rows_t[:extent], q_t), diagonal)
        spread = (power_s * inverse_s - power_t * inverse_t).astype(BF)
        query_parts.append(dot(key_s[:, :extent], spread))
        part = dot(q_s, spread, ((1,), (1,)))
        if half == 0:
            key_grad = part
        else:
            key_grad = jnp.concatenate([part[:, :HD] + key_grad, part[:, HD:]], axis=1)
    grads = [
        jnp.concatenate([p[:, h * HD : (h + 1) * HD] for p in query_parts], axis=1)
        for h in range(4)
    ] + [key_grad]
    return [rotated(g * INV_ROOT, cosine, -sine).astype(BF) for g in grads]


def attend_kernel(count, carry_count, table, *refs):
    carried, refs = refs[:carry_count], refs[carry_count:]
    inputs, (cosine, sine, out, other, back, back_other, both_s, both_t, grads) = refs[: 4 * count], refs[4 * count :]
    for seq in range(count):
        own_s, got_s, own_t, got_t = inputs[4 * seq : 4 * seq + 4]
        lanes = slice(seq * SEQ, (seq + 1) * SEQ)
        for both, own, got in ((both_s, own_s, got_s), (both_t, own_t, got_t)):
            both[:ROWS, lanes] = own[...]
            both[ROWS:, lanes] = got[...]
    for seq in range(count):
        lanes = slice(seq * SEQ, (seq + 1) * SEQ)
        for kv in range(2):
            blocks = [table[AT_QUERY + 4 * kv + h] for h in range(4)] + [table[AT_KEY + kv]]
            rows = [pl.ds(pl.multiple_of(n * HD, HD), HD) for n in blocks]
            student = [both_s[at, lanes] for at in rows]
            teacher = [both_t[at, lanes] for at in rows]
            made = attention_gradient(student, teacher, cosine[...], sine[...])
            for at, value in zip(rows, made):
                grads[at, lanes] = value
    for n in range(8):
        row = pl.multiple_of(table[AT_CORE + n], SHARD)
        target = out if n < 4 else other
        target[n % 4 * SHARD : (n % 4 + 1) * SHARD, :] = grads[pl.ds(row, SHARD), :]
    for n in range(10):
        row = pl.multiple_of(ROWS + table[AT_BACK + n] * UNIT, UNIT)
        target = back if n < 5 else back_other
        unit = slice(n % 5 * UNIT, (n % 5 + 1) * UNIT)
        target[unit, target.shape[1] - count * SEQ :] = grads[pl.ds(row, UNIT), :]
    for value, target in zip(carried, (back, back_other)):
        target[:, : value.shape[1]] = value[...]


def attend(table, angles, sequences, carried=()):
    count = len(sequences)
    operands = [(table, None)] + [(value, block(value.shape)) for value in carried]
    wide = count * SEQ + (carried[0].shape[1] if carried else 0)
    for sequence in sequences:
        for own, (got, at) in sequence:
            operands += [(own, block((ROWS, SEQ))), (got, block((EXCHANGED, SEQ), 0, at))]
    operands += [(value, block((HALF, SEQ))) for value in angles]
    return call(
        lambda *refs: attend_kernel(count, len(carried), *refs),
        "attend",
        operands,
        [((CORE, count * SEQ), BF)] * 2 + [((SHARD, wide), BF)] * 2,
        [pltpu.VMEM((ROWS + EXCHANGED, count * SEQ), BF)] * 3,
        1.0 + 3.5 * count,
    )


TILE = 512


def fill(table, held, grads, backs):
    first = 0
    for grad in grads:
        held[:, first : first + grad.shape[1]] = grad[...]
        first += grad.shape[1]
    for unit in range(5):
        row = table[AT_FILL + unit]

        @pl.when(row >= 0)
        def _():
            at, first = pl.ds(pl.multiple_of(row, UNIT), UNIT), 0
            for back in backs:
                lanes = slice(first, first + back.shape[1])
                held[at, lanes] = back[unit * UNIT : (unit + 1) * UNIT, :]
                first = lanes.stop


def first_kernel(counts, table, *refs):
    grads, backs, tokens, (out, held) = split(refs, counts)

    @pl.when(pl.program_id(0) == 0)
    def _():
        fill(table, held, grads, backs)

    out[...] = dot(held[:, :SPAN], tokens[0][...]) + dot(held[:, SPAN:], tokens[1][...])


def second_kernel(parts, counts, table, *refs):
    grads, backs, tokens, befores, rest = split(refs, (*counts, len(parts)))
    outs, held = rest[:-1], rest[-1]

    @pl.when(pl.program_id(0) == 0)
    def _():
        fill(table, held, grads, backs)

    for (step, first, _), before, out in zip(parts, befores, outs):
        rows = pl.ds(pl.multiple_of(table[AT_STEP + step] + first, 16), PART)
        total = before[...] + dot(held[rows, :SPAN], tokens[0][...])
        total += dot(held[rows, SPAN:], tokens[1][...])
        out[...] = total.astype(out.dtype)


def weight_call(kernel, table, grads, backs, tokens, more, outs, microseconds):
    tile = lambda t, table: (0, t)
    return pl.pallas_call(
        lambda *refs: kernel((len(grads), len(backs), len(tokens)), *refs),
        grid_spec=pltpu.PrefetchScalarGridSpec(
            num_scalar_prefetch=1,
            grid=(D // TILE,),
            in_specs=[block(value.shape) for value in grads + backs]
            + [pl.BlockSpec((x.shape[0], TILE), tile) for x in tokens]
            + [pl.BlockSpec((PART, TILE), index) for _, index in more],
            out_specs=[pl.BlockSpec((rows, TILE), tile) for rows, _ in outs],
            scratch_shapes=[pltpu.VMEM((CORE, 2 * SPAN), BF)],
        ),
        out_shape=[jax.ShapeDtypeStruct((rows, D), dtype) for rows, dtype in outs],
        compiler_params=params(56),
        cost_estimate=cost(microseconds),
        name="weight_gradient",
    )(table, *grads, *backs, *tokens, *[value for value, _ in more])


def part_index(step, first):
    return lambda t, table: (table[AT_STEP + step] // PART + first // PART, t)


def adam_kernel(a, b, c, weight, one, two, weight_out, one_out, two_out):
    gradient = a[...].astype(F32) + (b[...].astype(F32) + c[...].astype(F32))
    first_new = BETA_ONE * one[...] + (1.0 - BETA_ONE) * gradient
    second_new = BETA_TWO * two[...] + (1.0 - BETA_TWO) * gradient * gradient
    step_dir = (
        first_new
        / (1.0 - BETA_ONE**STEP)
        / (jnp.sqrt(second_new / (1.0 - BETA_TWO**STEP)) + EPSILON)
    )
    master = weight[...]
    weight_out[...] = master - LEARN_RATE * (step_dir + DECAY * master)
    one_out[...] = first_new
    two_out[...] = second_new


def adam_body(*refs):
    pairs, rest = refs[:6], refs[6:]
    for at in range(2):

        @pl.when(pl.program_id(0) == at)
        def _():
            adam_kernel(*pairs[at::2], *rest)


ADAM_TILE = 1024


def adam(pairs, weight, one, two):
    straight = pl.BlockSpec((PART, ADAM_TILE), lambda k, t: (k, t))
    last = D // ADAM_TILE - 1
    low = pl.BlockSpec((PART, ADAM_TILE), lambda k, t: (0, jnp.where(k == 0, t, last)))
    high = pl.BlockSpec((PART, ADAM_TILE), lambda k, t: (0, jnp.where(k == 0, 0, t)))
    return pl.pallas_call(
        adam_body,
        grid=(2, D // ADAM_TILE),
        in_specs=[low, high] * 3 + [straight] * 3,
        out_specs=[straight] * 3,
        out_shape=[jax.ShapeDtypeStruct((SHARD, D), F32)] * 3,
        compiler_params=params(56),
        name="adam",
    )(*[value for pair in pairs for value in pair], weight, one, two)


def rotary_tables():
    positions = jnp.arange(SEQ).astype(F32)
    exponents = jnp.arange(HALF).astype(F32) * (2.0 / HD)
    frequency = THETA ** (-exponents)
    angles = frequency[:, None] * positions[None, :]
    return jnp.cos(angles), jnp.sin(angles)


def ring_gather(shard, up_again):
    below = send(shard, ALONG_Y[1])
    above = send(shard, ALONG_Y[3])
    far = send(below, ALONG_Y[1]) if up_again else send(above, ALONG_Y[3])
    return [shard, above, far, below]


def both_cores(pieces):
    return pieces + [send(piece, TO_CORE) for piece in pieces]


def per_device(tokens, student_weight, snapshot, moment_one, moment_two):
    own = tokens[0]
    master = student_weight[0]
    table = jnp.asarray(TABLE)[lax.axis_index("fsdp")]
    angles = rotary_tables()

    teacher = lax.ppermute(snapshot[0], "blk", [(g, (g + 1) % 8) for g in range(8)])
    plane = send(own, TO_PLANE)
    student_rows = both_cores(ring_gather(master.astype(BF), True))
    teacher_own = ring_gather(teacher, False)

    own_two, plane_two = [(own, 0), (own, 1)], [(plane, 0), (plane, 1)]
    two = [(0, 0), (1, 0)]
    *own_s, given = project(table, angles, own_two, [student_rows], two, [[0, 1]])
    teacher_own[2], teacher_own[3], given = lax.optimization_barrier(
        (teacher_own[2], teacher_own[3], given)
    )
    teacher_rows = both_cores(teacher_own)
    *own_t, given = project(table, angles, own_two, [teacher_rows], two, [[-1, -1, 0, 1]], given)
    got_own = send(given, TO_PLANE)
    plane_after, _ = lax.optimization_barrier((plane, own_t[0]))
    plane_two = [(plane_after, 0), (plane_after, 1)]
    *made, given_s, given_t = project(
        table,
        angles,
        plane_two,
        [student_rows, teacher_rows],
        two + [(0, 1), (1, 1)],
        [[0, 1], [2, 3]],
    )
    plane_s, plane_t = made[:2], made[2:]
    got_s, got_t = send(given_s, TO_PLANE), send(given_t, TO_PLANE)

    second = attend(
        table,
        angles,
        [[(plane_s[n], (got_own, n)), (plane_t[n], (got_own, 2 + n))] for n in range(2)],
    )
    got_s, got_t, _ = lax.optimization_barrier((got_s, got_t, second[2]))
    first = [attend(table, angles, [[(own_s[0], (got_s, 0)), (own_t[0], (got_t, 0))]])]
    back_first = [send(second[2], TO_PLANE), send(second[3], TO_PLANE)]
    got_s, got_t, *back_first, carried = lax.optimization_barrier(
        (got_s, got_t, *back_first, first[0][2])
    )
    back_first[1] = send(back_first[1], TO_CORE)
    first.append(
        attend(
            table,
            angles,
            [[(own_s[1], (got_s, 1)), (own_t[1], (got_t, 1))]],
            (carried, first[0][3]),
        )
    )
    back_second = [send(first[1][2], TO_PLANE), send(first[1][3], TO_BOTH)]
    (before,) = weight_call(
        first_kernel,
        table,
        [part[0] for part in first] + [send(part[1], TO_CORE) for part in first],
        back_first,
        [own, send(own, TO_CORE)],
        [],
        [(CORE, F32)],
        6.0,
    )

    def weight_blocks(parts):
        return weight_call(
            lambda *refs: second_kernel(parts, *refs),
            table,
            [second[0], send(second[1], TO_CORE)],
            back_second,
            [plane_after, send(plane_after, TO_CORE)],
            [(before, part_index(step, first)) for step, first, _ in parts],
            [(PART, dtype) for _, _, dtype in parts],
            5.0,
        )

    up, down = ALONG_Y[1], ALONG_Y[3]
    far_low, far_high, next_high, last_low = weight_blocks(
        ((2, 0, BF), (2, PART, BF), (1, PART, BF), (3, 0, BF))
    )
    far_low, far_high = send(far_low, up), send(far_high, down)
    from_below, from_above = [None, send(next_high, up)], [send(last_low, down), None]
    next_low, last_high, *own_parts = weight_blocks(
        ((1, 0, F32), (3, PART, F32), (0, 0, F32), (0, PART, F32))
    )
    from_below[0] = send((next_low + far_low.astype(F32)).astype(BF), up)
    from_above[1] = send((last_high + far_high.astype(F32)).astype(BF), down)
    pairs = [own_parts, from_below, from_above]
    updated = adam(pairs, master, moment_one[0], moment_two[0])
    return tuple(value[None] for value in updated)


def solution(mesh):
    spec = P("blk", "fsdp", None)
    return jax.shard_map(
        per_device,
        mesh=mesh,
        in_specs=(spec,) * 5,
        out_specs=(spec,) * 3,
        check_vma=False,
    )
```

```python
import math

import jax
import jax.numpy as jnp
import numpy as np
from jax import lax
from jax.experimental import pallas as pl
from jax.experimental.pallas import tpu as pltpu
from jax.sharding import PartitionSpec as P

HEADS = 16
KVH = 4
HD = 128
SEQ = 256
STEP = 100
D = 2048
THETA = 500000.0
BETA_ONE = 0.9
BETA_TWO = 0.95
LEARN_RATE = 0.002
DECAY = 0.1
EPSILON = 1e-08
MASKED = -1e30

BF = jnp.bfloat16
F32 = jnp.float32
SHARD = 160
ROWS = 8 * SHARD
UNIT = 32
PART = SHARD // 2
HALF = HD // 2
CORE = 4 * SHARD
EXCHANGED = 2 * HD
INV_ROOT = 1.0 / math.sqrt(HD)

AT_WEIGHT, AT_GIVEN, AT_QUERY, AT_KEY, AT_CORE, AT_STEP, AT_FILL, AT_BACK = 0, 8, 9, 17, 19, 27, 31, 36
GIVEN = (1024, 768)
QUERY = (tuple(range(8)), (10, 11, 0, 1, 2, 3, 4, 5))
KEY = ((10, 11), (8, 9))


def given_units(plane, core):
    rows = [GIVEN[plane] + UNIT * unit for unit in range(8)]
    return [(u, r // 320 * 160 + r % 160) for u, r in enumerate(rows) if r % 320 // 160 == core]


def build_table():
    table = np.zeros((16, 46), np.int32)
    for d in range(16):
        z, y, c = d // 8, d % 8 // 2, d % 2
        gathered = [320 * ((y + s) % 4) + 160 * (c ^ r) for r in range(2) for s in range(4)]
        cores = [320 * k + 160 * (c ^ r) for r in range(2) for k in range(4)]
        steps = [160 * ((y + s) % 4) for s in range(4)]
        fill = ([row for _, row in given_units(z, c)] + [-1] * 5)[:5]
        back = []
        for r in range(2):
            back += ([unit for unit, _ in given_units(1 - z, c ^ r)] + [0] * 5)[:5]
        table[d] = gathered + [GIVEN[z], *QUERY[z], *KEY[z]] + cores + steps + fill + back
    return table


TABLE = build_table()


def pairs_of(function):
    out = []
    for d in range(16):
        z, y, c = function(d // 8, d % 8 // 2, d % 2)
        out.append((d, z % 2 * 8 + y % 4 * 2 + c % 2))
    return out


TO_CORE = pairs_of(lambda z, y, c: (z, y, c + 1))
TO_PLANE = pairs_of(lambda z, y, c: (z + 1, y, c))
TO_BOTH = pairs_of(lambda z, y, c: (z + 1, y, c + 1))
ALONG_Y = [pairs_of(lambda z, y, c, s=s: (z, y + s, c)) for s in range(4)]


def send(value, pairs):
    return lax.ppermute(value, "fsdp", pairs)


def params(mib):
    return pltpu.CompilerParams(vmem_limit_bytes=mib * 2**20)


def cost(microseconds):
    return pl.CostEstimate(flops=int(microseconds * 1e9), bytes_accessed=2**20, transcendentals=0)


def dot(a, b, dims=((1,), (0,))):
    return lax.dot_general(a, b, (dims, ((), ())), preferred_element_type=F32)


def rotated(raw, cosine, sine):
    front, back = raw[:HALF], raw[HALF:]
    return jnp.concatenate([front * cosine - back * sine, back * cosine + front * sine], axis=0)


def split(refs, counts):
    out, refs = [], list(refs)
    for count in counts:
        out.append(refs[:count])
        refs = refs[count:]
    return out + [refs]


ANY = pl.BlockSpec(memory_space=pl.ANY)


def block(shape, row=0, column=0):
    return pl.BlockSpec(shape, lambda s, table: (row, column))


def call(kernel, name, operands, outs, scratch, microseconds):
    return pl.pallas_call(
        kernel,
        grid_spec=pltpu.PrefetchScalarGridSpec(
            num_scalar_prefetch=1,
            grid=(1,),
            in_specs=[spec for _, spec in operands[1:]],
            out_specs=[spec[0] if spec else block(shape) for shape, _, *spec in outs],
            scratch_shapes=scratch,
        ),
        out_shape=[jax.ShapeDtypeStruct(shape, dtype) for shape, dtype, *_ in outs],
        compiler_params=params(56),
        cost_estimate=cost(microseconds),
        name=name,
    )(*[value for value, _ in operands])


def project_kernel(jobs, groups, x_count, set_count, table, *refs):
    refs = list(refs)
    carried, refs = refs[0], refs[1:]
    xs, refs = refs[:x_count], refs[x_count:]
    cosine, sine, refs = refs[0], refs[1], refs[2:]
    arrays, refs = refs[: 8 * set_count], refs[8 * set_count :]
    outs, refs = refs[: len(jobs)], refs[len(jobs) :]
    givens, refs = refs[: len(groups)], refs[len(groups) :]
    held, sems = refs[:-1], refs[-1]

    def copy(at, n):
        rows = pl.ds(pl.multiple_of(table[AT_WEIGHT + n], SHARD), SHARD)
        return pltpu.make_async_copy(arrays[8 * at + n], held[at].at[rows], sems.at[8 * at + n])

    for at in range(set_count):
        for n in range(8):
            copy(at, n).start()
    for at in range(set_count):
        for n in range(8):
            copy(at, n).wait()
        for job, (x, own_set) in enumerate(jobs):
            if own_set != at:
                continue
            for half in range(2):
                part = dot(held[at][half * CORE : (half + 1) * CORE, :], xs[x][...], ((1,), (1,)))
                for h in range(5):
                    row = half * CORE + h * HD
                    value = rotated(part[h * HD : (h + 1) * HD], cosine[...], sine[...])
                    outs[job][row : row + HD, :] = value.astype(BF)
    rows = pl.ds(pl.multiple_of(table[AT_GIVEN], EXCHANGED), EXCHANGED)
    for given, group in zip(givens, groups):
        for n, job in enumerate(group):
            lanes = slice(n * SEQ, (n + 1) * SEQ)
            given[:, lanes] = outs[job][rows, :] if job >= 0 else carried[:, lanes]


def project(table, angles, xs, sets, jobs, groups, carried=None):
    if carried is None:
        carried = jnp.zeros((16, 128), BF)
    operands = [(table, None), (carried, block(carried.shape))]
    operands += [(x, block((SEQ, D), at)) for x, at in xs]
    operands += [(value, block((HALF, SEQ))) for value in angles]
    operands += [(array, ANY) for arrays in sets for array in arrays]
    return call(
        lambda *refs: project_kernel(jobs, groups, len(xs), len(sets), *refs),
        "project",
        operands,
        [((ROWS, SEQ), BF)] * len(jobs) + [((EXCHANGED, SEQ * len(group)), BF) for group in groups],
        [pltpu.VMEM((ROWS, D), BF)] * len(sets) + [pltpu.SemaphoreType.DMA((8 * len(sets),))],
        0.5 if len(sets) == 1 else 8.0,
    )


SCALE = INV_ROOT * math.log2(math.e)
SPAN = 2 * SEQ


def softmax_parts(scores, causal):
    scores = jnp.where(causal, scores * SCALE, MASKED)
    power = jnp.exp2(scores - jnp.max(scores, axis=0, keepdims=True))
    return power, (1.0 / HEADS) / jnp.sum(power, axis=0, keepdims=True)


def attention_gradient(student, teacher, cosine, sine):
    lane = lax.broadcasted_iota(jnp.int32, (SEQ, 4 * SEQ), 1) % SEQ
    causal = lax.broadcasted_iota(jnp.int32, (SEQ, 4 * SEQ), 0) <= lane
    queries = jnp.concatenate(student[:4], axis=1)
    power_s, inverse_s = softmax_parts(dot(student[4].T, queries), causal)
    others = jnp.concatenate(teacher[:4], axis=1)
    power_t, inverse_t = softmax_parts(dot(teacher[4].T, others), causal)
    spread = (power_s * inverse_s - power_t * inverse_t).astype(BF)
    query_grads = dot(student[4], spread)
    grads = [query_grads[:, h * SEQ : (h + 1) * SEQ] for h in range(4)]
    grads.append(dot(queries, spread, ((1,), (1,))))
    return [rotated(g * INV_ROOT, cosine, -sine).astype(BF) for g in grads]


def attend_kernel(count, carry_count, table, *refs):
    carried, refs = refs[:carry_count], refs[carry_count:]
    inputs, (cosine, sine, out, other, back, back_other, both_s, both_t, grads) = refs[: 4 * count], refs[4 * count :]
    for seq in range(count):
        own_s, got_s, own_t, got_t = inputs[4 * seq : 4 * seq + 4]
        lanes = slice(seq * SEQ, (seq + 1) * SEQ)
        for both, own, got in ((both_s, own_s, got_s), (both_t, own_t, got_t)):
            both[:ROWS, lanes] = own[...]
            both[ROWS:, lanes] = got[...]
    for seq in range(count):
        lanes = slice(seq * SEQ, (seq + 1) * SEQ)
        for kv in range(2):
            blocks = [table[AT_QUERY + 4 * kv + h] for h in range(4)] + [table[AT_KEY + kv]]
            rows = [pl.ds(pl.multiple_of(n * HD, HD), HD) for n in blocks]
            student = [both_s[at, lanes] for at in rows]
            teacher = [both_t[at, lanes] for at in rows]
            made = attention_gradient(student, teacher, cosine[...], sine[...])
            for at, value in zip(rows, made):
                grads[at, lanes] = value
    for n in range(8):
        row = pl.multiple_of(table[AT_CORE + n], SHARD)
        target = out if n < 4 else other
        lanes = slice(target.shape[1] - count * SEQ, target.shape[1])
        target[n % 4 * SHARD : (n % 4 + 1) * SHARD, lanes] = grads[pl.ds(row, SHARD), :]
    for n in range(10):
        row = pl.multiple_of(ROWS + table[AT_BACK + n] * UNIT, UNIT)
        target = back if n < 5 else back_other
        unit = slice(n % 5 * UNIT, (n % 5 + 1) * UNIT)
        target[unit, target.shape[1] - count * SEQ :] = grads[pl.ds(row, UNIT), :]
    for value, target in zip(carried, (back, back_other, other)):
        target[: value.shape[0], : value.shape[1]] = value[...]
    for value in carried[3:]:
        other[CORE:, :] = value[...]


def attend(table, angles, sequences, carried=()):
    count = len(sequences)
    operands = [(table, None)] + [(value, block(value.shape)) for value in carried]
    wide = count * SEQ + (carried[0].shape[1] if carried else 0)
    for sequence in sequences:
        for own, (got, at) in sequence:
            operands += [(own, block((ROWS, SEQ))), (got, block((EXCHANGED, SEQ), 0, at))]
    operands += [(value, block((HALF, SEQ))) for value in angles]
    return call(
        lambda *refs: attend_kernel(count, len(carried), *refs),
        "attend",
        operands,
        [((CORE, count * SEQ), BF), ((CORE + (SHARD if carried else 0), wide), BF)]
        + [((SHARD, wide), BF)] * 2,
        [pltpu.VMEM((ROWS + EXCHANGED, count * SEQ), BF)] * 3,
        1.0 + 3.5 * count,
    )


TILE = 1024


def fill(table, held, grads, backs):
    first = 0
    for grad in grads:
        held[:, first : first + grad.shape[1]] = grad[...]
        first += grad.shape[1]
    for unit in range(5):
        row = table[AT_FILL + unit]

        @pl.when(row >= 0)
        def _():
            at, first = pl.ds(pl.multiple_of(row, UNIT), UNIT), 0
            for back in backs:
                lanes = slice(first, first + back.shape[1])
                held[at, lanes] = back[unit * UNIT : (unit + 1) * UNIT, :]
                first = lanes.stop


def weight_kernel(parts, counts, table, *refs):
    grads, backs, tokens, rest = split(refs, counts)
    outs, held = rest[:-1], rest[-1]

    @pl.when(pl.program_id(0) == 0)
    def _():
        fill(table, held, grads, backs)

    for (step, first, _), out in zip(parts, outs):
        rows = pl.ds(pl.multiple_of(table[AT_STEP + step] + first, 16), PART)
        total = dot(held[rows, :SPAN], tokens[0][...])
        for n in range(1, 4):
            total += dot(held[rows, n * SPAN : (n + 1) * SPAN], tokens[n][...])
        out[...] = total.astype(out.dtype)


def weight_gradient(parts, table, grads, backs, tokens):
    tile = lambda t, table: (0, t)
    return pl.pallas_call(
        lambda *refs: weight_kernel(parts, (len(grads), len(backs), len(tokens)), *refs),
        grid_spec=pltpu.PrefetchScalarGridSpec(
            num_scalar_prefetch=1,
            grid=(D // TILE,),
            in_specs=[block((rows, x.shape[1]), at) for x, rows, at in grads + backs]
            + [pl.BlockSpec((SPAN, TILE), tile)] * 4,
            out_specs=[pl.BlockSpec((PART, TILE), tile)] * len(parts),
            scratch_shapes=[pltpu.VMEM((CORE, 4 * SPAN), BF)],
        ),
        out_shape=[jax.ShapeDtypeStruct((PART, D), dtype) for _, _, dtype in parts],
        compiler_params=params(56),
        cost_estimate=cost(8.0),
        name="weight_gradient",
    )(table, *[x for x, _, _ in grads + backs], *tokens)


def adam_kernel(a, b, c, weight, one, two, weight_out, one_out, two_out):
    gradient = a[...].astype(F32) + (b[...].astype(F32) + c[...].astype(F32))
    first_new = BETA_ONE * one[...] + (1.0 - BETA_ONE) * gradient
    second_new = BETA_TWO * two[...] + (1.0 - BETA_TWO) * gradient * gradient
    step_dir = (
        first_new
        / (1.0 - BETA_ONE**STEP)
        / (jnp.sqrt(second_new / (1.0 - BETA_TWO**STEP)) + EPSILON)
    )
    master = weight[...]
    weight_out[...] = master - LEARN_RATE * (step_dir + DECAY * master)
    one_out[...] = first_new
    two_out[...] = second_new


def adam_body(*refs):
    pairs, rest = refs[:6], refs[6:]
    for at in range(2):

        @pl.when(pl.program_id(0) == at)
        def _():
            adam_kernel(*pairs[at::2], *rest)


def adam(pairs, weight, one, two):
    straight = pl.BlockSpec((PART, D), lambda k: (k, 0))
    whole = pl.BlockSpec((PART, D), lambda k: (0, 0))
    return pl.pallas_call(
        adam_body,
        grid=(2,),
        in_specs=[whole] * 6 + [straight] * 3,
        out_specs=[straight] * 3,
        out_shape=[jax.ShapeDtypeStruct((SHARD, D), F32)] * 3,
        compiler_params=params(56),
        name="adam",
    )(*[value for pair in pairs for value in pair], weight, one, two)


def rotary_tables():
    positions = jnp.arange(SEQ).astype(F32)
    exponents = jnp.arange(HALF).astype(F32) * (2.0 / HD)
    frequency = THETA ** (-exponents)
    angles = frequency[:, None] * positions[None, :]
    return jnp.cos(angles), jnp.sin(angles)


def ring_gather(shard, up_again):
    below = send(shard, ALONG_Y[1])
    above = send(shard, ALONG_Y[3])
    far = send(below, ALONG_Y[1]) if up_again else send(above, ALONG_Y[3])
    return [shard, above, far, below]


def both_cores(pieces):
    return pieces + [send(piece, TO_CORE) for piece in pieces]


def per_device(tokens, student_weight, snapshot, moment_one, moment_two):
    own = tokens[0]
    master = student_weight[0]
    table = jnp.asarray(TABLE)[lax.axis_index("fsdp")]
    angles = rotary_tables()

    teacher = lax.ppermute(snapshot[0], "blk", [(g, (g + 1) % 8) for g in range(8)])
    plane = send(own, TO_PLANE)
    student_rows = both_cores(ring_gather(master.astype(BF), True))
    teacher_own = ring_gather(teacher, False)

    own_two, plane_two = [(own, 0), (own, 1)], [(plane, 0), (plane, 1)]
    two = [(0, 0), (1, 0)]
    *own_s, given = project(table, angles, own_two, [student_rows], two, [[0, 1]])
    teacher_own[2], teacher_own[3], given = lax.optimization_barrier(
        (teacher_own[2], teacher_own[3], given)
    )
    teacher_rows = both_cores(teacher_own)
    *own_t, given = project(table, angles, own_two, [teacher_rows], two, [[-1, -1, 0, 1]], given)
    got_own = send(given, TO_PLANE)
    plane_after, _ = lax.optimization_barrier((plane, own_t[0]))
    plane_two = [(plane_after, 0), (plane_after, 1)]
    *made, given_0, given_1 = project(
        table,
        angles,
        plane_two,
        [student_rows, teacher_rows],
        two + [(0, 1), (1, 1)],
        [[0, 2], [1, 3]],
    )
    plane_s, plane_t = made[:2], made[2:]
    got_0, got_1 = send(given_0, TO_PLANE), send(given_1, TO_PLANE)

    second = attend(
        table,
        angles,
        [[(plane_s[n], (got_own, n)), (plane_t[n], (got_own, 2 + n))] for n in range(2)],
    )
    got_0, _ = lax.optimization_barrier((got_0, second[2]))
    first = [attend(table, angles, [[(own_s[0], (got_0, 0)), (own_t[0], (got_0, 1))]])]
    back_first = [send(second[2], TO_PLANE), send(second[3], TO_PLANE)]
    core_second, core_own = send(second[1], TO_CORE), send(own, TO_CORE)
    core_plane = send(plane_after, TO_CORE)
    got_1, *back_first, core_second, core_own, core_plane, carried = lax.optimization_barrier(
        (got_1, *back_first, core_second, core_own, core_plane, first[0][2])
    )
    first.append(
        attend(
            table,
            angles,
            [[(own_s[1], (got_1, 0)), (own_t[1], (got_1, 1))]],
            (carried, first[0][3], first[0][1], back_first[1]),
        )
    )
    back_second = [send(first[1][2], TO_PLANE), send(first[1][3], TO_BOTH)]
    core_first = send(first[1][1], TO_CORE)
    grads = [(first[0][0], CORE, 0), (first[1][0], CORE, 0), (core_first, CORE, 0)]
    grads += [(second[0], CORE, 0), (core_second, CORE, 0)]
    backs = [(back_first[0], SHARD, 0), (core_first, SHARD, CORE // SHARD)]
    backs += [(value, SHARD, 0) for value in back_second]

    def weight_blocks(parts):
        return weight_gradient(parts, table, grads, backs, [own, core_own, plane_after, core_plane])

    up, down = ALONG_Y[1], ALONG_Y[3]
    far_low, far_high, next_high, last_low = weight_blocks(
        ((2, 0, BF), (2, PART, BF), (1, PART, BF), (3, 0, BF))
    )
    far_low, far_high = send(far_low, up), send(far_high, down)
    from_below, from_above = [None, send(next_high, up)], [send(last_low, down), None]
    next_low, last_high, *own_parts = weight_blocks(
        ((1, 0, F32), (3, PART, F32), (0, 0, F32), (0, PART, F32))
    )
    from_below[0] = send((next_low + far_low.astype(F32)).astype(BF), up)
    from_above[1] = send((last_high + far_high.astype(F32)).astype(BF), down)
    pairs = [own_parts, from_below, from_above]
    updated = adam(pairs, master, moment_one[0], moment_two[0])
    return tuple(value[None] for value in updated)


def solution(mesh):
    spec = P("blk", "fsdp", None)
    return jax.shard_map(
        per_device,
        mesh=mesh,
        in_specs=(spec,) * 5,
        out_specs=(spec,) * 3,
        check_vma=False,
    )
```

```python
import math

import jax
import jax.numpy as jnp
import numpy as np
from jax import lax
from jax.experimental import pallas as pl
from jax.experimental.pallas import tpu as pltpu
from jax.sharding import PartitionSpec as P

HEADS = 16
KVH = 4
HD = 128
SEQ = 256
STEP = 100
D = 2048
THETA = 500000.0
BETA_ONE = 0.9
BETA_TWO = 0.95
LEARN_RATE = 0.002
DECAY = 0.1
EPSILON = 1e-08
MASKED = -1e30

BF = jnp.bfloat16
F32 = jnp.float32
SHARD = 160
ROWS = 8 * SHARD
UNIT = 32
PART = SHARD // 2
HALF = HD // 2
CORE = 4 * SHARD
EXCHANGED = 2 * HD
INV_ROOT = 1.0 / math.sqrt(HD)

AT_WEIGHT, AT_GIVEN, AT_QUERY, AT_KEY, AT_CORE, AT_STEP, AT_FILL, AT_BACK = 0, 8, 9, 17, 19, 27, 31, 36
GIVEN = (1024, 768)
QUERY = (tuple(range(8)), (10, 11, 0, 1, 2, 3, 4, 5))
KEY = ((10, 11), (8, 9))


def given_units(plane, core):
    rows = [GIVEN[plane] + UNIT * unit for unit in range(8)]
    return [(u, r // 320 * 160 + r % 160) for u, r in enumerate(rows) if r % 320 // 160 == core]


def build_table():
    table = np.zeros((16, 46), np.int32)
    for d in range(16):
        z, y, c = d // 8, d % 8 // 2, d % 2
        gathered = [320 * ((y + s) % 4) + 160 * (c ^ r) for r in range(2) for s in range(4)]
        cores = [320 * k + 160 * (c ^ r) for r in range(2) for k in range(4)]
        steps = [160 * ((y + s) % 4) for s in range(4)]
        fill = ([row for _, row in given_units(z, c)] + [-1] * 5)[:5]
        back = []
        for r in range(2):
            back += ([unit for unit, _ in given_units(1 - z, c ^ r)] + [0] * 5)[:5]
        table[d] = gathered + [GIVEN[z], *QUERY[z], *KEY[z]] + cores + steps + fill + back
    return table


TABLE = build_table()


def pairs_of(function):
    out = []
    for d in range(16):
        z, y, c = function(d // 8, d % 8 // 2, d % 2)
        out.append((d, z % 2 * 8 + y % 4 * 2 + c % 2))
    return out


TO_CORE = pairs_of(lambda z, y, c: (z, y, c + 1))
TO_PLANE = pairs_of(lambda z, y, c: (z + 1, y, c))
TO_BOTH = pairs_of(lambda z, y, c: (z + 1, y, c + 1))
ALONG_Y = [pairs_of(lambda z, y, c, s=s: (z, y + s, c)) for s in range(4)]


def send(value, pairs):
    return lax.ppermute(value, "fsdp", pairs)


def params(mib):
    return pltpu.CompilerParams(vmem_limit_bytes=mib * 2**20)


def cost(microseconds):
    return pl.CostEstimate(flops=int(microseconds * 1e9), bytes_accessed=2**20, transcendentals=0)


def dot(a, b, dims=((1,), (0,))):
    return lax.dot_general(a, b, (dims, ((), ())), preferred_element_type=F32)


def rotated(raw, cosine, sine):
    front, back = raw[:HALF], raw[HALF:]
    return jnp.concatenate([front * cosine - back * sine, back * cosine + front * sine], axis=0)


def split(refs, counts):
    out, refs = [], list(refs)
    for count in counts:
        out.append(refs[:count])
        refs = refs[count:]
    return out + [refs]


ANY = pl.BlockSpec(memory_space=pl.ANY)


def block(shape, row=0, column=0):
    return pl.BlockSpec(shape, lambda s, table: (row, column))


def call(kernel, name, operands, outs, scratch, microseconds):
    return pl.pallas_call(
        kernel,
        grid_spec=pltpu.PrefetchScalarGridSpec(
            num_scalar_prefetch=1,
            grid=(1,),
            in_specs=[spec for _, spec in operands[1:]],
            out_specs=[spec[0] if spec else block(shape) for shape, _, *spec in outs],
            scratch_shapes=scratch,
        ),
        out_shape=[jax.ShapeDtypeStruct(shape, dtype) for shape, dtype, *_ in outs],
        compiler_params=params(56),
        cost_estimate=cost(microseconds),
        name=name,
    )(*[value for value, _ in operands])


def project_kernel(jobs, groups, x_count, set_count, table, *refs):
    refs = list(refs)
    carried, refs = refs[0], refs[1:]
    xs, refs = refs[:x_count], refs[x_count:]
    cosine, sine, refs = refs[0], refs[1], refs[2:]
    arrays, refs = refs[: 8 * set_count], refs[8 * set_count :]
    outs, refs = refs[: len(jobs)], refs[len(jobs) :]
    givens, refs = refs[: len(groups)], refs[len(groups) :]
    held, sems = refs[:-1], refs[-1]

    def copy(at, n):
        rows = pl.ds(pl.multiple_of(table[AT_WEIGHT + n], SHARD), SHARD)
        return pltpu.make_async_copy(arrays[8 * at + n], held[at].at[rows], sems.at[8 * at + n])

    for at in range(set_count):
        for n in range(8):
            copy(at, n).start()
    for at in range(set_count):
        for n in range(8):
            copy(at, n).wait()
        for job, (x, own_set) in enumerate(jobs):
            if own_set != at:
                continue
            for half in range(2):
                part = dot(held[at][half * CORE : (half + 1) * CORE, :], xs[x][...], ((1,), (1,)))
                for h in range(5):
                    row = half * CORE + h * HD
                    value = rotated(part[h * HD : (h + 1) * HD], cosine[...], sine[...])
                    outs[job][row : row + HD, :] = value.astype(BF)
    rows = pl.ds(pl.multiple_of(table[AT_GIVEN], EXCHANGED), EXCHANGED)
    for given, group in zip(givens, groups):
        for n, job in enumerate(group):
            lanes = slice(n * SEQ, (n + 1) * SEQ)
            given[:, lanes] = outs[job][rows, :] if job >= 0 else carried[:, lanes]


def project(table, angles, xs, sets, jobs, groups, carried=None):
    carried = angles[0] if carried is None else carried
    operands = [(table, None), (carried, block(carried.shape))]
    operands += [(x, block((SEQ, D), at)) for x, at in xs]
    operands += [(value, block((HALF, SEQ))) for value in angles]
    operands += [(array, ANY) for arrays in sets for array in arrays]
    return call(
        lambda *refs: project_kernel(jobs, groups, len(xs), len(sets), *refs),
        "project",
        operands,
        [((ROWS, SEQ), BF)] * len(jobs) + [((EXCHANGED, SEQ * len(group)), BF) for group in groups],
        [pltpu.VMEM((ROWS, D), BF)] * len(sets) + [pltpu.SemaphoreType.DMA((8 * len(sets),))],
        0.5 if len(sets) == 1 else 8.0,
    )


SCALE = INV_ROOT * math.log2(math.e)
SPAN = 2 * SEQ


def softmax_parts(scores, causal):
    scores = jnp.where(causal, scores * SCALE, MASKED)
    power = jnp.exp2(scores - jnp.max(scores, axis=0, keepdims=True))
    return power, (1.0 / HEADS) / jnp.sum(power, axis=0, keepdims=True)


def attention_gradient(student, teacher, cosine, sine):
    lane = lax.broadcasted_iota(jnp.int32, (SEQ, 4 * SEQ), 1) % SEQ
    causal = lax.broadcasted_iota(jnp.int32, (SEQ, 4 * SEQ), 0) <= lane
    queries = jnp.concatenate(student[:4], axis=1)
    power_s, inverse_s = softmax_parts(dot(student[4].T, queries), causal)
    others = jnp.concatenate(teacher[:4], axis=1)
    power_t, inverse_t = softmax_parts(dot(teacher[4].T, others), causal)
    spread = (power_s * inverse_s - power_t * inverse_t).astype(BF)
    query_grads = dot(student[4], spread)
    grads = [query_grads[:, h * SEQ : (h + 1) * SEQ] for h in range(4)]
    grads.append(dot(queries, spread, ((1,), (1,))))
    return [rotated(g * INV_ROOT, cosine, -sine).astype(BF) for g in grads]


def attend_kernel(count, carry_count, table, *refs):
    carried, refs = refs[:carry_count], refs[carry_count:]
    inputs, (cosine, sine, out, other, back, back_other, both_s, both_t, grads) = refs[: 4 * count], refs[4 * count :]
    for seq in range(count):
        own_s, got_s, own_t, got_t = inputs[4 * seq : 4 * seq + 4]
        lanes = slice(seq * SEQ, (seq + 1) * SEQ)
        for both, own, got in ((both_s, own_s, got_s), (both_t, own_t, got_t)):
            both[:ROWS, lanes] = own[...]
            both[ROWS:, lanes] = got[...]
    for seq in range(count):
        lanes = slice(seq * SEQ, (seq + 1) * SEQ)
        for kv in range(2):
            blocks = [table[AT_QUERY + 4 * kv + h] for h in range(4)] + [table[AT_KEY + kv]]
            rows = [pl.ds(pl.multiple_of(n * HD, HD), HD) for n in blocks]
            student = [both_s[at, lanes] for at in rows]
            teacher = [both_t[at, lanes] for at in rows]
            made = attention_gradient(student, teacher, cosine[...], sine[...])
            for at, value in zip(rows, made):
                grads[at, lanes] = value
    for n in range(8):
        row = pl.multiple_of(table[AT_CORE + n], SHARD)
        target = out if n < 4 else other
        target[n % 4 * SHARD : (n % 4 + 1) * SHARD, :] = grads[pl.ds(row, SHARD), :]
    for n in range(10):
        row = pl.multiple_of(ROWS + table[AT_BACK + n] * UNIT, UNIT)
        target = back if n < 5 else back_other
        unit = slice(n % 5 * UNIT, (n % 5 + 1) * UNIT)
        target[unit, target.shape[1] - count * SEQ :] = grads[pl.ds(row, UNIT), :]
    for value, target in zip(carried, (back, back_other)):
        target[:, : value.shape[1]] = value[...]


def attend(table, angles, sequences, carried=()):
    count = len(sequences)
    operands = [(table, None)] + [(value, block(value.shape)) for value in carried]
    wide = count * SEQ + (carried[0].shape[1] if carried else 0)
    for sequence in sequences:
        for own, (got, at) in sequence:
            operands += [(own, block((ROWS, SEQ))), (got, block((EXCHANGED, SEQ), 0, at))]
    operands += [(value, block((HALF, SEQ))) for value in angles]
    return call(
        lambda *refs: attend_kernel(count, len(carried), *refs),
        "attend",
        operands,
        [((CORE, count * SEQ), BF)] * 2 + [((SHARD, wide), BF)] * 2,
        [pltpu.VMEM((ROWS + EXCHANGED, count * SEQ), BF)] * 3,
        1.0 + 3.5 * count,
    )


TILE = 1024


def fill(table, held, grads, backs):
    first = 0
    for grad in grads:
        held[:, first : first + grad.shape[1]] = grad[...]
        first += grad.shape[1]
    for unit in range(5):
        row = table[AT_FILL + unit]

        @pl.when(row >= 0)
        def _():
            at, first = pl.ds(pl.multiple_of(row, UNIT), UNIT), 0
            for back in backs:
                lanes = slice(first, first + back.shape[1])
                held[at, lanes] = back[unit * UNIT : (unit + 1) * UNIT, :]
                first = lanes.stop


def first_kernel(counts, table, *refs):
    grads, backs, tokens, (out, held) = split(refs, counts)

    @pl.when(pl.program_id(0) == 0)
    def _():
        fill(table, held, grads, backs)

    out[...] = dot(held[:, :SPAN], tokens[0][...]) + dot(held[:, SPAN:], tokens[1][...])


def second_kernel(parts, counts, table, *refs):
    grads, backs, tokens, befores, rest = split(refs, (*counts, len(parts)))
    outs, held = rest[:-1], rest[-1]

    @pl.when(pl.program_id(0) == 0)
    def _():
        fill(table, held, grads, backs)

    for (step, first, _), before, out in zip(parts, befores, outs):
        rows = pl.ds(pl.multiple_of(table[AT_STEP + step] + first, 16), PART)
        total = before[...] + dot(held[rows, :SPAN], tokens[0][...])
        total += dot(held[rows, SPAN:], tokens[1][...])
        out[...] = total.astype(out.dtype)


def weight_call(kernel, table, grads, backs, tokens, more, outs, microseconds):
    tile = lambda t, table: (0, t)
    return pl.pallas_call(
        lambda *refs: kernel((len(grads), len(backs), len(tokens)), *refs),
        grid_spec=pltpu.PrefetchScalarGridSpec(
            num_scalar_prefetch=1,
            grid=(D // TILE,),
            in_specs=[block(value.shape) for value in grads + backs]
            + [pl.BlockSpec((x.shape[0], TILE), tile) for x in tokens]
            + [pl.BlockSpec((PART, TILE), index) for _, index in more],
            out_specs=[pl.BlockSpec((rows, TILE), tile) for rows, _ in outs],
            scratch_shapes=[pltpu.VMEM((CORE, 2 * SPAN), BF)],
        ),
        out_shape=[jax.ShapeDtypeStruct((rows, D), dtype) for rows, dtype in outs],
        compiler_params=params(56),
        cost_estimate=cost(microseconds),
        name="weight_gradient",
    )(table, *grads, *backs, *tokens, *[value for value, _ in more])


def part_index(step, first):
    return lambda t, table: (table[AT_STEP + step] // PART + first // PART, t)


def adam_kernel(a, b, c, weight, one, two, weight_out, one_out, two_out):
    gradient = a[...].astype(F32) + (b[...].astype(F32) + c[...].astype(F32))
    first_new = BETA_ONE * one[...] + (1.0 - BETA_ONE) * gradient
    second_new = BETA_TWO * two[...] + (1.0 - BETA_TWO) * gradient * gradient
    step_dir = (
        first_new
        / (1.0 - BETA_ONE**STEP)
        / (jnp.sqrt(second_new / (1.0 - BETA_TWO**STEP)) + EPSILON)
    )
    master = weight[...]
    weight_out[...] = master - LEARN_RATE * (step_dir + DECAY * master)
    one_out[...] = first_new
    two_out[...] = second_new


def adam_body(*refs):
    pairs, rest = refs[:6], refs[6:]
    for at in range(2):

        @pl.when(pl.program_id(0) == at)
        def _():
            adam_kernel(*pairs[at::2], *rest)


def add_kernel(a, b, c, d, low, high):
    low[...] = (a[...] + b[...].astype(F32)).astype(BF)
    high[...] = (c[...] + d[...].astype(F32)).astype(BF)


def add(*values):
    whole = pl.BlockSpec((PART, D), lambda: (0, 0))
    return pl.pallas_call(
        add_kernel,
        in_specs=[whole] * 4,
        out_specs=[whole] * 2,
        out_shape=[jax.ShapeDtypeStruct((PART, D), BF)] * 2,
        compiler_params=params(56),
        cost_estimate=cost(0.5),
        name="add",
    )(*values)


def adam(pairs, weight, one, two):
    straight = pl.BlockSpec((PART, D), lambda k: (k, 0))
    whole = pl.BlockSpec((PART, D), lambda k: (0, 0))
    return pl.pallas_call(
        adam_body,
        grid=(2,),
        in_specs=[whole] * 6 + [straight] * 3,
        out_specs=[straight] * 3,
        out_shape=[jax.ShapeDtypeStruct((SHARD, D), F32)] * 3,
        compiler_params=params(56),
        name="adam",
    )(*[value for pair in pairs for value in pair], weight, one, two)


def rotary_tables():
    positions = jnp.arange(SEQ).astype(F32)
    exponents = jnp.arange(HALF).astype(F32) * (2.0 / HD)
    frequency = THETA ** (-exponents)
    angles = frequency[:, None] * positions[None, :]
    return jnp.cos(angles), jnp.sin(angles)


def ring_gather(shard, up_again):
    below = send(shard, ALONG_Y[1])
    above = send(shard, ALONG_Y[3])
    far = send(below, ALONG_Y[1]) if up_again else send(above, ALONG_Y[3])
    return [shard, above, far, below]


def both_cores(pieces):
    return pieces + [send(piece, TO_CORE) for piece in pieces]


def per_device(tokens, student_weight, snapshot, moment_one, moment_two):
    own = tokens[0]
    master = student_weight[0]
    table = jnp.asarray(TABLE)[lax.axis_index("fsdp")]
    angles = rotary_tables()

    teacher = lax.ppermute(snapshot[0], "blk", [(g, (g + 1) % 8) for g in range(8)])
    plane = send(own, TO_PLANE)
    student_rows = both_cores(ring_gather(master.astype(BF), True))
    teacher_own = ring_gather(teacher, False)

    own_two, plane_two = [(own, 0), (own, 1)], [(plane, 0), (plane, 1)]
    two = [(0, 0), (1, 0)]
    *own_s, given = project(table, angles, own_two, [student_rows], two, [[0, 1]])
    teacher_own[2], teacher_own[3], given = lax.optimization_barrier(
        (teacher_own[2], teacher_own[3], given)
    )
    teacher_rows = both_cores(teacher_own)
    *own_t, given = project(table, angles, own_two, [teacher_rows], two, [[-1, -1, 0, 1]], given)
    got_own = send(given, TO_PLANE)
    plane_after, _ = lax.optimization_barrier((plane, own_t[0]))
    plane_two = [(plane_after, 0), (plane_after, 1)]
    *made, given_s, given_t = project(
        table,
        angles,
        plane_two,
        [student_rows, teacher_rows],
        two + [(0, 1), (1, 1)],
        [[0, 1], [2, 3]],
    )
    plane_s, plane_t = made[:2], made[2:]
    got_s, got_t = send(given_s, TO_PLANE), send(given_t, TO_PLANE)

    second = attend(
        table,
        angles,
        [[(plane_s[n], (got_own, n)), (plane_t[n], (got_own, 2 + n))] for n in range(2)],
    )
    got_s, got_t, _ = lax.optimization_barrier((got_s, got_t, second[2]))
    first = [attend(table, angles, [[(own_s[0], (got_s, 0)), (own_t[0], (got_t, 0))]])]
    back_first = [send(second[2], TO_PLANE), send(second[3], TO_PLANE)]
    got_s, got_t, *back_first, carried = lax.optimization_barrier(
        (got_s, got_t, *back_first, first[0][2])
    )
    back_first[1] = send(back_first[1], TO_CORE)
    first.append(
        attend(
            table,
            angles,
            [[(own_s[1], (got_s, 1)), (own_t[1], (got_t, 1))]],
            (carried, first[0][3]),
        )
    )
    back_second = [send(first[1][2], TO_PLANE), send(first[1][3], TO_BOTH)]
    (before,) = weight_call(
        first_kernel,
        table,
        [part[0] for part in first] + [send(part[1], TO_CORE) for part in first],
        back_first,
        [own, send(own, TO_CORE)],
        [],
        [(CORE, F32)],
        6.0,
    )

    def weight_blocks(parts):
        return weight_call(
            lambda *refs: second_kernel(parts, *refs),
            table,
            [second[0], send(second[1], TO_CORE)],
            back_second,
            [plane_after, send(plane_after, TO_CORE)],
            [(before, part_index(step, first)) for step, first, _ in parts],
            [(PART, dtype) for _, _, dtype in parts],
            5.0,
        )

    up, down = ALONG_Y[1], ALONG_Y[3]
    far_low, far_high, next_high, last_low = weight_blocks(
        ((2, 0, BF), (2, PART, BF), (1, PART, BF), (3, 0, BF))
    )
    far_low, far_high = send(far_low, up), send(far_high, down)
    from_below, from_above = [None, send(next_high, up)], [send(last_low, down), None]
    next_low, last_high, *own_parts = weight_blocks(
        ((1, 0, F32), (3, PART, F32), (0, 0, F32), (0, PART, F32))
    )
    next_low, last_high = add(next_low, far_low, last_high, far_high)
    from_below[0], from_above[1] = send(next_low, up), send(last_high, down)
    pairs = [own_parts, from_below, from_above]
    updated = adam(pairs, master, moment_one[0], moment_two[0])
    return tuple(value[None] for value in updated)


def solution(mesh):
    spec = P("blk", "fsdp", None)
    return jax.shard_map(
        per_device,
        mesh=mesh,
        in_specs=(spec,) * 5,
        out_specs=(spec,) * 3,
        check_vma=False,
    )
```

```python
import math

import jax
import jax.numpy as jnp
import numpy as np
from jax import lax
from jax.experimental import pallas as pl
from jax.experimental.pallas import tpu as pltpu
from jax.sharding import PartitionSpec as P

HEADS = 16
KVH = 4
HD = 128
SEQ = 256
STEP = 100
D = 2048
THETA = 500000.0
BETA_ONE = 0.9
BETA_TWO = 0.95
LEARN_RATE = 0.002
DECAY = 0.1
EPSILON = 1e-08
MASKED = -1e30

BF = jnp.bfloat16
F32 = jnp.float32
SHARD = 160
ROWS = 8 * SHARD
UNIT = 32
PART = SHARD // 2
HALF = HD // 2
CORE = 4 * SHARD
EXCHANGED = 2 * HD
INV_ROOT = 1.0 / math.sqrt(HD)

AT_WEIGHT, AT_GIVEN, AT_QUERY, AT_KEY, AT_CORE, AT_STEP, AT_FILL, AT_BACK = 0, 8, 9, 17, 19, 27, 31, 36
GIVEN = (1024, 768)
QUERY = (tuple(range(8)), (10, 11, 0, 1, 2, 3, 4, 5))
KEY = ((10, 11), (8, 9))


def given_units(plane, core):
    rows = [GIVEN[plane] + UNIT * unit for unit in range(8)]
    return [(u, r // 320 * 160 + r % 160) for u, r in enumerate(rows) if r % 320 // 160 == core]


def build_table():
    table = np.zeros((16, 46), np.int32)
    for d in range(16):
        z, y, c = d // 8, d % 8 // 2, d % 2
        gathered = [320 * ((y + s) % 4) + 160 * (c ^ r) for r in range(2) for s in range(4)]
        cores = [320 * k + 160 * (c ^ r) for r in range(2) for k in range(4)]
        steps = [160 * ((y + s) % 4) for s in range(4)]
        fill = ([row for _, row in given_units(z, c)] + [-1] * 5)[:5]
        back = []
        for r in range(2):
            back += ([unit for unit, _ in given_units(1 - z, c ^ r)] + [0] * 5)[:5]
        table[d] = gathered + [GIVEN[z], *QUERY[z], *KEY[z]] + cores + steps + fill + back
    return table


TABLE = build_table()


def pairs_of(function):
    out = []
    for d in range(16):
        z, y, c = function(d // 8, d % 8 // 2, d % 2)
        out.append((d, z % 2 * 8 + y % 4 * 2 + c % 2))
    return out


TO_CORE = pairs_of(lambda z, y, c: (z, y, c + 1))
TO_PLANE = pairs_of(lambda z, y, c: (z + 1, y, c))
TO_BOTH = pairs_of(lambda z, y, c: (z + 1, y, c + 1))
ALONG_Y = [pairs_of(lambda z, y, c, s=s: (z, y + s, c)) for s in range(4)]


def send(value, pairs):
    return lax.ppermute(value, "fsdp", pairs)


def params(mib):
    return pltpu.CompilerParams(vmem_limit_bytes=mib * 2**20)


def cost(microseconds):
    return pl.CostEstimate(flops=int(microseconds * 1e9), bytes_accessed=2**20, transcendentals=0)


def dot(a, b, dims=((1,), (0,))):
    return lax.dot_general(a, b, (dims, ((), ())), preferred_element_type=F32)


def rotated(raw, cosine, sine):
    front, back = raw[:HALF], raw[HALF:]
    return jnp.concatenate([front * cosine - back * sine, back * cosine + front * sine], axis=0)


def split(refs, counts):
    out, refs = [], list(refs)
    for count in counts:
        out.append(refs[:count])
        refs = refs[count:]
    return out + [refs]


ANY = pl.BlockSpec(memory_space=pl.ANY)


def block(shape, row=0, column=0):
    return pl.BlockSpec(shape, lambda s, table: (row, column))


def call(kernel, name, operands, outs, scratch, microseconds, mib=32):
    return pl.pallas_call(
        kernel,
        grid_spec=pltpu.PrefetchScalarGridSpec(
            num_scalar_prefetch=1,
            grid=(1,),
            in_specs=[spec for _, spec in operands[1:]],
            out_specs=[spec[0] if spec else block(shape) for shape, _, *spec in outs],
            scratch_shapes=scratch,
        ),
        out_shape=[jax.ShapeDtypeStruct(shape, dtype) for shape, dtype, *_ in outs],
        compiler_params=params(mib),
        cost_estimate=cost(microseconds),
        name=name,
    )(*[value for value, _ in operands])


def project_kernel(jobs, groups, x_count, set_count, table, *refs):
    refs = list(refs)
    carried, refs = refs[0], refs[1:]
    xs, refs = refs[:x_count], refs[x_count:]
    cosine, sine, refs = refs[0], refs[1], refs[2:]
    arrays, refs = refs[: 8 * set_count], refs[8 * set_count :]
    outs, refs = refs[: len(jobs)], refs[len(jobs) :]
    givens, refs = refs[: len(groups)], refs[len(groups) :]
    held, sems = refs[:-1], refs[-1]

    def copy(at, n):
        rows = pl.ds(pl.multiple_of(table[AT_WEIGHT + n], SHARD), SHARD)
        return pltpu.make_async_copy(arrays[8 * at + n], held[at].at[rows], sems.at[8 * at + n])

    for at in range(set_count):
        for n in range(8):
            copy(at, n).start()
    for at in range(set_count):
        for n in range(8):
            copy(at, n).wait()
        for job, (x, own_set) in enumerate(jobs):
            if own_set != at:
                continue
            for half in range(2):
                part = dot(held[at][half * CORE : (half + 1) * CORE, :], xs[x][...], ((1,), (1,)))
                for h in range(5):
                    row = half * CORE + h * HD
                    value = rotated(part[h * HD : (h + 1) * HD], cosine[...], sine[...])
                    outs[job][row : row + HD, :] = value.astype(BF)
    rows = pl.ds(pl.multiple_of(table[AT_GIVEN], EXCHANGED), EXCHANGED)
    for given, group in zip(givens, groups):
        for n, job in enumerate(group):
            lanes = slice(n * SEQ, (n + 1) * SEQ)
            given[:, lanes] = outs[job][rows, :] if job >= 0 else carried[:, lanes]


def project(table, angles, xs, sets, jobs, groups, carried=None):
    carried = angles[0] if carried is None else carried
    operands = [(table, None), (carried, block(carried.shape))]
    operands += [(x, block((SEQ, D), at)) for x, at in xs]
    operands += [(value, block((HALF, SEQ))) for value in angles]
    operands += [(array, ANY) for arrays in sets for array in arrays]
    return call(
        lambda *refs: project_kernel(jobs, groups, len(xs), len(sets), *refs),
        "project",
        operands,
        [((ROWS, SEQ), BF)] * len(jobs) + [((EXCHANGED, SEQ * len(group)), BF) for group in groups],
        [pltpu.VMEM((ROWS, D), BF)] * len(sets) + [pltpu.SemaphoreType.DMA((8 * len(sets),))],
        0.5 if len(sets) == 1 else 8.0,
    )


SCALE = INV_ROOT * math.log2(math.e)
SPAN = 2 * SEQ


def softmax_parts(scores, causal):
    scores = jnp.where(causal, scores * SCALE, MASKED)
    power = jnp.exp2(scores - jnp.max(scores, axis=0, keepdims=True))
    return power, (1.0 / HEADS) / jnp.sum(power, axis=0, keepdims=True)


def attention_gradient(student, teacher, cosine, sine):
    lane = lax.broadcasted_iota(jnp.int32, (SEQ, 4 * SEQ), 1) % SEQ
    causal = lax.broadcasted_iota(jnp.int32, (SEQ, 4 * SEQ), 0) <= lane
    queries = jnp.concatenate(student[:4], axis=1)
    power_s, inverse_s = softmax_parts(dot(student[4].T, queries), causal)
    others = jnp.concatenate(teacher[:4], axis=1)
    power_t, inverse_t = softmax_parts(dot(teacher[4].T, others), causal)
    spread = (power_s * inverse_s - power_t * inverse_t).astype(BF)
    query_grads = dot(student[4], spread)
    grads = [query_grads[:, h * SEQ : (h + 1) * SEQ] for h in range(4)]
    grads.append(dot(queries, spread, ((1,), (1,))))
    return [rotated(g * INV_ROOT, cosine, -sine).astype(BF) for g in grads]


def attend_kernel(count, carry_count, table, *refs):
    carried, refs = refs[:carry_count], refs[carry_count:]
    inputs, (cosine, sine, out, other, back, back_other, both_s, both_t, grads) = refs[: 4 * count], refs[4 * count :]
    for seq in range(count):
        own_s, got_s, own_t, got_t = inputs[4 * seq : 4 * seq + 4]
        lanes = slice(seq * SEQ, (seq + 1) * SEQ)
        for both, own, got in ((both_s, own_s, got_s), (both_t, own_t, got_t)):
            both[:ROWS, lanes] = own[...]
            both[ROWS:, lanes] = got[...]
    for seq in range(count):
        lanes = slice(seq * SEQ, (seq + 1) * SEQ)
        for kv in range(2):
            blocks = [table[AT_QUERY + 4 * kv + h] for h in range(4)] + [table[AT_KEY + kv]]
            rows = [pl.ds(pl.multiple_of(n * HD, HD), HD) for n in blocks]
            student = [both_s[at, lanes] for at in rows]
            teacher = [both_t[at, lanes] for at in rows]
            made = attention_gradient(student, teacher, cosine[...], sine[...])
            for at, value in zip(rows, made):
                grads[at, lanes] = value
    for n in range(8):
        row = pl.multiple_of(table[AT_CORE + n], SHARD)
        target = out if n < 4 else other
        target[n % 4 * SHARD : (n % 4 + 1) * SHARD, :] = grads[pl.ds(row, SHARD), :]
    for n in range(10):
        row = pl.multiple_of(ROWS + table[AT_BACK + n] * UNIT, UNIT)
        target = back if n < 5 else back_other
        unit = slice(n % 5 * UNIT, (n % 5 + 1) * UNIT)
        target[unit, target.shape[1] - count * SEQ :] = grads[pl.ds(row, UNIT), :]
    for value, target in zip(carried, (back, back_other)):
        target[:, : value.shape[1]] = value[...]


def attend(table, angles, sequences, carried=()):
    count = len(sequences)
    operands = [(table, None)] + [(value, block(value.shape)) for value in carried]
    wide = count * SEQ + (carried[0].shape[1] if carried else 0)
    for sequence in sequences:
        for own, (got, at) in sequence:
            operands += [(own, block((ROWS, SEQ))), (got, block((EXCHANGED, SEQ), 0, at))]
    operands += [(value, block((HALF, SEQ))) for value in angles]
    return call(
        lambda *refs: attend_kernel(count, len(carried), *refs),
        "attend",
        operands,
        [((CORE, count * SEQ), BF)] * 2 + [((SHARD, wide), BF)] * 2,
        [pltpu.VMEM((ROWS + EXCHANGED, count * SEQ), BF)] * 3,
        1.0 + 3.5 * count,
        32,
    )


TILE = 1024


def fill(table, held, grads, backs):
    first = 0
    for grad in grads:
        held[:, first : first + grad.shape[1]] = grad[...]
        first += grad.shape[1]
    for unit in range(5):
        row = table[AT_FILL + unit]

        @pl.when(row >= 0)
        def _():
            at, first = pl.ds(pl.multiple_of(row, UNIT), UNIT), 0
            for back in backs:
                lanes = slice(first, first + back.shape[1])
                held[at, lanes] = back[unit * UNIT : (unit + 1) * UNIT, :]
                first = lanes.stop


def first_kernel(counts, table, *refs):
    grads, backs, tokens, (out, held) = split(refs, counts)

    @pl.when(pl.program_id(0) == 0)
    def _():
        fill(table, held, grads, backs)

    out[...] = dot(held[:, :SPAN], tokens[0][...]) + dot(held[:, SPAN:], tokens[1][...])


def second_kernel(parts, counts, table, *refs):
    grads, backs, tokens, befores, rest = split(refs, (*counts, len(parts)))
    outs, held = rest[:-1], rest[-1]

    @pl.when(pl.program_id(0) == 0)
    def _():
        fill(table, held, grads, backs)

    for (step, first, _), before, out in zip(parts, befores, outs):
        rows = pl.ds(pl.multiple_of(table[AT_STEP + step] + first, 16), PART)
        total = before[...] + dot(held[rows, :SPAN], tokens[0][...])
        total += dot(held[rows, SPAN:], tokens[1][...])
        out[...] = total.astype(out.dtype)


def weight_call(kernel, table, grads, backs, tokens, more, outs, microseconds):
    tile = lambda t, table: (0, t)
    return pl.pallas_call(
        lambda *refs: kernel((len(grads), len(backs), len(tokens)), *refs),
        grid_spec=pltpu.PrefetchScalarGridSpec(
            num_scalar_prefetch=1,
            grid=(D // TILE,),
            in_specs=[block(value.shape) for value in grads + backs]
            + [pl.BlockSpec((x.shape[0], TILE), tile) for x in tokens]
            + [pl.BlockSpec((PART, TILE), index) for _, index in more],
            out_specs=[pl.BlockSpec((rows, TILE), tile) for rows, _ in outs],
            scratch_shapes=[pltpu.VMEM((CORE, 2 * SPAN), BF)],
        ),
        out_shape=[jax.ShapeDtypeStruct((rows, D), dtype) for rows, dtype in outs],
        compiler_params=params(32),
        cost_estimate=cost(microseconds),
        name="weight_gradient",
    )(table, *grads, *backs, *tokens, *[value for value, _ in more])


def part_index(step, first):
    return lambda t, table: (table[AT_STEP + step] // PART + first // PART, t)


def adam_kernel(a, b, c, weight, one, two, weight_out, one_out, two_out):
    gradient = a[...].astype(F32) + (b[...].astype(F32) + c[...].astype(F32))
    first_new = BETA_ONE * one[...] + (1.0 - BETA_ONE) * gradient
    second_new = BETA_TWO * two[...] + (1.0 - BETA_TWO) * gradient * gradient
    step_dir = (
        first_new
        / (1.0 - BETA_ONE**STEP)
        / (jnp.sqrt(second_new / (1.0 - BETA_TWO**STEP)) + EPSILON)
    )
    master = weight[...]
    weight_out[...] = master - LEARN_RATE * (step_dir + DECAY * master)
    one_out[...] = first_new
    two_out[...] = second_new


def adam_body(*refs):
    pairs, rest = refs[:6], refs[6:]
    for at in range(2):

        @pl.when(pl.program_id(0) == at)
        def _():
            adam_kernel(*pairs[at::2], *rest)


def add_kernel(a, b, c, d, low, high):
    low[...] = (a[...] + b[...].astype(F32)).astype(BF)
    high[...] = (c[...] + d[...].astype(F32)).astype(BF)


def add(*values):
    whole = pl.BlockSpec((PART, D), lambda: (0, 0))
    return pl.pallas_call(
        add_kernel,
        in_specs=[whole] * 4,
        out_specs=[whole] * 2,
        out_shape=[jax.ShapeDtypeStruct((PART, D), BF)] * 2,
        compiler_params=params(32),
        cost_estimate=cost(0.5),
        name="add",
    )(*values)


def adam(pairs, weight, one, two):
    straight = pl.BlockSpec((PART, D), lambda k: (k, 0))
    whole = pl.BlockSpec((PART, D), lambda k: (0, 0))
    return pl.pallas_call(
        adam_body,
        grid=(2,),
        in_specs=[whole] * 6 + [straight] * 3,
        out_specs=[straight] * 3,
        out_shape=[jax.ShapeDtypeStruct((SHARD, D), F32)] * 3,
        compiler_params=params(32),
        name="adam",
    )(*[value for pair in pairs for value in pair], weight, one, two)


def rotary_tables():
    positions = jnp.arange(SEQ).astype(F32)
    exponents = jnp.arange(HALF).astype(F32) * (2.0 / HD)
    frequency = THETA ** (-exponents)
    angles = frequency[:, None] * positions[None, :]
    return jnp.cos(angles), jnp.sin(angles)


def ring_gather(shard, up_again):
    below = send(shard, ALONG_Y[1])
    above = send(shard, ALONG_Y[3])
    far = send(below, ALONG_Y[1]) if up_again else send(above, ALONG_Y[3])
    return [shard, above, far, below]


def both_cores(pieces):
    return pieces + [send(piece, TO_CORE) for piece in pieces]


def per_device(tokens, student_weight, snapshot, moment_one, moment_two):
    own = tokens[0]
    master = student_weight[0]
    table = jnp.asarray(TABLE)[lax.axis_index("fsdp")]
    angles = rotary_tables()

    teacher = lax.ppermute(snapshot[0], "blk", [(g, (g + 1) % 8) for g in range(8)])
    plane = send(own, TO_PLANE)
    student_rows = both_cores(ring_gather(master.astype(BF), True))
    teacher_own = ring_gather(teacher, False)

    own_two, plane_two = [(own, 0), (own, 1)], [(plane, 0), (plane, 1)]
    two = [(0, 0), (1, 0)]
    *own_s, given = project(table, angles, own_two, [student_rows], two, [[0, 1]])
    teacher_own[2], teacher_own[3], given = lax.optimization_barrier(
        (teacher_own[2], teacher_own[3], given)
    )
    teacher_rows = both_cores(teacher_own)
    *own_t, given = project(table, angles, own_two, [teacher_rows], two, [[-1, -1, 0, 1]], given)
    got_own = send(given, TO_PLANE)
    plane_after, _ = lax.optimization_barrier((plane, own_t[0]))
    plane_two = [(plane_after, 0), (plane_after, 1)]
    *made, given_s, given_t = project(
        table,
        angles,
        plane_two,
        [student_rows, teacher_rows],
        two + [(0, 1), (1, 1)],
        [[0, 1], [2, 3]],
    )
    plane_s, plane_t = made[:2], made[2:]
    got_s, got_t = send(given_s, TO_PLANE), send(given_t, TO_PLANE)

    second = attend(
        table,
        angles,
        [[(plane_s[n], (got_own, n)), (plane_t[n], (got_own, 2 + n))] for n in range(2)],
    )
    got_s, got_t, _ = lax.optimization_barrier((got_s, got_t, second[2]))
    first = [attend(table, angles, [[(own_s[0], (got_s, 0)), (own_t[0], (got_t, 0))]])]
    back_first = [send(second[2], TO_PLANE), send(second[3], TO_PLANE)]
    got_s, got_t, *back_first, carried = lax.optimization_barrier(
        (got_s, got_t, *back_first, first[0][2])
    )
    back_first[1] = send(back_first[1], TO_CORE)
    first.append(
        attend(
            table,
            angles,
            [[(own_s[1], (got_s, 1)), (own_t[1], (got_t, 1))]],
            (carried, first[0][3]),
        )
    )
    back_second = [send(first[1][2], TO_PLANE), send(first[1][3], TO_BOTH)]
    (before,) = weight_call(
        first_kernel,
        table,
        [part[0] for part in first] + [send(part[1], TO_CORE) for part in first],
        back_first,
        [own, send(own, TO_CORE)],
        [],
        [(CORE, F32)],
        6.0,
    )

    def weight_blocks(parts):
        return weight_call(
            lambda *refs: second_kernel(parts, *refs),
            table,
            [second[0], send(second[1], TO_CORE)],
            back_second,
            [plane_after, send(plane_after, TO_CORE)],
            [(before, part_index(step, first)) for step, first, _ in parts],
            [(PART, dtype) for _, _, dtype in parts],
            5.0,
        )

    up, down = ALONG_Y[1], ALONG_Y[3]
    far_low, far_high, next_high, last_low = weight_blocks(
        ((2, 0, BF), (2, PART, BF), (1, PART, BF), (3, 0, BF))
    )
    far_low, far_high = send(far_low, up), send(far_high, down)
    from_below, from_above = [None, send(next_high, up)], [send(last_low, down), None]
    next_low, last_high, *own_parts = weight_blocks(
        ((1, 0, F32), (3, PART, F32), (0, 0, F32), (0, PART, F32))
    )
    next_low, last_high = add(next_low, far_low, last_high, far_high)
    from_below[0], from_above[1] = send(next_low, up), send(last_high, down)
    pairs = [own_parts, from_below, from_above]
    updated = adam(pairs, master, moment_one[0], moment_two[0])
    return tuple(value[None] for value in updated)


def solution(mesh):
    spec = P("blk", "fsdp", None)
    return jax.shard_map(
        per_device,
        mesh=mesh,
        in_specs=(spec,) * 5,
        out_specs=(spec,) * 3,
        check_vma=False,
    )
```

```python
import math

import jax
import jax.numpy as jnp
import numpy as np
from jax import lax
from jax.experimental import pallas as pl
from jax.experimental.pallas import tpu as pltpu
from jax.sharding import PartitionSpec as P

HEADS = 16
KVH = 4
HD = 128
SEQ = 256
STEP = 100
D = 2048
THETA = 500000.0
BETA_ONE = 0.9
BETA_TWO = 0.95
LEARN_RATE = 0.002
DECAY = 0.1
EPSILON = 1e-08
MASKED = -1e30

BF = jnp.bfloat16
F32 = jnp.float32
SHARD = 160
ROWS = 8 * SHARD
UNIT = 32
PART = SHARD // 2
HALF = HD // 2
CORE = 4 * SHARD
EXCHANGED = 2 * HD
INV_ROOT = 1.0 / math.sqrt(HD)

AT_WEIGHT, AT_GIVEN, AT_QUERY, AT_KEY, AT_CORE, AT_STEP, AT_FILL, AT_BACK = 0, 8, 9, 17, 19, 27, 31, 36
GIVEN = (1024, 768)
QUERY = (tuple(range(8)), (10, 11, 0, 1, 2, 3, 4, 5))
KEY = ((10, 11), (8, 9))


def given_units(plane, core):
    rows = [GIVEN[plane] + UNIT * unit for unit in range(8)]
    return [(u, r // 320 * 160 + r % 160) for u, r in enumerate(rows) if r % 320 // 160 == core]


def build_table():
    table = np.zeros((16, 46), np.int32)
    for d in range(16):
        z, y, c = d // 8, d % 8 // 2, d % 2
        gathered = [320 * ((y + s) % 4) + 160 * (c ^ r) for r in range(2) for s in range(4)]
        cores = [320 * k + 160 * (c ^ r) for r in range(2) for k in range(4)]
        steps = [160 * ((y + s) % 4) for s in range(4)]
        fill = ([row for _, row in given_units(z, c)] + [-1] * 5)[:5]
        back = []
        for r in range(2):
            back += ([unit for unit, _ in given_units(1 - z, c ^ r)] + [0] * 5)[:5]
        table[d] = gathered + [GIVEN[z], *QUERY[z], *KEY[z]] + cores + steps + fill + back
    return table


TABLE = build_table()


def pairs_of(function):
    out = []
    for d in range(16):
        z, y, c = function(d // 8, d % 8 // 2, d % 2)
        out.append((d, z % 2 * 8 + y % 4 * 2 + c % 2))
    return out


TO_CORE = pairs_of(lambda z, y, c: (z, y, c + 1))
TO_PLANE = pairs_of(lambda z, y, c: (z + 1, y, c))
TO_BOTH = pairs_of(lambda z, y, c: (z + 1, y, c + 1))
ALONG_Y = [pairs_of(lambda z, y, c, s=s: (z, y + s, c)) for s in range(4)]


def send(value, pairs):
    return lax.ppermute(value, "fsdp", pairs)


def params(mib):
    return pltpu.CompilerParams(vmem_limit_bytes=mib * 2**20)


def cost(microseconds):
    return pl.CostEstimate(flops=int(microseconds * 1e9), bytes_accessed=2**20, transcendentals=0)


def dot(a, b, dims=((1,), (0,))):
    return lax.dot_general(a, b, (dims, ((), ())), preferred_element_type=F32)


def rotated(raw, cosine, sine):
    front, back = raw[:HALF], raw[HALF:]
    return jnp.concatenate([front * cosine - back * sine, back * cosine + front * sine], axis=0)


def split(refs, counts):
    out, refs = [], list(refs)
    for count in counts:
        out.append(refs[:count])
        refs = refs[count:]
    return out + [refs]


ANY = pl.BlockSpec(memory_space=pl.ANY)


def block(shape, row=0, column=0):
    return pl.BlockSpec(shape, lambda s, table: (row, column))


def call(kernel, name, operands, outs, scratch, microseconds, mib=32):
    return pl.pallas_call(
        kernel,
        grid_spec=pltpu.PrefetchScalarGridSpec(
            num_scalar_prefetch=1,
            grid=(1,),
            in_specs=[spec for _, spec in operands[1:]],
            out_specs=[spec[0] if spec else block(shape) for shape, _, *spec in outs],
            scratch_shapes=scratch,
        ),
        out_shape=[jax.ShapeDtypeStruct(shape, dtype) for shape, dtype, *_ in outs],
        compiler_params=params(mib),
        cost_estimate=cost(microseconds),
        name=name,
    )(*[value for value, _ in operands])


def project_kernel(jobs, groups, x_count, set_count, table, *refs):
    refs = list(refs)
    carried, refs = refs[0], refs[1:]
    xs, refs = refs[:x_count], refs[x_count:]
    cosine, sine, refs = refs[0], refs[1], refs[2:]
    arrays, refs = refs[: 8 * set_count], refs[8 * set_count :]
    outs, refs = refs[: len(jobs)], refs[len(jobs) :]
    givens, refs = refs[: len(groups)], refs[len(groups) :]
    held, sems = refs[:-1], refs[-1]

    def copy(at, n):
        rows = pl.ds(pl.multiple_of(table[AT_WEIGHT + n], SHARD), SHARD)
        return pltpu.make_async_copy(arrays[8 * at + n], held[at].at[rows], sems.at[8 * at + n])

    for at in range(set_count):
        for n in range(8):
            copy(at, n).start()
    for at in range(set_count):
        for n in range(8):
            copy(at, n).wait()
        for job, (x, own_set) in enumerate(jobs):
            if own_set != at:
                continue
            for half in range(2):
                part = dot(held[at][half * CORE : (half + 1) * CORE, :], xs[x][...], ((1,), (1,)))
                for h in range(5):
                    row = half * CORE + h * HD
                    value = rotated(part[h * HD : (h + 1) * HD], cosine[...], sine[...])
                    outs[job][row : row + HD, :] = value.astype(BF)
    rows = pl.ds(pl.multiple_of(table[AT_GIVEN], EXCHANGED), EXCHANGED)
    for given, group in zip(givens, groups):
        for n, job in enumerate(group):
            lanes = slice(n * SEQ, (n + 1) * SEQ)
            given[:, lanes] = outs[job][rows, :] if job >= 0 else carried[:, lanes]


def project(table, angles, xs, sets, jobs, groups, carried=None):
    carried = angles[0] if carried is None else carried
    operands = [(table, None), (carried, block(carried.shape))]
    operands += [(x, block((SEQ, D), at)) for x, at in xs]
    operands += [(value, block((HALF, SEQ))) for value in angles]
    operands += [(array, ANY) for arrays in sets for array in arrays]
    return call(
        lambda *refs: project_kernel(jobs, groups, len(xs), len(sets), *refs),
        "project",
        operands,
        [((ROWS, SEQ), BF)] * len(jobs) + [((EXCHANGED, SEQ * len(group)), BF) for group in groups],
        [pltpu.VMEM((ROWS, D), BF)] * len(sets) + [pltpu.SemaphoreType.DMA((8 * len(sets),))],
        0.5 if len(sets) == 1 else 8.0,
    )


SCALE = INV_ROOT * math.log2(math.e)
SPAN = 2 * SEQ


def softmax_parts(scores, causal):
    scores = jnp.where(causal, scores * SCALE, MASKED)
    power = jnp.exp2(scores - jnp.max(scores, axis=0, keepdims=True))
    return power, (1.0 / HEADS) / jnp.sum(power, axis=0, keepdims=True)


def attention_gradient(student, teacher, cosine, sine):
    lane = lax.broadcasted_iota(jnp.int32, (SEQ, 4 * SEQ), 1) % SEQ
    causal = lax.broadcasted_iota(jnp.int32, (SEQ, 4 * SEQ), 0) <= lane
    queries = jnp.concatenate(student[:4], axis=1)
    power_s, inverse_s = softmax_parts(dot(student[4].T, queries), causal)
    others = jnp.concatenate(teacher[:4], axis=1)
    power_t, inverse_t = softmax_parts(dot(teacher[4].T, others), causal)
    spread = (power_s * inverse_s - power_t * inverse_t).astype(BF)
    query_grads = dot(student[4], spread)
    grads = [query_grads[:, h * SEQ : (h + 1) * SEQ] for h in range(4)]
    grads.append(dot(queries, spread, ((1,), (1,))))
    return [rotated(g * INV_ROOT, cosine, -sine).astype(BF) for g in grads]


def attend_kernel(count, carry_count, table, *refs):
    carried, refs = refs[:carry_count], refs[carry_count:]
    inputs, (cosine, sine, out, other, back, back_other, both_s, both_t, grads) = refs[: 4 * count], refs[4 * count :]
    for seq in range(count):
        own_s, got_s, own_t, got_t = inputs[4 * seq : 4 * seq + 4]
        lanes = slice(seq * SEQ, (seq + 1) * SEQ)
        for both, own, got in ((both_s, own_s, got_s), (both_t, own_t, got_t)):
            both[:ROWS, lanes] = own[...]
            both[ROWS:, lanes] = got[...]
    for seq in range(count):
        lanes = slice(seq * SEQ, (seq + 1) * SEQ)
        for kv in range(2):
            blocks = [table[AT_QUERY + 4 * kv + h] for h in range(4)] + [table[AT_KEY + kv]]
            rows = [pl.ds(pl.multiple_of(n * HD, HD), HD) for n in blocks]
            student = [both_s[at, lanes] for at in rows]
            teacher = [both_t[at, lanes] for at in rows]
            made = attention_gradient(student, teacher, cosine[...], sine[...])
            for at, value in zip(rows, made):
                grads[at, lanes] = value
    for n in range(8):
        row = pl.multiple_of(table[AT_CORE + n], SHARD)
        target = out if n < 4 else other
        target[n % 4 * SHARD : (n % 4 + 1) * SHARD, :] = grads[pl.ds(row, SHARD), :]
    for n in range(10):
        row = pl.multiple_of(ROWS + table[AT_BACK + n] * UNIT, UNIT)
        target = back if n < 5 else back_other
        unit = slice(n % 5 * UNIT, (n % 5 + 1) * UNIT)
        target[unit, target.shape[1] - count * SEQ :] = grads[pl.ds(row, UNIT), :]
    for value, target in zip(carried, (back, back_other)):
        target[:, : value.shape[1]] = value[...]


def attend(table, angles, sequences, carried=()):
    count = len(sequences)
    operands = [(table, None)] + [(value, block(value.shape)) for value in carried]
    wide = count * SEQ + (carried[0].shape[1] if carried else 0)
    for sequence in sequences:
        for own, (got, at) in sequence:
            operands += [(own, block((ROWS, SEQ))), (got, block((EXCHANGED, SEQ), 0, at))]
    operands += [(value, block((HALF, SEQ))) for value in angles]
    return call(
        lambda *refs: attend_kernel(count, len(carried), *refs),
        "attend",
        operands,
        [((CORE, count * SEQ), BF)] * 2 + [((SHARD, wide), BF)] * 2,
        [pltpu.VMEM((ROWS + EXCHANGED, count * SEQ), BF)] * 3,
        1.0 + 3.5 * count,
        32,
    )


TILE = 1024


def fill(table, held, grads, backs):
    first = 0
    for grad in grads:
        held[:, first : first + grad.shape[1]] = grad[...]
        first += grad.shape[1]
    for unit in range(5):
        row = table[AT_FILL + unit]

        @pl.when(row >= 0)
        def _():
            at, first = pl.ds(pl.multiple_of(row, UNIT), UNIT), 0
            for back in backs:
                lanes = slice(first, first + back.shape[1])
                held[at, lanes] = back[unit * UNIT : (unit + 1) * UNIT, :]
                first = lanes.stop


def first_kernel(counts, table, *refs):
    grads, backs, tokens, (out, held) = split(refs, counts)

    @pl.when(pl.program_id(0) == 0)
    def _():
        fill(table, held, grads, backs)

    out[...] = dot(held[:, :SPAN], tokens[0][...]) + dot(held[:, SPAN:], tokens[1][...])


def second_kernel(parts, counts, table, *refs):
    grads, backs, tokens, befores, rest = split(refs, (*counts, len(parts)))
    outs, held = rest[:-1], rest[-1]

    @pl.when(pl.program_id(0) == 0)
    def _():
        fill(table, held, grads, backs)

    for (step, first, _), before, out in zip(parts, befores, outs):
        rows = pl.ds(pl.multiple_of(table[AT_STEP + step] + first, 16), PART)
        total = before[...] + dot(held[rows, :SPAN], tokens[0][...])
        total += dot(held[rows, SPAN:], tokens[1][...])
        out[...] = total.astype(out.dtype)


def weight_call(kernel, table, grads, backs, tokens, more, outs, microseconds):
    tile = lambda t, table: (0, t)
    return pl.pallas_call(
        lambda *refs: kernel((len(grads), len(backs), len(tokens)), *refs),
        grid_spec=pltpu.PrefetchScalarGridSpec(
            num_scalar_prefetch=1,
            grid=(D // TILE,),
            in_specs=[block(value.shape) for value in grads + backs]
            + [pl.BlockSpec((x.shape[0], TILE), tile) for x in tokens]
            + [pl.BlockSpec((PART, TILE), index) for _, index in more],
            out_specs=[pl.BlockSpec((rows, TILE), tile) for rows, _ in outs],
            scratch_shapes=[pltpu.VMEM((CORE, 2 * SPAN), BF)],
        ),
        out_shape=[jax.ShapeDtypeStruct((rows, D), dtype) for rows, dtype in outs],
        compiler_params=params(32),
        cost_estimate=cost(microseconds),
        name="weight_gradient",
    )(table, *grads, *backs, *tokens, *[value for value, _ in more])


def part_index(step, first):
    return lambda t, table: (table[AT_STEP + step] // PART + first // PART, t)


def adam_kernel(a, b, c, weight, one, two, weight_out, one_out, two_out):
    gradient = a[...].astype(F32) + (b[...].astype(F32) + c[...].astype(F32))
    first_new = BETA_ONE * one[...] + (1.0 - BETA_ONE) * gradient
    second_new = BETA_TWO * two[...] + (1.0 - BETA_TWO) * gradient * gradient
    step_dir = (
        first_new
        / (1.0 - BETA_ONE**STEP)
        / (jnp.sqrt(second_new / (1.0 - BETA_TWO**STEP)) + EPSILON)
    )
    master = weight[...]
    weight_out[...] = master - LEARN_RATE * (step_dir + DECAY * master)
    one_out[...] = first_new
    two_out[...] = second_new


def adam_body(*refs):
    pairs, rest = refs[:6], refs[6:]
    for at in range(2):

        @pl.when(pl.program_id(0) == at)
        def _():
            adam_kernel(*pairs[at::2], *rest)


def add_kernel(a, b, c, d, low, high):
    low[...] = (a[...] + b[...].astype(F32)).astype(BF)
    high[...] = (c[...] + d[...].astype(F32)).astype(BF)


def add(*values):
    whole = pl.BlockSpec((PART, D), lambda: (0, 0))
    return pl.pallas_call(
        add_kernel,
        in_specs=[whole] * 4,
        out_specs=[whole] * 2,
        out_shape=[jax.ShapeDtypeStruct((PART, D), BF)] * 2,
        compiler_params=params(32),
        cost_estimate=cost(0.5),
        name="add",
    )(*values)


def adam(pairs, weight, one, two):
    straight = pl.BlockSpec((PART, D), lambda k: (k, 0))
    whole = pl.BlockSpec((PART, D), lambda k: (0, 0))
    return pl.pallas_call(
        adam_body,
        grid=(2,),
        in_specs=[whole] * 6 + [straight] * 3,
        out_specs=[straight] * 3,
        out_shape=[jax.ShapeDtypeStruct((SHARD, D), F32)] * 3,
        compiler_params=params(32),
        name="adam",
    )(*[value for pair in pairs for value in pair], weight, one, two)


def rotary_tables():
    positions = jnp.arange(SEQ).astype(F32)
    exponents = jnp.arange(HALF).astype(F32) * (2.0 / HD)
    frequency = THETA ** (-exponents)
    angles = frequency[:, None] * positions[None, :]
    return jnp.cos(angles), jnp.sin(angles)


def ring_gather(shard, up_again):
    below = send(shard, ALONG_Y[1])
    above = send(shard, ALONG_Y[3])
    far = send(below, ALONG_Y[1]) if up_again else send(above, ALONG_Y[3])
    return [shard, above, far, below]


def both_cores(pieces):
    return pieces + [send(piece, TO_CORE) for piece in pieces]


def per_device(tokens, student_weight, snapshot, moment_one, moment_two):
    own = tokens[0]
    master = student_weight[0]
    table = jnp.asarray(TABLE)[lax.axis_index("fsdp")]
    angles = rotary_tables()

    teacher = lax.ppermute(snapshot[0], "blk", [(g, (g + 1) % 8) for g in range(8)])
    plane = send(own, TO_PLANE)
    student_rows = both_cores(ring_gather(master.astype(BF), True))
    teacher_own = ring_gather(teacher, False)

    own_two, plane_two = [(own, 0), (own, 1)], [(plane, 0), (plane, 1)]
    two = [(0, 0), (1, 0)]
    *own_s, given = project(table, angles, own_two, [student_rows], two, [[0, 1]])
    teacher_own[2], teacher_own[3], given = lax.optimization_barrier(
        (teacher_own[2], teacher_own[3], given)
    )
    teacher_rows = both_cores(teacher_own)
    *own_t, given = project(table, angles, own_two, [teacher_rows], two, [[-1, -1, 0, 1]], given)
    got_own = send(given, TO_PLANE)
    plane_after, _ = lax.optimization_barrier((plane, own_t[0]))
    plane_two = [(plane_after, 0), (plane_after, 1)]
    *plane_s, given = project(table, angles, plane_two, [student_rows], two, [[0, 1]])
    got_s = send(given, TO_PLANE)
    *plane_t, given_0, given_1 = project(table, angles, plane_two, [teacher_rows], two, [[0], [1]])
    got_t = [send(given_0, TO_PLANE), send(given_1, TO_PLANE)]

    second = attend(
        table,
        angles,
        [[(plane_s[n], (got_own, n)), (plane_t[n], (got_own, 2 + n))] for n in range(2)],
    )
    got_s, got_t[0], _ = lax.optimization_barrier((got_s, got_t[0], second[2]))
    first = [attend(table, angles, [[(own_s[0], (got_s, 0)), (own_t[0], (got_t[0], 0))]])]
    back_first = [send(second[2], TO_PLANE), send(second[3], TO_PLANE)]
    got_t[1], *back_first, carried = lax.optimization_barrier((got_t[1], *back_first, first[0][2]))
    back_first[1] = send(back_first[1], TO_CORE)
    first.append(
        attend(
            table,
            angles,
            [[(own_s[1], (got_s, 1)), (own_t[1], (got_t[1], 0))]],
            (carried, first[0][3]),
        )
    )
    back_second = [send(first[1][2], TO_PLANE), send(first[1][3], TO_BOTH)]
    (before,) = weight_call(
        first_kernel,
        table,
        [part[0] for part in first] + [send(part[1], TO_CORE) for part in first],
        back_first,
        [own, send(own, TO_CORE)],
        [],
        [(CORE, F32)],
        6.0,
    )

    def weight_blocks(parts):
        return weight_call(
            lambda *refs: second_kernel(parts, *refs),
            table,
            [second[0], send(second[1], TO_CORE)],
            back_second,
            [plane_after, send(plane_after, TO_CORE)],
            [(before, part_index(step, first)) for step, first, _ in parts],
            [(PART, dtype) for _, _, dtype in parts],
            5.0,
        )

    up, down = ALONG_Y[1], ALONG_Y[3]
    far_low, far_high, next_high, last_low = weight_blocks(
        ((2, 0, BF), (2, PART, BF), (1, PART, BF), (3, 0, BF))
    )
    far_low, far_high = send(far_low, up), send(far_high, down)
    from_below, from_above = [None, send(next_high, up)], [send(last_low, down), None]
    next_low, last_high, *own_parts = weight_blocks(
        ((1, 0, F32), (3, PART, F32), (0, 0, F32), (0, PART, F32))
    )
    next_low, last_high = add(next_low, far_low, last_high, far_high)
    from_below[0], from_above[1] = send(next_low, up), send(last_high, down)
    pairs = [own_parts, from_below, from_above]
    updated = adam(pairs, master, moment_one[0], moment_two[0])
    return tuple(value[None] for value in updated)


def solution(mesh):
    spec = P("blk", "fsdp", None)
    return jax.shard_map(
        per_device,
        mesh=mesh,
        in_specs=(spec,) * 5,
        out_specs=(spec,) * 3,
        check_vma=False,
    )
```
